32 devices in a mesh: batch: 8 (over y, x, core), seq: 4 (over z).
Axes of the slice: x: 2, y: 2, z: 4, core: 2. Of those that a mesh axis runs over, the one named last changes fastest.
Arguments:
- inputs: bfloat16 [16, 1024, 1152], P('batch', 'seq'), may hold values from -6 to 6
- conds: bfloat16 [16, 1152], P('batch'), may hold values from -6 to 6
- heights: int32 [16], P('batch'), may hold values from 16 to 32, as said below
- widths: int32 [16], P('batch'), may hold values from 12 to 32, as said below
- qkv_weight: bfloat16 [1152, 3456], P('batch'), may hold values from -0.1875 to 0.1875
- qv_bias: bfloat16 [2304], P('batch'), may hold values from -1.796875 to 1.796875
- out_weight: bfloat16 [1152, 1152], P('batch'), may hold values from -1.5 to 1.5
- out_bias: bfloat16 [1152], P('batch'), may hold values from -1.796875 to 1.796875
- up_weight: bfloat16 [1152, 4608], P('batch'), may hold values from -0.1875 to 0.1875
- up_bias: bfloat16 [4608], P('batch'), may hold values from -1.796875 to 1.796875
- down_weight: bfloat16 [4608, 1152], P('batch'), may hold values from -0.09375 to 0.09375
- down_bias: bfloat16 [1152], P('batch'), may hold values from -1.796875 to 1.796875
- mod_weight: bfloat16 [1152, 6912], P('batch'), may hold values from -0.1875 to 0.1875
- mod_bias: bfloat16 [6912], P('batch'), may hold values from -3 to 3
- cotangent: bfloat16 [16, 1024, 1152], P('batch', 'seq'), may hold values from -6 to 6
Outputs:
- output: bfloat16 [16, 1024, 1152], P('batch', 'seq')
- input_grad: float32 [16, 1024, 1152], P('batch', 'seq')
- cond_grad: float32 [16, 1152], P('batch')
- qkv_weight_grad: float32 [1152, 3456], P('batch')
- qv_bias_grad: float32 [2304], P('batch')
- out_weight_grad: float32 [1152, 1152], P('batch')
- out_bias_grad: float32 [1152], P('batch')
- up_weight_grad: float32 [1152, 4608], P('batch')
- up_bias_grad: float32 [4608], P('batch')
- down_weight_grad: float32 [4608, 1152], P('batch')
- down_bias_grad: float32 [1152], P('batch')
- mod_weight_grad: float32 [1152, 6912], P('batch')
- mod_bias_grad: float32 [6912], P('batch')
The draws below stay inside these ranges and needn't reach their ends.
Inputs may be any that keep to these rules, and one draw needn't show every extreme that they name: In each aligned group of 2 samples, one sample drawn from the seed has heights = 32. The sample drawn from the seed also has widths = 32.
All inputs are finite; a program needn't handle non-finite values.
Results may differ from the reference program's by a relative error of at most 0.012.
The reference program's roundings to bfloat16 on the way count: a program that leaves them out, or rounds other values in their place, can miss the bound.
Values may be sent and summed in bfloat16 or wider, within the bound.
No kernel may reach another device: no remote copies, remote signals or barrier semaphores. Data moves between devices by JAX's collectives and lax.ppermute only.
A program may use at most 320 MiB of HBM per device.

```python
import jax
import jax.numpy as jnp
from jax import lax

HEADS = 16
HEAD = 72
D = 1152
FF = 4608
GRID = 32
SLOTS = 1024
SAMP_DEV = 2
SAMPLES = 16


def grid_sides(key):
    tall = jax.random.randint(jax.random.fold_in(key, 11), (SAMPLES,), GRID // 2, GRID + 1)
    broad = jax.random.randint(jax.random.fold_in(key, 12), (SAMPLES,), 3 * GRID // 8, GRID + 1)
    chosen = jax.random.randint(jax.random.fold_in(key, 13), (SAMPLES // SAMP_DEV,), 0, SAMP_DEV)
    filled = jnp.arange(SAMPLES, dtype=jnp.int32) % SAMP_DEV == jnp.repeat(chosen, SAMP_DEV)
    return (jnp.where(filled, GRID, tall).astype(jnp.int32), jnp.where(filled, GRID, broad).astype(jnp.int32))


def draw_heights(key, part):
    sides = grid_sides(key)
    return sides[0]


def draw_widths(key, part):
    sides = grid_sides(key)
    return sides[1]


def shard_levels(stream_key, dims, cuts, least, high):
    factor_of, own = 1.0, jax.random.fold_in(stream_key, 6)
    for dim, shards_of in cuts:
        steps = jnp.exp(jax.random.uniform(jax.random.fold_in(own, dim), (shards_of,), jnp.float32, least / len(cuts), high / len(cuts)))
        factor_of = factor_of * jnp.repeat(steps, dims[dim] // shards_of).reshape([-1 if axis == dim else 1 for axis in range(len(dims))])
    return factor_of


def centred(own_key, shape, scale, bound, cuts=(), kind=jnp.bfloat16):
    drawn = jax.random.normal(own_key, shape, jnp.float32) * scale
    if len(cuts) > 0:
        drawn = shard_levels(own_key, shape, cuts, -0.22, 0.18) * drawn
    return jnp.clip(drawn, min=-bound, max=bound).astype(kind)


def setup_inputs(seed: int = 0) -> dict:
    arg_keys = jax.random.split(jax.random.key(seed), 16)
    return {
        "inputs": centred(arg_keys[0], (SAMPLES, SLOTS, D), 1.0, 6.0, ((0, 8), (1, 4))),
        "conds": centred(arg_keys[1], (SAMPLES, D), 1.0, 6.0, ((0, 8),)),
        "heights": draw_heights(jax.random.fold_in(arg_keys[15], 71), 0),
        "widths": draw_widths(jax.random.fold_in(arg_keys[15], 71), 0),
        "qkv_weight": centred(arg_keys[4], (D, 3 * D), D ** -0.5, 0.1875, ((0, 8),)),
        "qv_bias": centred(arg_keys[5], (2 * D,), 0.3, 1.796875, ((0, 8),)),
        "out_weight": centred(arg_keys[6], (D, D), (max(D // 64, 1)) ** -0.5, 1.5, ((0, 8),)),
        "out_bias": centred(arg_keys[7], (D,), 0.3, 1.796875, ((0, 8),)),
        "up_weight": centred(arg_keys[8], (D, FF), D ** -0.5, 0.1875, ((0, 8),)),
        "up_bias": centred(arg_keys[9], (FF,), 0.3, 1.796875, ((0, 8),)),
        "down_weight": centred(arg_keys[10], (FF, D), FF ** -0.5, 0.09375, ((0, 8),)),
        "down_bias": centred(arg_keys[11], (D,), 0.3, 1.796875, ((0, 8),)),
        "mod_weight": centred(arg_keys[12], (D, 6 * D), D ** -0.5, 0.1875, ((0, 8),)),
        "mod_bias": centred(arg_keys[13], (6 * D,), 0.5, 3.0, ((0, 8),)),
        "cotangent": centred(arg_keys[14], (SAMPLES, SLOTS, D), 1.0, 6.0, ((0, 8), (1, 4))),
    }


@jax.custom_vjp
def low(v):
    return lax.optimization_barrier(v.astype(jnp.bfloat16)).astype(jnp.float32)

@jax.custom_vjp
def low_back(v):
    return v

def low_keep(v):
    return (low(v), None)

def low_pass(kept, grad):
    return (grad,)

def back_keep(v):
    return (v, None)

def back_low(kept, grad):
    return (low(grad),)
low.defvjp(low_keep, low_pass)
low_back.defvjp(back_keep, back_low)

def product(left, right):
    return jnp.matmul(left, right, precision=lax.Precision.HIGHEST)

def layer_norm(values):
    centre = values - lax.optimization_barrier(jnp.mean(values, axis=-1, keepdims=True))
    spread = lax.optimization_barrier(jnp.mean(centre * centre, axis=-1, keepdims=True))
    return centre * lax.rsqrt(spread + 1e-06)

def block_forward(weights, inputs, conds, valid):
    qkv_weight, qv_bias, out_weight, out_bias, up_weight, up_bias, down_weight, down_bias, mod_weight, mod_bias = weights
    modulation = low_back(product(low(jax.nn.silu(conds)), mod_weight) + mod_bias)
    shift1, scale1, gate1, shift2, scale2, gate2 = jnp.split(modulation[:, None, :], 6, axis=-1)
    moved = low(layer_norm(inputs) * (1.0 + scale1) + shift1)
    offsets = jnp.concatenate([qv_bias[:D], jnp.zeros((D,), jnp.float32), qv_bias[D:]])
    qkv = low(low_back(product(moved, qkv_weight) + offsets))
    query, key, value = jnp.split(qkv, 3, axis=-1)
    query = query.reshape(query.shape[0], SLOTS, HEADS, HEAD)
    key = key.reshape(key.shape[0], SLOTS, HEADS, HEAD)
    value = value.reshape(value.shape[0], SLOTS, HEADS, HEAD)
    scores = low_back(jnp.einsum('bqhd,bkhd->bhqk', query, key, precision=lax.Precision.HIGHEST) * HEAD ** (-0.5))
    scores = jnp.where(valid[:, None, None, :], scores, -1000000000.0)
    probs = low(jax.nn.softmax(scores, axis=-1))
    attended = jnp.einsum('bhqk,bkhd->bqhd', probs, value, precision=lax.Precision.HIGHEST)
    attended = low(low_back(attended.reshape(attended.shape[0], SLOTS, D)))
    projected = low_back(product(attended, out_weight) + out_bias)
    middle = inputs + gate1 * projected
    moved2 = low(layer_norm(middle) * (1.0 + scale2) + shift2)
    upper = low_back(product(moved2, up_weight) + up_bias)
    act = low(jax.nn.gelu(upper, approximate=True))
    lowered = low_back(product(act, down_weight) + down_bias)
    return middle + gate2 * lowered

def reference(inputs, conds, heights, widths, qkv_weight, qv_bias, out_weight, out_bias, up_weight, up_bias, down_weight, down_bias, mod_weight, mod_bias, cotangent):
    valid = jnp.arange(SLOTS, dtype=jnp.int32)[None, :] < (heights * widths)[:, None]
    weights = tuple((w.astype(jnp.float32) for w in (qkv_weight, qv_bias, out_weight, out_bias, up_weight, up_bias, down_weight, down_bias, mod_weight, mod_bias)))

    def grouped(array):
        return array.reshape((-1, 2) + array.shape[1:])

    def whole(weights, tokens, condition):

        def advance(carry, pieces):
            return (carry, jax.checkpoint(block_forward)(weights, pieces[0], pieces[1], pieces[2]))
        carry, results = lax.scan(advance, jnp.float32(0.0), (grouped(tokens), grouped(condition), grouped(valid)))
        return results.reshape(tokens.shape)
    result, pullback = jax.vjp(whole, weights, inputs.astype(jnp.float32), conds.astype(jnp.float32))
    weight_grads, input_grad, cond_grad = pullback(cotangent.astype(jnp.float32))
    return (result.astype(jnp.bfloat16), input_grad, cond_grad, weight_grads[0], weight_grads[1], weight_grads[2], weight_grads[3], weight_grads[4], weight_grads[5], weight_grads[6], weight_grads[7], weight_grads[8], weight_grads[9])
```

```python
import functools

import jax
import jax.numpy as jnp
from jax import lax
from jax.experimental import pallas as pl
from jax.experimental.pallas import tpu as pltpu
from jax.sharding import PartitionSpec as P

HEADS = 16
HEAD = 72
SCALE = HEAD ** (-0.5)
f32 = jnp.float32
bf16 = jnp.bfloat16
NT = (((1,), (1,)), ((), ()))
TN = (((0,), (0,)), ((), ()))


def dot(a, b, dims=(((1,), (0,)), ((), ()))):
    return lax.dot_general(a, b, dims, preferred_element_type=f32)


def attend_kernel(heads, limits, mine, theirs, out_mine, out_theirs, lse, qs, ks, vs, os, ls):
    half = mine.shape[0]
    total = 2 * half
    chunks = limits.shape[0]
    chunk = total // chunks
    wide = heads * HEAD
    lane = lax.broadcasted_iota(jnp.int32, (1, chunk), 1)
    valid = jnp.concatenate([lane < limits[i] for i in range(chunks)], axis=1)
    block = 256
    for h in range(heads):
        lo = h * HEAD
        for part, ref in ((0, mine), (1, theirs)):
            rows = slice(part * half, (part + 1) * half)
            qs[rows, :] = ref[:, lo : lo + HEAD]
            ks[rows, :] = ref[:, wide + lo : wide + lo + HEAD]
            vs[rows, :] = ref[:, 2 * wide + lo : 2 * wide + lo + HEAD]

        def step(i, carry):
            at = pl.ds(pl.multiple_of(i * block, block), block)
            scores = dot(qs[at, :], ks[...], NT) * SCALE
            scores = jnp.where(valid, scores, -1000000000.0)
            peak = jnp.max(scores, axis=1, keepdims=True)
            expo = jnp.exp(scores - peak)
            summed = jnp.sum(expo, axis=1, keepdims=True)
            probs = (expo * (1.0 / summed)).astype(bf16)
            os[at, :] = dot(probs, vs[...]).astype(bf16)
            ls[at, :] = peak + jnp.log(summed)
            return carry

        lax.fori_loop(0, total // block, step, 0)
        out_mine[:, lo : lo + HEAD] = os[:half, :]
        out_theirs[:, lo : lo + HEAD] = os[half:, :]
        lse[h : h + 1, :] = jnp.transpose(ls[...])


def attend(limits, mine, theirs):
    half, wide3 = mine.shape
    wide = wide3 // 3
    heads = wide // HEAD
    total = 2 * half
    return pl.pallas_call(
        functools.partial(attend_kernel, heads),
        out_shape=(
            jax.ShapeDtypeStruct((half, wide), bf16),
            jax.ShapeDtypeStruct((half, wide), bf16),
            jax.ShapeDtypeStruct((heads, total), f32),
        ),
        in_specs=[
            pl.BlockSpec(memory_space=pltpu.SMEM),
            pl.BlockSpec(memory_space=pltpu.VMEM),
            pl.BlockSpec(memory_space=pltpu.VMEM),
        ],
        out_specs=(pl.BlockSpec(memory_space=pltpu.VMEM),) * 3,
        scratch_shapes=[
            pltpu.VMEM((total, HEAD), bf16),
            pltpu.VMEM((total, HEAD), bf16),
            pltpu.VMEM((total, HEAD), bf16),
            pltpu.VMEM((total, HEAD), bf16),
            pltpu.VMEM((total, 1), f32),
        ],
        compiler_params=pltpu.CompilerParams(vmem_limit_bytes=40 * 2**20),
        cost_estimate=pl.CostEstimate(
            flops=4 * heads * total * total * 128,
            bytes_accessed=8 * total * wide,
            transcendentals=heads * total * total,
        ),
    )(limits, mine, theirs)


def back_kernel(heads, limits, mine, theirs, d_mine, d_theirs, lse, out_mine, out_theirs, qs, ks, vs, ds, dq, dk, dv):
    half = mine.shape[0]
    total = 2 * half
    chunks = limits.shape[0]
    chunk = total // chunks
    wide = heads * HEAD
    sub = lax.broadcasted_iota(jnp.int32, (chunk, 1), 0)
    valid = jnp.concatenate([sub < limits[i] for i in range(chunks)], axis=0)
    block = 256
    for h in range(heads):
        lo = h * HEAD
        for part, ref, d_ref in ((0, mine, d_mine), (1, theirs, d_theirs)):
            rows = slice(part * half, (part + 1) * half)
            qs[rows, :] = ref[:, lo : lo + HEAD]
            ks[rows, :] = ref[:, wide + lo : wide + lo + HEAD]
            vs[rows, :] = ref[:, 2 * wide + lo : 2 * wide + lo + HEAD]
            ds[rows, :] = d_ref[:, lo : lo + HEAD]
        dk[...] = jnp.zeros_like(dk)
        dv[...] = jnp.zeros_like(dv)

        def step(i, carry):
            at = pl.ds(pl.multiple_of(i * block, block), block)
            query = qs[at, :]
            d_out = ds[at, :]
            scores = dot(ks[...], query, NT) * SCALE - lse[h : h + 1, at]
            exact = jnp.where(valid, jnp.exp(jnp.where(valid, scores, -1000000000.0)), 0.0)
            d_probs = dot(vs[...], d_out, NT)
            dv[...] += dot(exact.astype(bf16), d_out)
            product = exact * d_probs
            centred = jnp.sum(product, axis=0, keepdims=True)
            d_scores = (product - exact * centred).astype(bf16)
            dk[...] += dot(d_scores, query)
            dq[at, :] = (dot(d_scores, ks[...], TN) * SCALE).astype(bf16)
            return carry

        lax.fori_loop(0, total // block, step, 0)
        for part, ref in ((0, out_mine), (1, out_theirs)):
            rows = slice(part * half, (part + 1) * half)
            ref[:, lo : lo + HEAD] = dq[rows, :]
            ref[:, wide + lo : wide + lo + HEAD] = (dk[rows, :] * SCALE).astype(bf16)
            ref[:, 2 * wide + lo : 2 * wide + lo + HEAD] = dv[rows, :].astype(bf16)


def attend_back(limits, mine, theirs, d_mine, d_theirs, lse):
    half, wide3 = mine.shape
    wide = wide3 // 3
    heads = wide // HEAD
    total = 2 * half
    return pl.pallas_call(
        functools.partial(back_kernel, heads),
        out_shape=(
            jax.ShapeDtypeStruct((half, wide3), bf16),
            jax.ShapeDtypeStruct((half, wide3), bf16),
        ),
        in_specs=[pl.BlockSpec(memory_space=pltpu.SMEM)] + [pl.BlockSpec(memory_space=pltpu.VMEM)] * 5,
        out_specs=(pl.BlockSpec(memory_space=pltpu.VMEM),) * 2,
        scratch_shapes=[
            pltpu.VMEM((total, HEAD), bf16),
            pltpu.VMEM((total, HEAD), bf16),
            pltpu.VMEM((total, HEAD), bf16),
            pltpu.VMEM((total, HEAD), bf16),
            pltpu.VMEM((total, HEAD), bf16),
            pltpu.VMEM((total, HEAD), f32),
            pltpu.VMEM((total, HEAD), f32),
        ],
        compiler_params=pltpu.CompilerParams(vmem_limit_bytes=40 * 2**20),
        cost_estimate=pl.CostEstimate(
            flops=10 * heads * total * total * 128,
            bytes_accessed=16 * total * wide,
            transcendentals=heads * total * total,
        ),
    )(limits, mine, theirs, d_mine, d_theirs, lse)


def pair_swap(array):
    size = lax.axis_size("batch")
    return lax.ppermute(array, "batch", [(i, i ^ 1) for i in range(size)])


def deal_pairs(turn, back=False):
    pairs = []
    seq = lax.axis_size("seq")
    for b in range(lax.axis_size("batch")):
        for s in range(seq):
            j = (s ^ turn) & 1
            dc = ((s >> 1) ^ (turn >> 1)) & 1
            here, there = b * seq + s, (b ^ dc) * seq + 2 * (b & 1) + j
            pairs.append((there, here) if back else (here, there))
    return pairs


def place_of(turn):
    b, s = lax.axis_index("batch"), lax.axis_index("seq")
    j = (s ^ turn) & 1
    half = (b ^ (s >> 1) ^ (turn >> 1)) & 1
    return j, half


def deal(array):
    half = array.shape[1] // 2
    parts = []
    for turn in range(4):
        j, c = place_of(turn)
        piece = lax.dynamic_slice(array, (j, c * half, 0), (1, half, array.shape[2]))[0]
        parts.append(lax.ppermute(piece, ("batch", "seq"), deal_pairs(turn)))
    return jnp.concatenate(parts, axis=0)


def undeal(array):
    half = array.shape[0] // 4
    out = jnp.zeros((2, 2 * half, array.shape[1]), array.dtype)
    for turn in range(4):
        got = lax.ppermute(array[turn * half : (turn + 1) * half], ("batch", "seq"), deal_pairs(turn, True))
        j, c = place_of(turn)
        out = lax.dynamic_update_slice(out, got[None], (j, c * half, 0))
    return out


def norm_forward(values):
    centre = values - jnp.mean(values, axis=-1, keepdims=True)
    factor = lax.rsqrt(jnp.mean(centre * centre, axis=-1, keepdims=True) + 1e-06)
    return centre * factor, factor


def norm_back(grad, normed, factor):
    return factor * (
        grad
        - jnp.mean(grad, axis=-1, keepdims=True)
        - normed * jnp.mean(grad * normed, axis=-1, keepdims=True)
    )


def gather(array, axis="batch"):
    return lax.all_gather(array, axis, axis=0, tiled=True)


def scatter_sum(array):
    part = lax.psum_scatter(array.astype(bf16), "batch", scatter_dimension=0, tiled=True)
    return lax.psum(part, "seq").astype(f32)


def body(
    inputs,
    conds,
    heights,
    widths,
    qkv_weight,
    qv_bias,
    out_weight,
    out_bias,
    up_weight,
    up_bias,
    down_weight,
    down_bias,
    mod_weight,
    mod_bias,
    cotangent,
):
    devices = lax.axis_size("batch")
    b, s = lax.axis_index("batch"), lax.axis_index("seq")
    c = b & 1
    width = inputs.shape[2]
    hidden = up_weight.shape[1]
    slot_dev = inputs.shape[1]
    half = slot_dev // 2
    rows = qkv_weight.shape[0]
    mods = mod_weight.shape[1]

    tokens16 = deal(inputs)
    counts = (heights * widths).astype(jnp.int32)
    upstream16 = deal(cotangent)

    small = jnp.concatenate([conds.reshape(-1), qv_bias, out_bias, up_bias, down_bias])
    sizes = [conds.size, qv_bias.size, out_bias.size, up_bias.size, down_bias.size]
    small = gather(small[None])
    spots = [sum(sizes[:i]) for i in range(6)]
    every = [small[:, spots[i] : spots[i + 1]] for i in range(5)]
    cond_all = every[0].reshape(2 * devices, width)
    qv_offset, out_offset, up_offset, down_offset = (e.reshape(-1).astype(f32) for e in every[1:])

    qkv_matrix = gather(qkv_weight)

    cond_single = cond_all.astype(f32)
    silu_all = jax.nn.silu(cond_single).astype(bf16)
    silu_rows = lax.dynamic_slice(silu_all, (0, b * rows), (2 * devices, rows))
    plane = lax.dynamic_index_in_dim(silu_rows.reshape(devices // 2, 4, rows), s, axis=1, keepdims=False)
    partial = dot(plane, mod_weight)
    own_bias = lax.dynamic_update_slice(jnp.zeros((mods,), f32), mod_bias.astype(f32), (b * mod_bias.shape[0],))
    partial = partial + own_bias[None]
    partial = jnp.broadcast_to(partial[:, None], (devices // 2, 2, mods)).reshape(devices, mods)
    modulation = lax.psum_scatter(partial, "batch", scatter_dimension=0, tiled=True)
    shift1, scale1, gate1, shift2, scale2, gate2 = jnp.split(modulation, 6, axis=-1)

    pair_counts = pair_swap(jnp.broadcast_to(counts[:, None], (2, 128)))[:, 0]
    group = jnp.where(c == 0, jnp.concatenate([counts, pair_counts]), jnp.concatenate([pair_counts, counts]))
    count = lax.dynamic_index_in_dim(group, s, keepdims=False)
    limits = []
    for part in range(2):
        core = c ^ part
        base = (s & 1) | (((s >> 1) ^ core) << 1)
        for turn in range(4):
            limits.append(count - (slot_dev * (base ^ turn) + half * core))
    limits = jnp.stack(limits).astype(jnp.int32)

    out_matrix = gather(out_weight)
    up_matrix = gather(up_weight)
    down_matrix = gather(down_weight)

    tokens = tokens16.astype(f32)
    normed, factor = norm_forward(tokens)
    moved = (normed * (1.0 + scale1) + shift1).astype(bf16)
    offsets = jnp.concatenate([qv_offset[:width], jnp.zeros((width,), f32), qv_offset[width:]])
    qkv = (dot(moved, qkv_matrix) + offsets).astype(bf16)

    def by_heads(array, parts):
        split = array.reshape(array.shape[0], parts, 2, width // 2)
        own = lax.dynamic_index_in_dim(split, c, axis=2, keepdims=False)
        other = lax.dynamic_index_in_dim(split, 1 - c, axis=2, keepdims=False)
        shape = (array.shape[0], parts * width // 2)
        return own.reshape(shape), pair_swap(other.reshape(shape))

    def by_tokens(own, other, parts):
        shape = (own.shape[0], parts, 1, width // 2)
        got = pair_swap(other).reshape(shape)
        own = own.reshape(shape)
        whole = jnp.where(c == 0, jnp.concatenate([own, got], axis=2), jnp.concatenate([got, own], axis=2))
        return whole.reshape(own.shape[0], parts * width)

    mine, theirs = by_heads(qkv, 3)
    att_mine, att_theirs, lse = attend(limits, mine, theirs)
    attended = by_tokens(att_mine, att_theirs, 1)
    projected = dot(attended, out_matrix) + out_offset
    middle = tokens + gate1 * projected
    normed2, factor2 = norm_forward(middle)
    moved2 = (normed2 * (1.0 + scale2) + shift2).astype(bf16)
    upper = dot(moved2, up_matrix) + up_offset
    gelu_value, gelu_pull = jax.vjp(lambda u: jax.nn.gelu(u, approximate=True), upper)
    act = gelu_value.astype(bf16)
    lowered = dot(act, down_matrix) + down_offset
    output = undeal((middle + gate2 * lowered).astype(bf16))

    upstream = upstream16.astype(f32)
    d_gate2 = jnp.sum(upstream * lowered, axis=0)
    d_lowered = (gate2 * upstream).astype(bf16)
    down_grad = scatter_sum(dot(act, d_lowered, TN))
    down_offset_grad = jnp.sum(d_lowered.astype(f32), axis=0)
    d_act = dot(d_lowered, down_matrix, NT)
    d_upper = gelu_pull(d_act)[0].astype(bf16)
    up_grad = scatter_sum(dot(moved2, d_upper, TN))
    up_offset_grad = jnp.sum(d_upper.astype(f32), axis=0)
    d_moved2 = dot(d_upper, up_matrix, NT)
    d_shift2 = jnp.sum(d_moved2, axis=0)
    d_scale2 = jnp.sum(d_moved2 * normed2, axis=0)
    d_middle = upstream + norm_back(d_moved2 * (1.0 + scale2), normed2, factor2)
    d_gate1 = jnp.sum(d_middle * projected, axis=0)
    d_projected = (gate1 * d_middle).astype(bf16)
    out_grad = scatter_sum(dot(attended, d_projected, TN))
    out_offset_grad = jnp.sum(d_projected.astype(f32), axis=0)
    d_attended = dot(d_projected, out_matrix, NT).astype(bf16)
    d_att_mine, d_att_theirs = by_heads(d_attended, 1)
    d_mine, d_theirs = attend_back(limits, mine, theirs, d_att_mine, d_att_theirs, lse)
    d_qkv = by_tokens(d_mine, d_theirs, 3)
    qkv_grad = scatter_sum(dot(moved, d_qkv, TN))
    column_sums = jnp.sum(d_qkv.astype(f32), axis=0)
    qv_offset_grad = jnp.concatenate([column_sums[:width], column_sums[2 * width :]])
    d_moved = dot(d_qkv, qkv_matrix, NT)
    d_shift1 = jnp.sum(d_moved, axis=0)
    d_scale1 = jnp.sum(d_moved * normed, axis=0)
    input_grad = undeal((d_middle + norm_back(d_moved * (1.0 + scale1), normed, factor)).astype(bf16)).astype(f32)

    partial_mod = jnp.concatenate([d_shift1, d_scale1, d_gate1, d_shift2, d_scale2, d_gate2])
    d_mod = (partial_mod + pair_swap(partial_mod)).astype(bf16)
    share = lax.dynamic_slice(d_mod, (c * (mods // 2),), (mods // 2,))
    all_mod = gather(gather(share[None], "seq"), "batch")
    d_mod_all = (
        all_mod.reshape(devices // 2, 2, 4, mods // 2).transpose(0, 2, 1, 3).reshape(2 * devices, mods)
    )
    mod_grad = dot(silu_rows, d_mod_all, TN)
    mod_offset_grad = jnp.sum(
        lax.dynamic_slice(d_mod_all, (0, b * mod_bias.shape[0]), (2 * devices, mod_bias.shape[0])).astype(f32), axis=0
    )
    d_silu_rows = dot(d_mod_all, mod_weight, NT)
    d_silu = lax.all_to_all(d_silu_rows.reshape(devices, 2, rows), "batch", 0, 0, tiled=True)
    d_silu = d_silu.transpose(1, 0, 2).reshape(2, width)
    cond_grad = jax.vjp(jax.nn.silu, conds.astype(f32))[1](d_silu)[0]

    own_shapes = (qv_bias.shape[0], out_bias.shape[0], up_bias.shape[0], down_bias.shape[0])
    bias = jnp.concatenate(
        [
            g.reshape(devices, -1)
            for g in (qv_offset_grad, out_offset_grad, up_offset_grad, down_offset_grad)
        ],
        axis=1,
    )
    bias = lax.psum(lax.psum_scatter(bias, "batch", scatter_dimension=0, tiled=True), "seq")[0]
    cuts = [sum(own_shapes[:i]) for i in range(5)]
    qv_g, out_g, up_g, down_g = (bias[cuts[i] : cuts[i + 1]] for i in range(4))
    return (
        output,
        input_grad,
        cond_grad,
        qkv_grad,
        qv_g,
        out_grad,
        out_g,
        up_grad,
        up_g,
        down_grad,
        down_g,
        mod_grad,
        mod_offset_grad,
    )


def solution(mesh):
    in_specs = (
        P("batch", "seq", None),
        P("batch", None),
        P("batch"),
        P("batch"),
        P("batch", None),
        P("batch"),
        P("batch", None),
        P("batch"),
        P("batch", None),
        P("batch"),
        P("batch", None),
        P("batch"),
        P("batch", None),
        P("batch"),
        P("batch", "seq", None),
    )
    out_specs = (
        P("batch", "seq", None),
        P("batch", "seq", None),
        P("batch", None),
        P("batch", None),
        P("batch"),
        P("batch", None),
        P("batch"),
        P("batch", None),
        P("batch"),
        P("batch", None),
        P("batch"),
        P("batch", None),
        P("batch"),
    )
    return jax.shard_map(body, mesh=mesh, in_specs=in_specs, out_specs=out_specs, check_vma=False)
```

```python
import functools

import jax
import jax.numpy as jnp
from jax import lax
from jax.experimental import pallas as pl
from jax.experimental.pallas import tpu as pltpu
from jax.sharding import PartitionSpec as P

HEADS = 16
HEAD = 72
SCALE = HEAD ** (-0.5)
LOG2E = 1.4426950408889634
f32 = jnp.float32
bf16 = jnp.bfloat16
NT = (((1,), (1,)), ((), ()))
TN = (((0,), (0,)), ((), ()))


def dot(a, b, dims=(((1,), (0,)), ((), ()))):
    return lax.dot_general(a, b, dims, preferred_element_type=f32)


WHOLE = pl.BlockSpec()
SMEM = pl.BlockSpec(memory_space=pltpu.SMEM)
HBM = pl.BlockSpec(memory_space=pltpu.HBM)
BLOCK = 512
PAD = 128
ROOT = 0.7978845608028654
VMEM_ATT = 48
LIGHT = pl.CostEstimate(flops=0, bytes_accessed=0, transcendentals=0)


def shaped(shape, kind):
    return pltpu.HBM(shape, kind)


def in_hbm(*arrays):
    return tuple(pltpu.with_memory_space_constraint(array, pltpu.HBM) for array in arrays)


def lanes(wide):
    return -(-wide // 128) * 128


def params(mib):
    return pltpu.CompilerParams(vmem_limit_bytes=mib * 2**20)


def on_core(core, work):
    for c in range(2):
        pl.when(core[0] == c)(functools.partial(work, c))


def split_kernel(core, source, mine, away):
    wide = source.shape[1] // 2

    def work(c):
        for ref, d in ((mine, c), (away, 1 - c)):
            ref[:, :wide] = source[:, d * wide : (d + 1) * wide]

    on_core(core, work)


def split_heads(core, array):
    rows, wide = array.shape[0], array.shape[1] // 2
    return pl.pallas_call(
        split_kernel,
        out_shape=(shaped((rows, wide), bf16), shaped((rows, lanes(wide)), bf16)),
        in_specs=[SMEM, WHOLE],
        out_specs=(WHOLE,) * 2,
        compiler_params=params(48),
        cost_estimate=LIGHT,
    )(core, *in_hbm(array))


def join_kernel(steps, core, *refs):
    own, got, whole = refs[:steps], refs[steps : 2 * steps], refs[2 * steps]
    narrow = own[0].shape[1] // 3
    wide = 2 * narrow * steps

    def work(c):
        for kind in range(3):
            for d, arrays in ((c, own), (1 - c, got)):
                for i, ref in enumerate(arrays):
                    at = kind * wide + (d * steps + i) * narrow
                    whole[:, at : at + narrow] = ref[:, kind * narrow : (kind + 1) * narrow]

    on_core(core, work)


def join_heads(core, own, got):
    steps, (rows, wide) = len(own), own[0].shape
    return pl.pallas_call(
        functools.partial(join_kernel, steps),
        out_shape=shaped((rows, 2 * steps * wide), own[0].dtype),
        in_specs=[SMEM] + [WHOLE] * (2 * steps),
        out_specs=WHOLE,
        compiler_params=params(48),
        cost_estimate=LIGHT,
    )(core, *in_hbm(*own, *got))


def assemble(spots, pieces, matrix, sems):
    copies = []
    for i, piece in enumerate(pieces):
        rows = pl.ds(pl.multiple_of(spots[i], 16), piece.shape[0])
        copies.append(pltpu.make_async_copy(piece, matrix.at[rows], sems.at[i]))
    for copy in copies:
        copy.start()
    for copy in copies:
        copy.wait()


def norm_rows(value):
    centre = value - jnp.mean(value, axis=1, keepdims=True)
    scale = lax.rsqrt(jnp.mean(centre * centre, axis=1, keepdims=True) + 1e-06)
    return centre * scale, scale


def back_rows(grad, normed, scale):
    return scale * (
        grad - jnp.mean(grad, axis=1, keepdims=True) - normed * jnp.mean(grad * normed, axis=1, keepdims=True)
    )


def row_chunks(rows, step=128):
    return [slice(i, i + step) for i in range(0, rows, step)]


def project_kernel(number, core, spots, tokens, mods, offset, *refs):
    pieces = refs[:number]
    mine, away, moved, whole, matrix, made, sems, out_sem = refs[number:]
    width = made.shape[1]
    half = width // 2
    for at in row_chunks(tokens.shape[0]):
        normed, _ = norm_rows(tokens[at, :].astype(f32))
        moved[at, :] = (normed * (1.0 + mods[:, width : 2 * width]) + mods[:, :width]).astype(bf16)
    assemble(spots, pieces, matrix, sems)
    out = pltpu.make_async_copy(matrix, whole, out_sem)
    out.start()
    for kind in range(3):
        at = slice(kind * width, (kind + 1) * width)
        made[...] = (dot(moved[...], matrix[:, at]) + offset[:, at]).astype(bf16)

        def work(c):
            for ref, d in ((mine, c), (away, 1 - c)):
                ref[:, kind * half : (kind + 1) * half] = made[:, d * half : (d + 1) * half]

        on_core(core, work)
    out.wait()


def project(core, gathered, tokens, mods, offset):
    spots, pieces = gathered
    rows, width = tokens.shape
    wide = pieces[0].shape[1]
    return pl.pallas_call(
        functools.partial(project_kernel, len(pieces)),
        out_shape=(
            shaped((rows, wide // 2), bf16),
            shaped((rows, lanes(wide // 2)), bf16),
            shaped((rows, width), bf16),
            shaped((width, wide), bf16),
        ),
        in_specs=[SMEM, SMEM, WHOLE, WHOLE, WHOLE] + [HBM] * len(pieces),
        out_specs=(WHOLE, WHOLE, WHOLE, HBM),
        scratch_shapes=[
            pltpu.VMEM((width, wide), bf16),
            pltpu.VMEM((rows, width), bf16),
            pltpu.SemaphoreType.DMA((len(pieces),)),
            pltpu.SemaphoreType.DMA,
        ],
        compiler_params=params(48),
        cost_estimate=LIGHT,
    )(core, spots, *in_hbm(tokens, mods, offset, *pieces))


def middle_kernel(number, core, spots, own, got, tokens, mods, offset, *refs):
    pieces = refs[:number]
    attended, projected, normed, factor, moved, whole, matrix, sems, out_sem = refs[number:]
    assemble(spots, pieces, matrix, sems)
    out = pltpu.make_async_copy(matrix, whole, out_sem)
    out.start()
    width = matrix.shape[1]
    half = width // 2

    def work(c):
        attended[:, c * half : (c + 1) * half] = own[...]
        attended[:, (1 - c) * half : (2 - c) * half] = got[:, :half]

    on_core(core, work)
    gate1, shift2, scale2 = (mods[:, i * width : (i + 1) * width] for i in (2, 3, 4))
    projected[...] = dot(attended[...], matrix[...]) + offset[...]
    for at in row_chunks(own.shape[0]):
        made = projected[at, :]
        value = tokens[at, :].astype(f32) + gate1 * made
        value, scale = norm_rows(value)
        normed[at, :] = value
        factor[at, :] = scale
        moved[at, :] = (value * (1.0 + scale2) + shift2).astype(bf16)
    out.wait()


def middle_part(core, gathered, own, got, tokens, mods, offset):
    spots, pieces = gathered
    rows, width = tokens.shape
    return pl.pallas_call(
        functools.partial(middle_kernel, len(pieces)),
        out_shape=(
            shaped((rows, width), bf16),
            shaped((rows, width), f32),
            shaped((rows, width), f32),
            shaped((rows, 1), f32),
            shaped((rows, width), bf16),
            shaped((width, width), bf16),
        ),
        in_specs=[SMEM, SMEM] + [WHOLE] * 5 + [HBM] * len(pieces),
        out_specs=(WHOLE,) * 5 + (HBM,),
        scratch_shapes=[
            pltpu.VMEM((width, width), bf16),
            pltpu.SemaphoreType.DMA((len(pieces),)),
            pltpu.SemaphoreType.DMA,
        ],
        compiler_params=params(48),
        cost_estimate=LIGHT,
    )(core, spots, *in_hbm(own, got, tokens, mods, offset, *pieces))


def pair_grad_kernel(add_got, where, left, right, *refs):
    made = refs[-1]
    half = left.shape[1] // 2
    side = where[1]
    for d in range(2):

        @pl.when(side == d)
        def _():
            value = dot(left[:, d * half : (d + 1) * half], right[...], TN)
            if add_got:
                value = value + refs[0][0].astype(f32)
            made[0] = value.astype(bf16)


def pair_grad(left, right, b, side, got=None):
    rows, wide = left.shape
    step = wide // 4
    where = jnp.stack([b >> 1, side]).astype(jnp.int32)
    shape = (4, step // 2, right.shape[1])
    block = pl.BlockSpec((1,) + shape[1:], lambda m, where: (m, 0, 0))
    specs = [
        pl.BlockSpec((rows, step), lambda m, where: (0, where[0] ^ m)),
        pl.BlockSpec(right.shape, lambda m, where: (0, 0)),
    ]
    return pl.pallas_call(
        functools.partial(pair_grad_kernel, got is not None),
        out_shape=shaped(shape, bf16),
        grid_spec=pltpu.PrefetchScalarGridSpec(
            num_scalar_prefetch=1,
            grid=(4,),
            in_specs=specs + ([block] if got is not None else []),
            out_specs=block,
        ),
        compiler_params=params(48),
        cost_estimate=LIGHT,
    )(where, *in_hbm(left, right, *([got] if got is not None else [])))


def up_kernel(moved, matrix, offset, act, slope):
    for at in row_chunks(moved.shape[0], 256):
        u = dot(moved[at, :], matrix[...]) + offset[...]
        square = u * u
        t = jnp.tanh(ROOT * (u + 0.044715 * (square * u)))
        act[at, :] = (0.5 * u * (1.0 + t)).astype(bf16)
        slope[at, :] = 0.5 * (1.0 + t) + (0.5 * ROOT) * u * (1.0 - t * t) * (1.0 + (3 * 0.044715) * square)


def up_part(moved, matrix, offset):
    (rows, width), hidden = moved.shape, matrix.shape[1]
    step = hidden // 4
    return pl.pallas_call(
        up_kernel,
        out_shape=(shaped((rows, hidden), bf16), shaped((rows, hidden), f32)),
        grid=(4,),
        in_specs=[WHOLE, pl.BlockSpec((width, step), lambda i: (0, i)), pl.BlockSpec((1, step), lambda i: (0, i))],
        out_specs=(pl.BlockSpec((rows, step), lambda i: (0, i)), pl.BlockSpec((rows, step), lambda i: (0, i))),
        compiler_params=params(48),
        cost_estimate=LIGHT,
    )(*in_hbm(moved, matrix, offset))


def slope_kernel(grad, matrix, slope, d_upper, sums):
    total = jnp.zeros(sums.shape, f32)
    for at in row_chunks(grad.shape[0], 256):
        value = (dot(grad[at, :], matrix[...], NT) * slope[at, :]).astype(bf16)
        d_upper[at, :] = value
        total = total + jnp.sum(value.astype(f32), axis=0, keepdims=True)
    sums[...] = total


def slope_part(grad, matrix, slope):
    (rows, width), hidden = grad.shape, matrix.shape[0]
    step = hidden // 4
    across = pl.BlockSpec((rows, step), lambda i: (0, i))
    return pl.pallas_call(
        slope_kernel,
        out_shape=(shaped((rows, hidden), bf16), shaped((1, hidden), f32)),
        grid=(4,),
        in_specs=[WHOLE, pl.BlockSpec((step, width), lambda i: (i, 0)), across],
        out_specs=(across, pl.BlockSpec((1, step), lambda i: (0, i))),
        compiler_params=params(48),
        cost_estimate=LIGHT,
    )(*in_hbm(grad, matrix, slope))


def down_kernel(act, matrix, offset, tokens, projected, mods, grad, output, d_gate, total):
    step = pl.program_id(0)
    width = matrix.shape[1]

    @pl.when(step == 0)
    def _():
        total[...] = dot(act[...], matrix[...])

    @pl.when(step > 0)
    def _():
        total[...] += dot(act[...], matrix[...])

    @pl.when(step == pl.num_programs(0) - 1)
    def _():
        gate1, gate2 = mods[:, 2 * width : 3 * width], mods[:, 5 * width :]
        summed = jnp.zeros(d_gate.shape, f32)
        for at in row_chunks(act.shape[0]):
            lowered = total[at, :] + offset[...]
            middle = tokens[at, :].astype(f32) + gate1 * projected[at, :]
            output[at, :] = (middle + gate2 * lowered).astype(bf16)
            summed = summed + jnp.sum(grad[at, :].astype(f32) * lowered, axis=0, keepdims=True)
        d_gate[...] = summed


def down_part(act, matrix, offset, tokens, projected, mods, grad):
    rows, hidden = act.shape
    step, width = hidden // 4, matrix.shape[1]
    return pl.pallas_call(
        down_kernel,
        out_shape=(shaped((rows, width), bf16), shaped((1, width), f32)),
        grid=(4,),
        in_specs=[pl.BlockSpec((rows, step), lambda i: (0, i)), pl.BlockSpec((step, width), lambda i: (i, 0))]
        + [WHOLE] * 5,
        out_specs=(WHOLE, WHOLE),
        scratch_shapes=[pltpu.VMEM((rows, width), f32)],
        compiler_params=params(48),
        cost_estimate=LIGHT,
    )(*in_hbm(act, matrix, offset, tokens, projected, mods, grad))


def middle_back_kernel(core, d_upper, matrix, normed, factor, projected, grad, mods, out_matrix, d_middle, d_projected, mine, away, sums, total):
    step = pl.program_id(0)
    width = matrix.shape[0]
    half = width // 2

    @pl.when(step == 0)
    def _():
        total[...] = dot(d_upper[...], matrix[...], NT)

    @pl.when(step > 0)
    def _():
        total[...] += dot(d_upper[...], matrix[...], NT)

    @pl.when(step == pl.num_programs(0) - 1)
    def _():
        gate1, scale2 = mods[:, 2 * width : 3 * width], mods[:, 4 * width : 5 * width]
        summed = [jnp.zeros((1, width), f32) for _ in range(4)]
        for at in row_chunks(grad.shape[0]):
            d_moved, n = total[at, :], normed[at, :]
            value = grad[at, :].astype(f32) + back_rows(d_moved * (1.0 + scale2), n, factor[at, :])
            d_middle[at, :] = value
            d_proj = (gate1 * value).astype(bf16)
            d_projected[at, :] = d_proj
            terms = d_moved, d_moved * n, value * projected[at, :], d_proj.astype(f32)
            summed = [u + jnp.sum(v, axis=0, keepdims=True) for u, v in zip(summed, terms)]
        total[...] = dot(d_projected[...], out_matrix[...], NT)

        def work(c):
            mine[...] = total[:, c * half : (c + 1) * half].astype(bf16)
            away[:, :half] = total[:, (1 - c) * half : (2 - c) * half].astype(bf16)

        on_core(core, work)
        for i, value in enumerate(summed):
            sums[i : i + 1, :] = value


def middle_back(core, d_upper, matrix, normed, factor, projected, grad, mods, out_matrix):
    rows, hidden = d_upper.shape
    step, width = hidden // 4, matrix.shape[0]
    return pl.pallas_call(
        middle_back_kernel,
        out_shape=(
            shaped((rows, width), f32),
            shaped((rows, width), bf16),
            shaped((rows, width // 2), bf16),
            shaped((rows, lanes(width // 2)), bf16),
            shaped((4, width), f32),
        ),
        grid=(4,),
        in_specs=[SMEM, pl.BlockSpec((rows, step), lambda i: (0, i)), pl.BlockSpec((width, step), lambda i: (0, i))]
        + [WHOLE] * 6,
        out_specs=(WHOLE,) * 5,
        scratch_shapes=[pltpu.VMEM((rows, width), f32)],
        compiler_params=params(48),
        cost_estimate=LIGHT,
    )(core, *in_hbm(d_upper, matrix, normed, factor, projected, grad, mods, out_matrix))


def input_back_kernel(d_qkv, matrix, tokens, mods, d_middle, input_grad, sums, columns, total):
    step = pl.program_id(0)
    width = matrix.shape[0]
    columns[...] = jnp.sum(d_qkv[...].astype(f32), axis=0, keepdims=True)

    @pl.when(step == 0)
    def _():
        total[...] = dot(d_qkv[...], matrix[...], NT)

    @pl.when(step > 0)
    def _():
        total[...] += dot(d_qkv[...], matrix[...], NT)

    @pl.when(step == pl.num_programs(0) - 1)
    def _():
        scale1 = mods[:, width : 2 * width]
        summed = [jnp.zeros((1, width), f32) for _ in range(2)]
        for at in row_chunks(tokens.shape[0]):
            normed, factor = norm_rows(tokens[at, :].astype(f32))
            d_moved = total[at, :]
            input_grad[at, :] = (d_middle[at, :] + back_rows(d_moved * (1.0 + scale1), normed, factor)).astype(bf16)
            summed = [u + jnp.sum(v, axis=0, keepdims=True) for u, v in zip(summed, (d_moved, d_moved * normed))]
        for i, value in enumerate(summed):
            sums[i : i + 1, :] = value


def input_back(d_qkv, matrix, tokens, mods, d_middle):
    rows, wide = d_qkv.shape
    width = matrix.shape[0]
    return pl.pallas_call(
        input_back_kernel,
        out_shape=(shaped((rows, width), bf16), shaped((2, width), f32), shaped((1, wide), f32)),
        grid=(wide // width,),
        in_specs=[pl.BlockSpec((rows, width), lambda i: (0, i)), pl.BlockSpec((width, width), lambda i: (0, i))]
        + [WHOLE] * 3,
        out_specs=(WHOLE, WHOLE, pl.BlockSpec((1, width), lambda i: (0, i))),
        scratch_shapes=[pltpu.VMEM((rows, width), f32)],
        compiler_params=params(48),
        cost_estimate=LIGHT,
    )(*in_hbm(d_qkv, matrix, tokens, mods, d_middle))


def block_grad_kernel(add_got, spots, left, right, *refs):
    made, chosen, turned = refs[-3:]
    rows = made.shape[1]

    @pl.when(pl.program_id(0) == 0)
    def _():
        turned[...] = jnp.transpose(left[...])
        for e in range(4):
            at = pl.ds(pl.multiple_of(spots[e], 16), rows)
            chosen[e * rows : (e + 1) * rows, :] = turned[at, :]

    value = dot(chosen[...], right[...])
    for e in range(4):
        part = value[e * rows : (e + 1) * rows, :]
        if add_got:
            part = part + refs[0][e].astype(f32)
        made[e] = part.astype(bf16)


def block_grad(left, right, b, side, got=None):
    (slots, wide), columns = left.shape, right.shape[1]
    rows = wide // 8
    spots = jnp.stack([((b >> 1) ^ m) * 2 * rows + side * rows for m in range(4)]).astype(jnp.int32)
    step = 1152 if columns % 1152 == 0 else columns
    block = pl.BlockSpec((4, rows, step), lambda i: (0, 0, i))
    return pl.pallas_call(
        functools.partial(block_grad_kernel, got is not None),
        out_shape=shaped((4, rows, columns), bf16),
        grid=(columns // step,),
        in_specs=[SMEM, WHOLE, pl.BlockSpec((slots, step), lambda i: (0, i))] + ([block] if got is not None else []),
        out_specs=block,
        scratch_shapes=[pltpu.VMEM((4 * rows, slots), bf16), pltpu.VMEM((wide, slots), bf16)],
        compiler_params=params(48),
        cost_estimate=LIGHT,
    )(spots, *in_hbm(left, right, *([got] if got is not None else [])))


def fill(h, heads, mine, theirs, qs, ks, vs):
    half, wide, lo = mine.shape[0], heads * HEAD, h * HEAD
    for part, ref in ((0, mine), (1, theirs)):
        rows = slice(part * half, (part + 1) * half)
        qs[rows, :HEAD] = ref[:, lo : lo + HEAD]
        ks[rows, :HEAD] = ref[:, wide + lo : wide + lo + HEAD]
        vs[rows, :] = ref[:, 2 * wide + lo : 2 * wide + lo + HEAD]


def mark_valid(limits, qs, ks):
    total = qs.shape[0]
    chunks = limits.shape[0]
    sub = lax.broadcasted_iota(jnp.int32, (total // chunks, 1), 0)
    bias = jnp.concatenate([jnp.where(sub < limits[i], 0.0, -1e30) for i in range(chunks)], axis=0)
    qs[...] = jnp.zeros_like(qs)
    ks[...] = jnp.zeros_like(ks)
    qs[:, HEAD : HEAD + 1] = jnp.ones((total, 1), bf16)
    ks[:, HEAD : HEAD + 1] = bias.astype(bf16)


def attend_kernel(heads, limits, mine, theirs, out_mine, out_theirs, lse, qs, ks, vs, os, ls):
    half = mine.shape[0]
    total = 2 * half
    mark_valid(limits, qs, ks)
    for h in range(heads):
        fill(h, heads, mine, theirs, qs, ks, vs)
        for i in range(total // BLOCK):
            at = slice(i * BLOCK, (i + 1) * BLOCK)
            scores = dot(qs[at, :], ks[...], NT) * (SCALE * LOG2E)
            peak = jnp.max(scores, axis=1, keepdims=True)
            expo = jnp.exp2(scores - peak)
            summed = jnp.sum(expo, axis=1, keepdims=True)
            probs = (expo * (1.0 / summed)).astype(bf16)
            os[at, :] = dot(probs, vs[...]).astype(bf16)
            ls[at, :] = peak + jnp.log2(summed)
        lo = h * HEAD
        out_mine[:, lo : lo + HEAD] = os[:half, :]
        out_theirs[:, lo : lo + HEAD] = os[half:, :]
        lse[h : h + 1, :] = jnp.transpose(ls[...])


def attend(limits, mine, theirs):
    half, wide3 = mine.shape
    wide = wide3 // 3
    heads = wide // HEAD
    total = 2 * half
    return pl.pallas_call(
        functools.partial(attend_kernel, heads),
        out_shape=(shaped((half, wide), bf16), shaped((half, lanes(wide)), bf16), shaped((heads, total), f32)),
        in_specs=[SMEM, WHOLE, WHOLE],
        out_specs=(WHOLE,) * 3,
        scratch_shapes=[
            pltpu.VMEM((total, PAD), bf16),
            pltpu.VMEM((total, PAD), bf16),
            pltpu.VMEM((total, HEAD), bf16),
            pltpu.VMEM((total, HEAD), bf16),
            pltpu.VMEM((total, 1), f32),
        ],
        compiler_params=params(VMEM_ATT),
        cost_estimate=LIGHT,
    )(limits, *in_hbm(mine, theirs))


def back_kernel(heads, first, number, limits, mine, theirs, d_mine, d_theirs, lse, out_mine, out_theirs, qs, ks, vs, ds, dq, dk, dv):
    half = mine.shape[0]
    total = 2 * half
    narrow = number * HEAD
    mark_valid(limits, qs, ks)
    for h in range(first, first + number):
        fill(h, heads, mine, theirs, qs, ks, vs)
        lo = h * HEAD
        ds[:half, :] = d_mine[:, lo : lo + HEAD]
        ds[half:, :] = d_theirs[:, lo : lo + HEAD]
        for i in range(total // BLOCK):
            at = slice(i * BLOCK, (i + 1) * BLOCK)
            query, d_out = qs[at, :], ds[at, :]
            exact = jnp.exp2(dot(ks[...], query, NT) * (SCALE * LOG2E) - lse[h : h + 1, at])
            d_probs = dot(vs[...], d_out, NT)
            more = dot(exact.astype(bf16), d_out)
            dv[...] = more if i == 0 else dv[...] + more
            product = exact * d_probs
            centred = jnp.sum(product, axis=0, keepdims=True)
            d_scores = (product - exact * centred).astype(bf16)
            more = dot(d_scores, query)
            dk[...] = more if i == 0 else dk[...] + more
            dq[at, :] = (dot(d_scores, ks[...], TN) * SCALE).astype(bf16)
        lo = (h - first) * HEAD
        for part, ref in ((0, out_mine), (1, out_theirs)):
            rows = slice(part * half, (part + 1) * half)
            ref[:, lo : lo + HEAD] = dq[rows, :HEAD]
            ref[:, narrow + lo : narrow + lo + HEAD] = (dk[rows, :HEAD] * SCALE).astype(bf16)
            ref[:, 2 * narrow + lo : 2 * narrow + lo + HEAD] = dv[rows, :].astype(bf16)


def attend_back(limits, mine, theirs, d_mine, d_theirs, lse, first, number):
    half, wide3 = mine.shape
    wide = wide3 // 3
    heads = wide // HEAD
    total = 2 * half
    return pl.pallas_call(
        functools.partial(back_kernel, heads, first, number),
        out_shape=(shaped((half, 3 * number * HEAD), bf16), shaped((half, lanes(3 * number * HEAD)), bf16)),
        in_specs=[SMEM] + [WHOLE] * 5,
        out_specs=(WHOLE,) * 2,
        scratch_shapes=[
            pltpu.VMEM((total, PAD), bf16),
            pltpu.VMEM((total, PAD), bf16),
            pltpu.VMEM((total, HEAD), bf16),
            pltpu.VMEM((total, HEAD), bf16),
            pltpu.VMEM((total, PAD), bf16),
            pltpu.VMEM((total, PAD), f32),
            pltpu.VMEM((total, HEAD), f32),
        ],
        compiler_params=params(VMEM_ATT),
        cost_estimate=LIGHT,
    )(limits, *in_hbm(mine, theirs, d_mine, d_theirs, lse))


def pair_swap(array):
    size = lax.axis_size("batch")
    return lax.ppermute(array, "batch", [(i, i ^ 1) for i in range(size)])


def deal_pairs(turn, back=False):
    pairs = []
    seq = lax.axis_size("seq")
    for b in range(lax.axis_size("batch")):
        for s in range(seq):
            j = (s ^ turn) & 1
            dc = ((s >> 1) ^ (turn >> 1)) & 1
            here, there = b * seq + s, (b ^ dc) * seq + 2 * (b & 1) + j
            pairs.append((there, here) if back else (here, there))
    return pairs


def place_of(turn):
    b, s = lax.axis_index("batch"), lax.axis_index("seq")
    j = (s ^ turn) & 1
    half = (b ^ (s >> 1) ^ (turn >> 1)) & 1
    return j, half


def deal(array):
    half = array.shape[1] // 2
    parts = []
    for turn in range(4):
        j, c = place_of(turn)
        piece = lax.dynamic_slice(array, (j, c * half, 0), (1, half, array.shape[2]))[0]
        parts.append(lax.ppermute(piece, ("batch", "seq"), deal_pairs(turn)))
    return jnp.concatenate(parts, axis=0)


def undeal(array):
    half = array.shape[0] // 4
    out = jnp.zeros((2, 2 * half, array.shape[1]), array.dtype)
    for turn in range(4):
        got = lax.ppermute(array[turn * half : (turn + 1) * half], ("batch", "seq"), deal_pairs(turn, True))
        j, c = place_of(turn)
        out = lax.dynamic_update_slice(out, got[None], (j, c * half, 0))
    return out


def norm_forward(values):
    centre = values - jnp.mean(values, axis=-1, keepdims=True)
    factor = lax.rsqrt(jnp.mean(centre * centre, axis=-1, keepdims=True) + 1e-06)
    return centre * factor, factor


def norm_back(grad, normed, factor):
    return factor * (
        grad
        - jnp.mean(grad, axis=-1, keepdims=True)
        - normed * jnp.mean(grad * normed, axis=-1, keepdims=True)
    )


def gather(array):
    return lax.all_gather(array, "batch", axis=0, tiled=True)


def hop(array, bits):
    size = lax.axis_size("batch")
    return lax.ppermute(array, "batch", [(i, i ^ bits) for i in range(size)])


class Hops:
    def __init__(self, array):
        self.array = array
        self.plain = lax.axis_size("batch") != 8
        if self.plain:
            self.whole = gather(array)
            self.moving = (self.whole,)
        else:
            self.moving = self.along_x, self.along_y = hop(array, 2), hop(array, 4)

    def pieces(self, *done):
        if self.plain:
            return jnp.zeros((1,), jnp.int32), [self.whole]
        rows = self.array.shape[0]
        cut = rows // 2 // 16 * 16
        b = lax.axis_index("batch")
        along_x, along_y = after((self.along_x, self.along_y), *done)
        corner = hop(along_x[:cut], 4), hop(along_y[cut:], 2)
        self.moving = along_x, along_y, *corner
        pieces = [(0, 0, self.array), (2, 0, along_x), (4, 0, along_y), (6, 0, corner[0]), (6, cut, corner[1])]
        pieces += [(bits ^ 1, at, hop(piece, 1)) for bits, at, piece in pieces]
        spots = jnp.stack([(b ^ bits) * rows + at for bits, at, _ in pieces]).astype(jnp.int32)
        return spots, [piece for _, _, piece in pieces]


def after(value, *done):
    return lax.optimization_barrier((value, done))[0]


def add(u, v):
    return (u.astype(f32) + v.astype(f32)).astype(bf16)


class Grad:
    def __init__(self, left, right, paired=False):
        self.left, self.right, self.paired = left, right, paired
        self.rows = left.shape[1] // lax.axis_size("batch")
        self.plain = lax.axis_size("batch") != 8 or lax.axis_size("seq") != 4

    def away(self, *done):
        if self.plain:
            made = self.made = dot(after(self.left, *done), self.right, TN).astype(bf16)
            return made
        self.left = after(self.left, *done)
        b = lax.axis_index("batch")
        made = (pair_grad if self.paired else block_grad)(self.left, self.right, b, 1 - (b & 1))
        self.got = hop(made, 1)
        return made

    def stay(self, *done):
        if self.plain:
            part = lax.psum_scatter(self.made, "batch", scatter_dimension=0, tiled=True)
            self.part = lax.psum(part, "seq")
            return self.part
        self.left = after(self.left, *done)
        b = lax.axis_index("batch")
        made = (pair_grad if self.paired else block_grad)(self.left, self.right, b, b & 1, self.got)
        both = made.reshape(4 * self.rows, -1)
        rows, cut = self.rows, self.rows // 2 // 8 * 8
        self.own, self.to_x, self.to_y, corner = (both[i * rows : (i + 1) * rows] for i in range(4))
        self.cut = cut
        self.got_x, self.got_y = hop(corner[:cut], 2), hop(corner[cut:], 4)
        return made

    def mix(self, *done):
        if self.plain:
            return self.part
        cut = self.cut
        to_x, to_y = after((self.to_x, self.to_y), *done)
        to_y = jnp.concatenate([add(to_y[:cut], self.got_x), to_y[cut:]], axis=0)
        to_x = jnp.concatenate([to_x[:cut], add(to_x[cut:], self.got_y)], axis=0)
        self.got_x, self.got_y = hop(to_x, 2), hop(to_y, 4)
        return to_x, to_y

    def finish(self, *done, extra=None):
        if self.plain:
            return (self.land(extra=extra),) * 2
        own = after(self.own, *done)
        part = (own.astype(f32) + self.got_x.astype(f32) + self.got_y.astype(f32)).astype(bf16)
        if extra is not None:
            part = jnp.concatenate([part, extra.astype(bf16)], axis=0)
        total = lax.psum(part, "seq")
        self.part, self.plain = total[: self.rows], True
        if extra is not None:
            self.extra = total[self.rows :].astype(f32)
        return part, total

    def land(self, *done, extra=None, chunks=1):
        if self.plain:
            if extra is not None:
                self.extra = lax.psum(extra, "seq")
            return self.part
        own = after(self.own, *done)
        part = (own.astype(f32) + self.got_x.astype(f32) + self.got_y.astype(f32)).astype(bf16)
        if extra is not None:
            part = jnp.concatenate([part, extra.astype(bf16)], axis=0)
        step = -(-part.shape[0] // chunks // 8) * 8
        self.parts = [part[i * step : (i + 1) * step] for i in range(chunks)]
        self.gots = [lax.ppermute(part, "seq", [(0, 1), (3, 2)]) for part in self.parts]
        return part

    def pass_on(self, pairs, done):
        if self.plain:
            return self.part
        parts = after(tuple(self.parts), *done)
        self.parts, gots = [], self.gots
        self.gots = []
        for part, got in zip(parts, gots):
            part = add(part, got)
            self.parts.append(part)
            self.gots.append(lax.ppermute(part, "seq", pairs))
        return tuple(self.parts)

    def across(self, *done):
        return self.pass_on([(1, 2), (2, 1)], done)

    def outward(self, *done):
        return self.pass_on([(1, 0), (2, 3)], done)

    def result(self, *done):
        if self.plain:
            part = after(self.part, *done).astype(f32)
            return part if not hasattr(self, "extra") else (part, self.extra)
        s = lax.axis_index("seq")
        ends = (s == 0) | (s == 3)
        parts = after(tuple(self.parts), *done)
        total = [jnp.where(ends, got, part).astype(f32) for part, got in zip(parts, self.gots)]
        total = total[0] if len(total) == 1 else jnp.concatenate(total, axis=0)
        if total.shape[0] > self.rows:
            return total[: self.rows], total[self.rows :]
        return total


def all_samples(row):
    rows = row[None]
    for bit in (1, 2):
        rows = jnp.concatenate([rows, lax.ppermute(rows, "seq", [(i, i ^ bit) for i in range(4)])], axis=0)
    bits = 2
    while bits < lax.axis_size("batch"):
        rows = jnp.concatenate([rows, hop(rows, bits)], axis=0)
        bits *= 2
    return rows


def xor_order(array, index):
    size, bit = array.shape[0], 1
    while bit < size:
        split = array.reshape((size // (2 * bit), 2, bit) + array.shape[1:])
        array = jnp.where((index & bit) != 0, split[:, ::-1], split).reshape(array.shape)
        bit *= 2
    return array


def body(
    inputs,
    conds,
    heights,
    widths,
    qkv_weight,
    qv_bias,
    out_weight,
    out_bias,
    up_weight,
    up_bias,
    down_weight,
    down_bias,
    mod_weight,
    mod_bias,
    cotangent,
):
    devices = lax.axis_size("batch")
    b, s = lax.axis_index("batch"), lax.axis_index("seq")
    c = b & 1
    width = inputs.shape[2]
    hidden = up_weight.shape[1]
    slot_dev = inputs.shape[1]
    half = slot_dev // 2
    rows = qkv_weight.shape[0]
    mods = mod_weight.shape[1]

    tokens16 = deal(inputs)
    upstream16 = deal(cotangent)

    core = jnp.reshape(c, (1,)).astype(jnp.int32)
    qkv_hops = Hops(qkv_weight)

    small = [conds.reshape(-1), qv_bias, out_bias, up_bias, down_bias, heights.astype(bf16), widths.astype(bf16)]
    spots = [sum(e.size for e in small[:i]) for i in range(len(small) + 1)]
    small.append(jnp.zeros((-spots[-1] % 128,), bf16))
    small = gather(jnp.concatenate(small)[None])
    every = [small[:, spots[i] : spots[i + 1]] for i in range(7)]
    cond_all = every[0].reshape(2 * devices, width)
    qv_offset, out_offset, up_offset, down_offset = (e.reshape(-1).astype(f32) for e in every[1:5])
    counts = (every[5].astype(jnp.int32) * every[6].astype(jnp.int32)).reshape(2 * devices)
    sample = 4 * (b // 2) + s
    count = lax.dynamic_index_in_dim(counts, sample, keepdims=False)

    silu_all = jax.nn.silu(cond_all.astype(f32)).astype(bf16)
    silu_rows = lax.dynamic_slice(silu_all, (0, b * rows), (2 * devices, rows))
    plane = lax.dynamic_index_in_dim(silu_rows.reshape(devices // 2, 4, rows), s, axis=1, keepdims=False)
    partial = dot(plane, mod_weight)
    qkv_pieces = qkv_hops.pieces(partial, tokens16)
    out_pieces = Hops(after(out_weight, qkv_hops.moving)).pieces()
    up_matrix = gather(after(up_weight, qkv_hops.moving))
    own_bias = lax.dynamic_update_slice(jnp.zeros((mods,), f32), mod_bias.astype(f32), (b * mod_bias.shape[0],))
    partial = partial + own_bias[None]
    partial = jnp.broadcast_to(partial[:, None], (devices // 2, 2, mods)).reshape(devices, mods)
    modulation = jnp.sum(lax.all_to_all(partial, "batch", 0, 0, tiled=True), axis=0, keepdims=True)
    shift1, scale1, gate1, shift2, scale2, gate2 = jnp.split(modulation, 6, axis=-1)

    limits = []
    for part in range(2):
        side = c ^ part
        base = (s & 1) | (((s >> 1) ^ side) << 1)
        for turn in range(4):
            limits.append(count - (slot_dev * (base ^ turn) + half * side))
    limits = jnp.stack(limits).astype(jnp.int32)

    offsets = jnp.concatenate([qv_offset[:width], jnp.zeros((width,), f32), qv_offset[width:]])
    mine, away, moved, qkv_matrix = project(core, qkv_pieces, tokens16, modulation, offsets[None])
    theirs = pair_swap(away)
    down_matrix = gather(after(down_weight, mine))
    att_mine, att_away, lse = attend(limits, mine, theirs)
    att_mine = after(att_mine, upstream16)
    attended, projected, normed2, factor2, moved2, out_matrix = middle_part(
        core, out_pieces, att_mine, pair_swap(att_away), tokens16, modulation, out_offset[None]
    )
    act, slope = up_part(moved2, up_matrix, up_offset[None])

    d_lowered = (gate2 * upstream16.astype(f32)).astype(bf16)
    down_offset_grad = jnp.sum(d_lowered.astype(f32), axis=0)
    down_g = Grad(act, d_lowered, True)
    mark = down_g.away(act)
    d_upper, up_sums = slope_part(after(d_lowered, mark), down_matrix, slope)
    mark = down_g.stay(d_upper)
    up_g = Grad(moved2, d_upper)
    mark = up_g.away(mark)
    mark = down_g.mix(mark)
    d_middle, d_projected, d_att_mine, d_att_away, sums2 = middle_back(
        core, after(d_upper, mark), up_matrix, normed2, factor2, projected, upstream16, modulation, out_matrix
    )
    d_shift2, d_scale2, d_gate1, out_offset_grad = sums2
    d_att_theirs = pair_swap(d_att_away)
    mark = up_g.stay(d_att_mine)
    out_g = Grad(attended, d_projected)
    mark = out_g.away(mark)
    mark = out_g.stay(mark)
    mark, down_total = down_g.finish(mark)
    mark = up_g.mix(mark)
    heads = HEADS // 2
    steps = 2
    own, got = [], []
    for i in range(steps):
        made = attend_back(
            limits, after(mine, mark), theirs, d_att_mine, d_att_theirs, lse, i * heads // steps, heads // steps
        )
        own.append(made[0])
        got.append(pair_swap(made[1]))
        mark = made
    mark = out_g.mix(mark)
    up_part_sum, up_total = up_g.finish(mark, down_total)
    mark = up_part_sum
    d_qkv = join_heads(core, own, got)
    qkv_g = Grad(moved, d_qkv)
    mark = qkv_g.away(mark)
    mark, out_total = out_g.finish(mark, down_total)
    input_grad, sums1, column_sums = input_back(after(d_qkv, mark), qkv_matrix, tokens16, modulation, d_middle)
    d_shift1, d_scale1 = sums1
    mark = qkv_g.stay(input_grad)
    input_grad = undeal(after(input_grad, mark)).astype(f32)
    column_sums = after(column_sums[0], mark)
    qv_offset_grad = jnp.concatenate([column_sums[:width], column_sums[2 * width :]])
    own_shapes = (qv_bias.shape[0], out_bias.shape[0], up_bias.shape[0], down_bias.shape[0])
    bias = jnp.concatenate(
        [
            g.reshape(devices, -1)
            for g in (qv_offset_grad, out_offset_grad, up_sums, down_offset_grad)
        ],
        axis=1,
    )
    length = bias.shape[1]
    bias = jnp.sum(lax.all_to_all(bias, "batch", 0, 0, tiled=True), axis=0, keepdims=True)
    bias = jnp.pad(bias, ((0, 7), (0, 3 * width - length)))
    output, d_gate2 = down_part(
        after(act, mark), down_matrix, down_offset[None], tokens16, projected, modulation, upstream16
    )
    mark = qkv_g.mix(output)
    output = undeal(after(output, mark))
    mark, qkv_total = qkv_g.finish(mark, up_total, out_total, extra=bias)

    partial_mod = jnp.concatenate([d_shift1, d_scale1, d_gate1, d_shift2, d_scale2, d_gate2[0]])
    partial_mod = after(partial_mod, mark)
    d_mod = (partial_mod + pair_swap(partial_mod)).astype(bf16)
    d_mod_all = all_samples(d_mod)
    mod_grad = dot(xor_order(silu_rows, sample), d_mod_all, TN)
    mod_offset_grad = jnp.sum(
        lax.dynamic_slice(d_mod_all, (0, b * mod_bias.shape[0]), (2 * devices, mod_bias.shape[0])).astype(f32), axis=0
    )
    d_silu_rows = xor_order(dot(d_mod_all, mod_weight, NT), sample)
    d_silu = lax.all_to_all(d_silu_rows.reshape(devices, 2 * rows), "batch", 0, 0, tiled=True)
    d_silu = d_silu.reshape(devices, 2, rows).transpose(1, 0, 2).reshape(2, width)
    cond_grad = jax.vjp(jax.nn.silu, conds.astype(f32))[1](d_silu)[0]

    down_grad, up_grad, out_grad = (grad.result(d_mod_all) for grad in (down_g, up_g, out_g))
    qkv_grad, bias = qkv_g.result()
    bias = bias[0, :length]
    cuts = [sum(own_shapes[:i]) for i in range(5)]
    qv_b, out_b, up_b, down_b = (bias[cuts[i] : cuts[i + 1]] for i in range(4))
    return (
        output,
        input_grad,
        cond_grad,
        qkv_grad,
        qv_b,
        out_grad,
        out_b,
        up_grad,
        up_b,
        down_grad,
        down_b,
        mod_grad,
        mod_offset_grad,
    )


def solution(mesh):
    in_specs = (
        P("batch", "seq", None),
        P("batch", None),
        P("batch"),
        P("batch"),
        P("batch", None),
        P("batch"),
        P("batch", None),
        P("batch"),
        P("batch", None),
        P("batch"),
        P("batch", None),
        P("batch"),
        P("batch", None),
        P("batch"),
        P("batch", "seq", None),
    )
    out_specs = (
        P("batch", "seq", None),
        P("batch", "seq", None),
        P("batch", None),
        P("batch", None),
        P("batch"),
        P("batch", None),
        P("batch"),
        P("batch", None),
        P("batch"),
        P("batch", None),
        P("batch"),
        P("batch", None),
        P("batch"),
    )
    return jax.shard_map(body, mesh=mesh, in_specs=in_specs, out_specs=out_specs, check_vma=False)
```

```python
import functools

import jax
import jax.numpy as jnp
from jax import lax
from jax.experimental import pallas as pl
from jax.experimental.pallas import tpu as pltpu
from jax.sharding import PartitionSpec as P

HEADS = 16
HEAD = 72
SCALE = HEAD ** (-0.5)
LOG2E = 1.4426950408889634
f32 = jnp.float32
bf16 = jnp.bfloat16
NT = (((1,), (1,)), ((), ()))
TN = (((0,), (0,)), ((), ()))


def dot(a, b, dims=(((1,), (0,)), ((), ()))):
    return lax.dot_general(a, b, dims, preferred_element_type=f32)


WHOLE = pl.BlockSpec()
SMEM = pl.BlockSpec(memory_space=pltpu.SMEM)
HBM = pl.BlockSpec(memory_space=pltpu.HBM)
BLOCK = 512
PAD = 128
ROOT = 0.7978845608028654
EARLY = 0.6
VMEM_ATT = 48


def lasts(microseconds):
    return pl.CostEstimate(
        flops=int(EARLY * microseconds * 1e9), bytes_accessed=int(EARLY * microseconds * 3.3e6), transcendentals=0
    )


def shaped(shape, kind):
    return pltpu.HBM(shape, kind)


def in_hbm(*arrays):
    return tuple(pltpu.with_memory_space_constraint(array, pltpu.HBM) for array in arrays)


def lanes(wide):
    return -(-wide // 128) * 128


def params(mib):
    return pltpu.CompilerParams(vmem_limit_bytes=mib * 2**20)


def on_core(core, work):
    for c in range(2):
        pl.when(core[0] == c)(functools.partial(work, c))


def split_kernel(core, source, mine, away):
    wide = source.shape[1] // 2

    def work(c):
        for ref, d in ((mine, c), (away, 1 - c)):
            ref[:, :wide] = source[:, d * wide : (d + 1) * wide]

    on_core(core, work)


def split_heads(core, array):
    rows, wide = array.shape[0], array.shape[1] // 2
    return pl.pallas_call(
        split_kernel,
        out_shape=(shaped((rows, wide), bf16), shaped((rows, lanes(wide)), bf16)),
        in_specs=[SMEM, WHOLE],
        out_specs=(WHOLE,) * 2,
        compiler_params=params(48),
        cost_estimate=lasts(2),
    )(core, *in_hbm(array))


def join_kernel(steps, core, *refs):
    own, got, whole = refs[:steps], refs[steps : 2 * steps], refs[2 * steps]
    narrow = own[0].shape[1] // 3
    wide = 2 * narrow * steps

    def work(c):
        for kind in range(3):
            for d, arrays in ((c, own), (1 - c, got)):
                for i, ref in enumerate(arrays):
                    at = kind * wide + (d * steps + i) * narrow
                    whole[:, at : at + narrow] = ref[:, kind * narrow : (kind + 1) * narrow]

    on_core(core, work)


def join_heads(core, own, got):
    steps, (rows, wide) = len(own), own[0].shape
    return pl.pallas_call(
        functools.partial(join_kernel, steps),
        out_shape=shaped((rows, 2 * steps * wide), own[0].dtype),
        in_specs=[SMEM] + [WHOLE] * (2 * steps),
        out_specs=WHOLE,
        compiler_params=params(48),
        cost_estimate=lasts(2),
    )(core, *in_hbm(*own, *got))


def assemble(spots, pieces, matrix, sems):
    copies = []
    for i, piece in enumerate(pieces):
        rows = pl.ds(pl.multiple_of(spots[i], 16), piece.shape[0])
        copies.append(pltpu.make_async_copy(piece, matrix.at[rows], sems.at[i]))
    for copy in copies:
        copy.start()
    for copy in copies:
        copy.wait()


def norm_rows(value):
    centre = value - jnp.mean(value, axis=1, keepdims=True)
    scale = lax.rsqrt(jnp.mean(centre * centre, axis=1, keepdims=True) + 1e-06)
    return centre * scale, scale


def back_rows(grad, normed, scale):
    return scale * (
        grad - jnp.mean(grad, axis=1, keepdims=True) - normed * jnp.mean(grad * normed, axis=1, keepdims=True)
    )


def row_chunks(rows, step=128):
    return [slice(i, i + step) for i in range(0, rows, step)]


def project_kernel(core, tokens, mods, offset, matrix, mine, away, moved, made):
    width = tokens.shape[1]
    half = width // 2

    @pl.when(pl.program_id(0) == 0)
    def _():
        for at in row_chunks(tokens.shape[0]):
            normed, _ = norm_rows(tokens[at, :].astype(f32))
            moved[at, :] = (normed * (1.0 + mods[:, width : 2 * width]) + mods[:, :width]).astype(bf16)

    made[...] = (dot(moved[...], matrix[...]) + offset[...]).astype(bf16)
    for kind in range(3):

        @pl.when(pl.program_id(0) == kind)
        def _():
            def work(c):
                for ref, d in ((mine, c), (away, 1 - c)):
                    ref[:, kind * half : (kind + 1) * half] = made[:, d * half : (d + 1) * half]

            on_core(core, work)


def project(core, matrix, tokens, mods, offset):
    rows, width = tokens.shape
    wide = matrix.shape[1]
    return pl.pallas_call(
        project_kernel,
        out_shape=(
            shaped((rows, wide // 2), bf16),
            shaped((rows, lanes(wide // 2)), bf16),
            shaped((rows, width), bf16),
        ),
        grid=(3,),
        in_specs=[
            SMEM,
            WHOLE,
            WHOLE,
            pl.BlockSpec((1, width), lambda i: (0, i)),
            pl.BlockSpec((width, width), lambda i: (0, i)),
        ],
        out_specs=(WHOLE,) * 3,
        scratch_shapes=[pltpu.VMEM((rows, width), bf16)],
        compiler_params=params(48),
        cost_estimate=lasts(13),
    )(core, *in_hbm(tokens, mods, offset, matrix))


def middle_kernel(number, core, spots, own, got, tokens, mods, offset, *refs):
    pieces = refs[:number]
    attended, projected, normed, factor, moved, whole, matrix, sems, out_sem = refs[number:]
    assemble(spots, pieces, matrix, sems)
    out = pltpu.make_async_copy(matrix, whole, out_sem)
    out.start()
    width = matrix.shape[1]
    half = width // 2

    def work(c):
        attended[:, c * half : (c + 1) * half] = own[...]
        attended[:, (1 - c) * half : (2 - c) * half] = got[:, :half]

    on_core(core, work)
    gate1, shift2, scale2 = (mods[:, i * width : (i + 1) * width] for i in (2, 3, 4))
    projected[...] = dot(attended[...], matrix[...]) + offset[...]
    for at in row_chunks(own.shape[0]):
        made = projected[at, :]
        value = tokens[at, :].astype(f32) + gate1 * made
        value, scale = norm_rows(value)
        normed[at, :] = value
        factor[at, :] = scale
        moved[at, :] = (value * (1.0 + scale2) + shift2).astype(bf16)
    out.wait()


def middle_part(core, gathered, own, got, tokens, mods, offset):
    spots, pieces = gathered
    rows, width = tokens.shape
    return pl.pallas_call(
        functools.partial(middle_kernel, len(pieces)),
        out_shape=(
            shaped((rows, width), bf16),
            shaped((rows, width), f32),
            shaped((rows, width), f32),
            shaped((rows, 1), f32),
            shaped((rows, width), bf16),
            shaped((width, width), bf16),
        ),
        in_specs=[SMEM, SMEM] + [WHOLE] * 5 + [HBM] * len(pieces),
        out_specs=(WHOLE,) * 5 + (HBM,),
        scratch_shapes=[
            pltpu.VMEM((width, width), bf16),
            pltpu.SemaphoreType.DMA((len(pieces),)),
            pltpu.SemaphoreType.DMA,
        ],
        compiler_params=params(48),
        cost_estimate=lasts(9),
    )(core, spots, *in_hbm(own, got, tokens, mods, offset, *pieces))


def up_kernel(moved, matrix, offset, act, slope):
    for at in row_chunks(moved.shape[0], 256):
        u = dot(moved[at, :], matrix[...]) + offset[...]
        square = u * u
        t = jnp.tanh(ROOT * (u + 0.044715 * (square * u)))
        act[at, :] = (0.5 * u * (1.0 + t)).astype(bf16)
        slope[at, :] = 0.5 * (1.0 + t) + (0.5 * ROOT) * u * (1.0 - t * t) * (1.0 + (3 * 0.044715) * square)


def up_part(moved, matrix, offset):
    (rows, width), hidden = moved.shape, matrix.shape[1]
    step = hidden // 4
    return pl.pallas_call(
        up_kernel,
        out_shape=(shaped((rows, hidden), bf16), shaped((rows, hidden), f32)),
        grid=(4,),
        in_specs=[WHOLE, pl.BlockSpec((width, step), lambda i: (0, i)), pl.BlockSpec((1, step), lambda i: (0, i))],
        out_specs=(pl.BlockSpec((rows, step), lambda i: (0, i)), pl.BlockSpec((rows, step), lambda i: (0, i))),
        compiler_params=params(48),
        cost_estimate=lasts(16),
    )(*in_hbm(moved, matrix, offset))


def slope_kernel(number, spots, grad, slope, *refs):
    pieces = refs[:number]
    d_upper, sums, whole, matrix, sems, out_sem = refs[number:]
    step = pl.program_id(0)
    size = sums.shape[1]
    out = pltpu.make_async_copy(matrix, whole, out_sem)

    @pl.when(step == 0)
    def _():
        assemble(spots, pieces, matrix, sems)
        out.start()

    part = matrix.at[pl.ds(pl.multiple_of(step * size, size), size)]
    total = jnp.zeros(sums.shape, f32)
    for at in row_chunks(grad.shape[0], 256):
        value = (dot(grad[at, :], part[...], NT) * slope[at, :]).astype(bf16)
        d_upper[at, :] = value
        total = total + jnp.sum(value.astype(f32), axis=0, keepdims=True)
    sums[...] = total

    @pl.when(step == pl.num_programs(0) - 1)
    def _():
        out.wait()


def slope_part(grad, gathered, slope):
    spots, pieces = gathered
    (rows, width), hidden = grad.shape, slope.shape[1]
    step = hidden // 4
    across = pl.BlockSpec((rows, step), lambda i: (0, i))
    return pl.pallas_call(
        functools.partial(slope_kernel, len(pieces)),
        out_shape=(shaped((rows, hidden), bf16), shaped((1, hidden), f32), shaped((hidden, width), bf16)),
        grid=(4,),
        in_specs=[SMEM, WHOLE, across] + [HBM] * len(pieces),
        out_specs=(across, pl.BlockSpec((1, step), lambda i: (0, i)), HBM),
        scratch_shapes=[
            pltpu.VMEM((hidden, width), bf16),
            pltpu.SemaphoreType.DMA((len(pieces),)),
            pltpu.SemaphoreType.DMA,
        ],
        compiler_params=params(48),
        cost_estimate=lasts(40),
    )(spots, *in_hbm(grad, slope, *pieces))


def down_kernel(act, matrix, offset, tokens, projected, mods, grad, output, d_gate, total):
    step = pl.program_id(0)
    width = matrix.shape[1]

    @pl.when(step == 0)
    def _():
        total[...] = dot(act[...], matrix[...])

    @pl.when(step > 0)
    def _():
        total[...] += dot(act[...], matrix[...])

    @pl.when(step == pl.num_programs(0) - 1)
    def _():
        gate1, gate2 = mods[:, 2 * width : 3 * width], mods[:, 5 * width :]
        summed = jnp.zeros(d_gate.shape, f32)
        for at in row_chunks(act.shape[0]):
            lowered = total[at, :] + offset[...]
            middle = tokens[at, :].astype(f32) + gate1 * projected[at, :]
            output[at, :] = (middle + gate2 * lowered).astype(bf16)
            summed = summed + jnp.sum(grad[at, :].astype(f32) * lowered, axis=0, keepdims=True)
        d_gate[...] = summed


def down_part(act, matrix, offset, tokens, projected, mods, grad):
    rows, hidden = act.shape
    step, width = hidden // 4, matrix.shape[1]
    return pl.pallas_call(
        down_kernel,
        out_shape=(shaped((rows, width), bf16), shaped((1, width), f32)),
        grid=(4,),
        in_specs=[pl.BlockSpec((rows, step), lambda i: (0, i)), pl.BlockSpec((step, width), lambda i: (i, 0))]
        + [WHOLE] * 5,
        out_specs=(WHOLE, WHOLE),
        scratch_shapes=[pltpu.VMEM((rows, width), f32)],
        compiler_params=params(48),
        cost_estimate=lasts(6),
    )(*in_hbm(act, matrix, offset, tokens, projected, mods, grad))


def middle_back_kernel(core, d_upper, matrix, normed, factor, projected, grad, mods, out_matrix, d_middle, d_projected, mine, away, sums, total):
    step = pl.program_id(0)
    width = matrix.shape[0]
    half = width // 2

    @pl.when(step == 0)
    def _():
        total[...] = dot(d_upper[...], matrix[...], NT)

    @pl.when(step > 0)
    def _():
        total[...] += dot(d_upper[...], matrix[...], NT)

    @pl.when(step == pl.num_programs(0) - 1)
    def _():
        gate1, scale2 = mods[:, 2 * width : 3 * width], mods[:, 4 * width : 5 * width]
        summed = [jnp.zeros((1, width), f32) for _ in range(4)]
        for at in row_chunks(grad.shape[0]):
            d_moved, n = total[at, :], normed[at, :]
            value = grad[at, :].astype(f32) + back_rows(d_moved * (1.0 + scale2), n, factor[at, :])
            d_middle[at, :] = value
            d_proj = (gate1 * value).astype(bf16)
            d_projected[at, :] = d_proj
            terms = d_moved, d_moved * n, value * projected[at, :], d_proj.astype(f32)
            summed = [u + jnp.sum(v, axis=0, keepdims=True) for u, v in zip(summed, terms)]
        total[...] = dot(d_projected[...], out_matrix[...], NT)

        def work(c):
            mine[...] = total[:, c * half : (c + 1) * half].astype(bf16)
            away[:, :half] = total[:, (1 - c) * half : (2 - c) * half].astype(bf16)

        on_core(core, work)
        for i, value in enumerate(summed):
            sums[i : i + 1, :] = value


def middle_back(core, d_upper, matrix, normed, factor, projected, grad, mods, out_matrix):
    rows, hidden = d_upper.shape
    step, width = hidden // 4, matrix.shape[0]
    return pl.pallas_call(
        middle_back_kernel,
        out_shape=(
            shaped((rows, width), f32),
            shaped((rows, width), bf16),
            shaped((rows, width // 2), bf16),
            shaped((rows, lanes(width // 2)), bf16),
            shaped((4, width), f32),
        ),
        grid=(4,),
        in_specs=[SMEM, pl.BlockSpec((rows, step), lambda i: (0, i)), pl.BlockSpec((width, step), lambda i: (0, i))]
        + [WHOLE] * 6,
        out_specs=(WHOLE,) * 5,
        scratch_shapes=[pltpu.VMEM((rows, width), f32)],
        compiler_params=params(48),
        cost_estimate=lasts(150),
    )(core, *in_hbm(d_upper, matrix, normed, factor, projected, grad, mods, out_matrix))


def input_back_kernel(d_qkv, matrix, tokens, mods, d_middle, input_grad, sums, columns, total):
    step = pl.program_id(0)
    width = matrix.shape[0]
    columns[...] = jnp.sum(d_qkv[...].astype(f32), axis=0, keepdims=True)

    @pl.when(step == 0)
    def _():
        total[...] = dot(d_qkv[...], matrix[...], NT)

    @pl.when(step > 0)
    def _():
        total[...] += dot(d_qkv[...], matrix[...], NT)

    @pl.when(step == pl.num_programs(0) - 1)
    def _():
        scale1 = mods[:, width : 2 * width]
        summed = [jnp.zeros((1, width), f32) for _ in range(2)]
        for at in row_chunks(tokens.shape[0]):
            normed, factor = norm_rows(tokens[at, :].astype(f32))
            d_moved = total[at, :]
            input_grad[at, :] = (d_middle[at, :] + back_rows(d_moved * (1.0 + scale1), normed, factor)).astype(bf16)
            summed = [u + jnp.sum(v, axis=0, keepdims=True) for u, v in zip(summed, (d_moved, d_moved * normed))]
        for i, value in enumerate(summed):
            sums[i : i + 1, :] = value


def input_back(d_qkv, matrix, tokens, mods, d_middle):
    rows, wide = d_qkv.shape
    width = matrix.shape[0]
    return pl.pallas_call(
        input_back_kernel,
        out_shape=(shaped((rows, width), bf16), shaped((2, width), f32), shaped((1, wide), f32)),
        grid=(wide // width,),
        in_specs=[pl.BlockSpec((rows, width), lambda i: (0, i)), pl.BlockSpec((width, width), lambda i: (0, i))]
        + [WHOLE] * 3,
        out_specs=(WHOLE, WHOLE, pl.BlockSpec((1, width), lambda i: (0, i))),
        scratch_shapes=[pltpu.VMEM((rows, width), f32)],
        compiler_params=params(48),
        cost_estimate=lasts(40),
    )(*in_hbm(d_qkv, matrix, tokens, mods, d_middle))


def cut_of(rows):
    return rows // 2 // 8 * 8


def keep(made, e, value):
    if len(made) == 1:
        made[0][e] = value
    elif e == 3 and len(made) == 5:
        cut = made[3].shape[0]
        made[3][...], made[4][...] = value[:cut], value[cut:]
    else:
        made[e][...] = value


def pair_grad_kernel(added, where, left, right, *refs):
    gots, made = refs[:added], refs[added:]
    half = left.shape[1] // 2
    step = pl.program_id(0)
    for d in range(2):

        @pl.when(where[1] == d)
        def _():
            value = dot(left[:, d * half : (d + 1) * half], right[...], TN)
            for e in range(4):

                @pl.when(step == e)
                def _():
                    more = gots[0][e].astype(f32) if added else 0.0
                    keep(made, e, (value + more).astype(bf16))


def grad_shapes(rows, columns, added):
    cut = cut_of(rows)
    return [(rows, columns)] * 3 + [(cut, columns), (rows - cut, columns)] if added else [(4, rows, columns)]


def pair_grad(left, right, b, side, gots=()):
    slots, wide = left.shape
    step = wide // 4
    where = jnp.stack([b >> 1, side]).astype(jnp.int32)
    shapes = grad_shapes(step // 2, right.shape[1], len(gots))
    whole = lambda shape: pl.BlockSpec(shape, lambda m, where: (0,) * len(shape))
    specs = [pl.BlockSpec((slots, step), lambda m, where: (0, where[0] ^ m)), whole(right.shape)]
    return pl.pallas_call(
        functools.partial(pair_grad_kernel, len(gots)),
        out_shape=tuple(shaped(shape, bf16) for shape in shapes),
        grid_spec=pltpu.PrefetchScalarGridSpec(
            num_scalar_prefetch=1,
            grid=(4,),
            in_specs=specs + [whole(got.shape) for got in gots],
            out_specs=tuple(whole(shape) for shape in shapes),
        ),
        compiler_params=params(48),
        cost_estimate=lasts(9),
    )(where, *in_hbm(left, right, *gots))


def block_grad_kernel(added, spots, left, right, *refs):
    gots, made, (chosen, turned) = refs[:added], refs[added:-2], refs[-2:]
    rows = made[0].shape[-2]

    @pl.when(pl.program_id(0) == 0)
    def _():
        turned[...] = jnp.transpose(left[...])
        for e in range(4):
            at = pl.ds(pl.multiple_of(spots[e], 16), rows)
            chosen[e * rows : (e + 1) * rows, :] = turned[at, :]

    value = dot(chosen[...], right[...])
    for e in range(4):
        part = value[e * rows : (e + 1) * rows, :]
        if added:
            part = part + gots[0][e].astype(f32)
        keep(made, e, part.astype(bf16))


def block_grad(left, right, b, side, gots=()):
    (slots, wide), columns = left.shape, right.shape[1]
    rows = wide // 8
    spots = jnp.stack([((b >> 1) ^ m) * 2 * rows + side * rows for m in range(4)]).astype(jnp.int32)
    step = 1152 if columns % 1152 == 0 else columns
    shapes = grad_shapes(rows, columns, len(gots))
    block = lambda shape: pl.BlockSpec(shape[:-1] + (step,), lambda i: (0,) * (len(shape) - 1) + (i,))
    return pl.pallas_call(
        functools.partial(block_grad_kernel, len(gots)),
        out_shape=tuple(shaped(shape, bf16) for shape in shapes),
        grid=(columns // step,),
        in_specs=[SMEM, WHOLE, pl.BlockSpec((slots, step), lambda i: (0, i))] + [block(got.shape) for got in gots],
        out_specs=tuple(block(shape) for shape in shapes),
        scratch_shapes=[pltpu.VMEM((4 * rows, slots), bf16), pltpu.VMEM((wide, slots), bf16)],
        compiler_params=params(48),
        cost_estimate=lasts(columns // 1152),
    )(spots, *in_hbm(left, right, *gots))


def mix_kernel(to_x, to_y, got_x, got_y, out_x, out_y):
    cut = got_x.shape[0]
    out_x[:cut, :] = to_x[:cut, :]
    out_x[cut:, :] = add(to_x[cut:, :], got_y[...])
    out_y[:cut, :] = add(to_y[:cut, :], got_x[...])
    out_y[cut:, :] = to_y[cut:, :]


def mix(to_x, to_y, got_x, got_y):
    rows, columns = to_x.shape
    step = 1152
    block = lambda array: pl.BlockSpec((array.shape[0], step), lambda i: (0, i))
    return pl.pallas_call(
        mix_kernel,
        out_shape=(shaped(to_x.shape, bf16),) * 2,
        grid=(columns // step,),
        in_specs=[block(array) for array in (to_x, to_y, got_x, got_y)],
        out_specs=(block(to_x),) * 2,
        compiler_params=params(48),
        cost_estimate=lasts(1),
    )(*in_hbm(to_x, to_y, got_x, got_y))


def fill(h, heads, mine, theirs, qs, ks, vs):
    half, wide, lo = mine.shape[0], heads * HEAD, h * HEAD
    for part, ref in ((0, mine), (1, theirs)):
        rows = slice(part * half, (part + 1) * half)
        qs[rows, :HEAD] = ref[:, lo : lo + HEAD]
        ks[rows, :HEAD] = ref[:, wide + lo : wide + lo + HEAD]
        vs[rows, :] = ref[:, 2 * wide + lo : 2 * wide + lo + HEAD]


def mark_valid(limits, qs, ks):
    total = qs.shape[0]
    chunks = limits.shape[0]
    sub = lax.broadcasted_iota(jnp.int32, (total // chunks, 1), 0)
    bias = jnp.concatenate([jnp.where(sub < limits[i], 0.0, -1e30) for i in range(chunks)], axis=0)
    qs[...] = jnp.zeros_like(qs)
    ks[...] = jnp.zeros_like(ks)
    qs[:, HEAD : HEAD + 1] = jnp.ones((total, 1), bf16)
    ks[:, HEAD : HEAD + 1] = bias.astype(bf16)


def attend_kernel(heads, limits, mine, theirs, out_mine, out_theirs, lse, qs, ks, vs, os, ls):
    half = mine.shape[0]
    total = 2 * half
    mark_valid(limits, qs, ks)
    for h in range(heads):
        fill(h, heads, mine, theirs, qs, ks, vs)
        for i in range(total // BLOCK):
            at = slice(i * BLOCK, (i + 1) * BLOCK)
            scores = dot(qs[at, :], ks[...], NT) * (SCALE * LOG2E)
            peak = jnp.max(scores, axis=1, keepdims=True)
            expo = jnp.exp2(scores - peak)
            summed = jnp.sum(expo, axis=1, keepdims=True)
            probs = (expo * (1.0 / summed)).astype(bf16)
            os[at, :] = dot(probs, vs[...]).astype(bf16)
            ls[at, :] = peak + jnp.log2(summed)
        lo = h * HEAD
        out_mine[:, lo : lo + HEAD] = os[:half, :]
        out_theirs[:, lo : lo + HEAD] = os[half:, :]
        lse[h : h + 1, :] = jnp.transpose(ls[...])


def attend(limits, mine, theirs):
    half, wide3 = mine.shape
    wide = wide3 // 3
    heads = wide // HEAD
    total = 2 * half
    return pl.pallas_call(
        functools.partial(attend_kernel, heads),
        out_shape=(shaped((half, wide), bf16), shaped((half, lanes(wide)), bf16), shaped((heads, total), f32)),
        in_specs=[SMEM, WHOLE, WHOLE],
        out_specs=(WHOLE,) * 3,
        scratch_shapes=[
            pltpu.VMEM((total, PAD), bf16),
            pltpu.VMEM((total, PAD), bf16),
            pltpu.VMEM((total, HEAD), bf16),
            pltpu.VMEM((total, HEAD), bf16),
            pltpu.VMEM((total, 1), f32),
        ],
        compiler_params=params(VMEM_ATT),
        cost_estimate=lasts(27),
    )(limits, *in_hbm(mine, theirs))


def back_kernel(heads, first, number, limits, mine, theirs, d_mine, d_theirs, lse, out_mine, out_theirs, qs, ks, vs, ds, dq, dk, dv):
    half = mine.shape[0]
    total = 2 * half
    narrow = number * HEAD
    mark_valid(limits, qs, ks)
    for h in range(first, first + number):
        fill(h, heads, mine, theirs, qs, ks, vs)
        lo = h * HEAD
        ds[:half, :] = d_mine[:, lo : lo + HEAD]
        ds[half:, :] = d_theirs[:, lo : lo + HEAD]
        for i in range(total // BLOCK):
            at = slice(i * BLOCK, (i + 1) * BLOCK)
            query, d_out = qs[at, :], ds[at, :]
            exact = jnp.exp2(dot(ks[...], query, NT) * (SCALE * LOG2E) - lse[h : h + 1, at])
            d_probs = dot(vs[...], d_out, NT)
            more = dot(exact.astype(bf16), d_out)
            dv[...] = more if i == 0 else dv[...] + more
            product = exact * d_probs
            centred = jnp.sum(product, axis=0, keepdims=True)
            d_scores = (product - exact * centred).astype(bf16)
            more = dot(d_scores, query)
            dk[...] = more if i == 0 else dk[...] + more
            dq[at, :] = (dot(d_scores, ks[...], TN) * SCALE).astype(bf16)
        lo = (h - first) * HEAD
        for part, ref in ((0, out_mine), (1, out_theirs)):
            rows = slice(part * half, (part + 1) * half)
            ref[:, lo : lo + HEAD] = dq[rows, :HEAD]
            ref[:, narrow + lo : narrow + lo + HEAD] = (dk[rows, :HEAD] * SCALE).astype(bf16)
            ref[:, 2 * narrow + lo : 2 * narrow + lo + HEAD] = dv[rows, :].astype(bf16)


def attend_back(limits, mine, theirs, d_mine, d_theirs, lse, first, number):
    half, wide3 = mine.shape
    wide = wide3 // 3
    heads = wide // HEAD
    total = 2 * half
    return pl.pallas_call(
        functools.partial(back_kernel, heads, first, number),
        out_shape=(shaped((half, 3 * number * HEAD), bf16), shaped((half, lanes(3 * number * HEAD)), bf16)),
        in_specs=[SMEM] + [WHOLE] * 5,
        out_specs=(WHOLE,) * 2,
        scratch_shapes=[
            pltpu.VMEM((total, PAD), bf16),
            pltpu.VMEM((total, PAD), bf16),
            pltpu.VMEM((total, HEAD), bf16),
            pltpu.VMEM((total, HEAD), bf16),
            pltpu.VMEM((total, PAD), bf16),
            pltpu.VMEM((total, PAD), f32),
            pltpu.VMEM((total, HEAD), f32),
        ],
        compiler_params=params(VMEM_ATT),
        cost_estimate=lasts(17),
    )(limits, *in_hbm(mine, theirs, d_mine, d_theirs, lse))


def pair_swap(array):
    size = lax.axis_size("batch")
    return lax.ppermute(array, "batch", [(i, i ^ 1) for i in range(size)])


def by_core(own, other):
    first = (lax.axis_index("batch") & 1) == 0
    return jnp.where(first, jnp.stack([own, other]), jnp.stack([other, own]))


def deal(array):
    c = lax.axis_index("batch") & 1
    samples, slots, width = array.shape
    halves = array.reshape(samples, 2, slots // 2, width)
    own = lax.dynamic_index_in_dim(halves, c, axis=1, keepdims=False)
    other = pair_swap(lax.dynamic_index_in_dim(halves, 1 - c, axis=1, keepdims=False))
    every = by_core(own, other).reshape(2 * samples, slots // 2, width)
    return lax.all_to_all(every, "seq", 0, 0, tiled=True).reshape(samples * slots, width)


def undeal(array):
    c = lax.axis_index("batch") & 1
    rows, width = array.shape
    every = lax.all_to_all(array.reshape(4, rows // 4, width), "seq", 0, 0, tiled=True)
    every = every.reshape(2, 2, rows // 4, width)
    own = lax.dynamic_index_in_dim(every, c, axis=0, keepdims=False)
    other = pair_swap(lax.dynamic_index_in_dim(every, 1 - c, axis=0, keepdims=False))
    return by_core(own, other).transpose(1, 0, 2, 3).reshape(2, rows // 2, width)


def gather(array):
    return lax.all_gather(array, "batch", axis=0, tiled=True)


def hop(array, bits):
    size = lax.axis_size("batch")
    return lax.ppermute(array, "batch", [(i, i ^ bits) for i in range(size)])


class Hops:
    def __init__(self, array):
        self.array = array
        self.plain = lax.axis_size("batch") != 8
        if self.plain:
            self.whole = gather(array)
            self.moving = (self.whole,)
        else:
            self.moving = self.along_x, self.along_y = hop(array, 2), hop(array, 4)

    def turn(self, *done):
        if self.plain:
            return self.moving
        self.cut = self.array.shape[0] // 2 // 16 * 16
        self.along_x, self.along_y = after((self.along_x, self.along_y), *done)
        self.corner = hop(self.along_x[: self.cut], 4), hop(self.along_y[self.cut :], 2)
        self.moving = self.along_x, self.along_y, *self.corner
        return self.moving

    def pieces(self, *done):
        if self.plain:
            return jnp.zeros((1,), jnp.int32), [self.whole]
        rows, cut = self.array.shape[0], self.cut
        b = lax.axis_index("batch")
        along_x, along_y, *corner = after(self.moving, *done)
        pieces = [(0, 0, self.array), (2, 0, along_x), (4, 0, along_y), (6, 0, corner[0]), (6, cut, corner[1])]
        pieces += [(bits ^ 1, at, hop(piece, 1)) for bits, at, piece in pieces]
        spots = jnp.stack([(b ^ bits) * rows + at for bits, at, _ in pieces]).astype(jnp.int32)
        return spots, [piece for _, _, piece in pieces]


def after(value, *done):
    return lax.optimization_barrier((value, done))[0]


def add(u, v):
    return (u.astype(f32) + v.astype(f32)).astype(bf16)


class Grad:
    def __init__(self, left, right, paired=False):
        self.left, self.right, self.paired = left, right, paired
        self.rows = left.shape[1] // lax.axis_size("batch")
        self.plain = lax.axis_size("batch") != 8 or lax.axis_size("seq") != 4

    def away(self, *done):
        if self.plain:
            made = self.made = dot(after(self.left, *done), self.right, TN).astype(bf16)
            return made
        self.left = after(self.left, *done)
        b = lax.axis_index("batch")
        made = (pair_grad if self.paired else block_grad)(self.left, self.right, b, 1 - (b & 1))
        self.gots = [hop(made[0], 1)]
        return made

    def stay(self, *done):
        if self.plain:
            part = lax.psum_scatter(self.made, "batch", scatter_dimension=0, tiled=True)
            self.part = lax.psum(part, "seq")
            return self.part
        self.left = after(self.left, *done)
        b = lax.axis_index("batch")
        made = (pair_grad if self.paired else block_grad)(self.left, self.right, b, b & 1, self.gots)
        self.own, self.to_x, self.to_y, corner_x, corner_y = made
        self.got_x, self.got_y = hop(corner_x, 2), hop(corner_y, 4)
        return made

    def mix(self, *done):
        if self.plain:
            return self.part
        to_x, to_y = after((self.to_x, self.to_y), *done)
        made = mix(to_x, to_y, self.got_x, self.got_y)
        self.got_x, self.got_y = hop(made[0], 2), hop(made[1], 4)
        return made

    def finish(self, *done, extra=None):
        if self.plain:
            return (self.land(extra=extra),) * 2
        own = after(self.own, *done)
        part = (own.astype(f32) + self.got_x.astype(f32) + self.got_y.astype(f32)).astype(bf16)
        if extra is not None:
            part = jnp.concatenate([part, extra.astype(bf16)], axis=0)
        total = lax.psum(part, "seq")
        self.part, self.plain = total[: self.rows], True
        if extra is not None:
            self.extra = total[self.rows :].astype(f32)
        return part, total

    def land(self, *done, extra=None, chunks=1):
        if self.plain:
            if extra is not None:
                self.extra = lax.psum(extra, "seq")
            return self.part
        own = after(self.own, *done)
        part = (own.astype(f32) + self.got_x.astype(f32) + self.got_y.astype(f32)).astype(bf16)
        if extra is not None:
            part = jnp.concatenate([part, extra.astype(bf16)], axis=0)
        step = -(-part.shape[0] // chunks // 8) * 8
        self.parts = [part[i * step : (i + 1) * step] for i in range(chunks)]
        self.gots = [lax.ppermute(part, "seq", [(0, 1), (3, 2)]) for part in self.parts]
        return part

    def pass_on(self, pairs, done):
        if self.plain:
            return self.part
        parts = after(tuple(self.parts), *done)
        self.parts, gots = [], self.gots
        self.gots = []
        for part, got in zip(parts, gots):
            part = add(part, got)
            self.parts.append(part)
            self.gots.append(lax.ppermute(part, "seq", pairs))
        return tuple(self.parts)

    def across(self, *done):
        return self.pass_on([(1, 2), (2, 1)], done)

    def outward(self, *done):
        return self.pass_on([(1, 0), (2, 3)], done)

    def result(self, *done):
        if self.plain:
            part = after(self.part, *done).astype(f32)
            return part if not hasattr(self, "extra") else (part, self.extra)
        s = lax.axis_index("seq")
        ends = (s == 0) | (s == 3)
        parts = after(tuple(self.parts), *done)
        total = [jnp.where(ends, got, part).astype(f32) for part, got in zip(parts, self.gots)]
        total = total[0] if len(total) == 1 else jnp.concatenate(total, axis=0)
        if total.shape[0] > self.rows:
            return total[: self.rows], total[self.rows :]
        return total


def all_samples(row):
    rows = row[None]
    for bit in (1, 2):
        rows = jnp.concatenate([rows, lax.ppermute(rows, "seq", [(i, i ^ bit) for i in range(4)])], axis=0)
    return rows


def all_pairs(rows):
    bits = 2
    while bits < lax.axis_size("batch"):
        rows = jnp.concatenate([rows, hop(rows, bits)], axis=0)
        bits *= 2
    return rows


def xor_order(array, index):
    size, bit = array.shape[0], 1
    while bit < size:
        split = array.reshape((size // (2 * bit), 2, bit) + array.shape[1:])
        array = jnp.where((index & bit) != 0, split[:, ::-1], split).reshape(array.shape)
        bit *= 2
    return array


def body(
    inputs,
    conds,
    heights,
    widths,
    qkv_weight,
    qv_bias,
    out_weight,
    out_bias,
    up_weight,
    up_bias,
    down_weight,
    down_bias,
    mod_weight,
    mod_bias,
    cotangent,
):
    devices = lax.axis_size("batch")
    b, s = lax.axis_index("batch"), lax.axis_index("seq")
    c = b & 1
    width = inputs.shape[2]
    hidden = up_weight.shape[1]
    slot_dev = inputs.shape[1]
    half = slot_dev // 2
    rows = qkv_weight.shape[0]
    mods = mod_weight.shape[1]

    tokens16 = deal(inputs)
    upstream16 = deal(cotangent)

    core = jnp.reshape(c, (1,)).astype(jnp.int32)
    qkv_matrix = gather(qkv_weight)
    out_hops = Hops(out_weight)

    small = [conds.reshape(-1), qv_bias, out_bias, up_bias, down_bias, heights.astype(bf16), widths.astype(bf16)]
    spots = [sum(e.size for e in small[:i]) for i in range(len(small) + 1)]
    small.append(jnp.zeros((-spots[-1] % 128,), bf16))
    small = gather(jnp.concatenate(small)[None])
    every = [small[:, spots[i] : spots[i + 1]] for i in range(7)]
    cond_all = every[0].reshape(2 * devices, width)
    qv_offset, out_offset, up_offset, down_offset = (e.reshape(-1).astype(f32) for e in every[1:5])
    counts = (every[5].astype(jnp.int32) * every[6].astype(jnp.int32)).reshape(2 * devices)
    sample = 4 * (b // 2) + s
    count = lax.dynamic_index_in_dim(counts, sample, keepdims=False)

    silu_all = jax.nn.silu(cond_all.astype(f32)).astype(bf16)
    silu_rows = lax.dynamic_slice(silu_all, (0, b * rows), (2 * devices, rows))
    plane = lax.dynamic_index_in_dim(silu_rows.reshape(devices // 2, 4, rows), s, axis=1, keepdims=False)
    partial = dot(plane, mod_weight)
    own_bias = lax.dynamic_update_slice(jnp.zeros((mods,), f32), mod_bias.astype(f32), (b * mod_bias.shape[0],))
    partial = partial + own_bias[None]
    partial = jnp.broadcast_to(partial[:, None], (devices // 2, 2, mods)).reshape(devices, mods)
    modulation = jnp.sum(lax.all_to_all(partial, "batch", 0, 0, tiled=True), axis=0, keepdims=True)
    gate2 = modulation[:, 5 * width :]
    out_hops.turn(modulation)
    tokens16 = after(tokens16, out_hops.moving)
    out_pieces = out_hops.pieces()
    up_matrix = gather(after(up_weight, modulation))

    limits = [count - (slot_dev * i + half * (c ^ part)) for part in range(2) for i in range(4)]
    limits = jnp.stack(limits).astype(jnp.int32)

    offsets = jnp.concatenate([qv_offset[:width], jnp.zeros((width,), f32), qv_offset[width:]])
    mine, away, moved = project(core, qkv_matrix, tokens16, modulation, offsets[None])
    theirs = pair_swap(away)
    down_hops = Hops(after(down_weight, mine))
    att_mine, att_away, lse = attend(limits, after(mine, out_pieces[1]), theirs)
    down_hops.turn(att_mine)
    down_pieces = down_hops.pieces()
    attended, projected, normed2, factor2, moved2, out_matrix = middle_part(
        core, out_pieces, att_mine, pair_swap(att_away), tokens16, modulation, out_offset[None]
    )
    act, slope = up_part(moved2, up_matrix, up_offset[None])

    d_lowered = (gate2 * upstream16.astype(f32)).astype(bf16)
    down_offset_grad = jnp.sum(d_lowered.astype(f32), axis=0)
    down_g = Grad(act, d_lowered, True)
    mark = down_g.away(act)
    d_upper, up_sums, down_matrix = slope_part(after(d_lowered, mark), down_pieces, slope)
    mark = down_g.stay(d_upper)
    output, d_gate2 = down_part(
        after(act, mark), down_matrix, down_offset[None], tokens16, projected, modulation, upstream16
    )
    up_g = Grad(moved2, d_upper)
    mark = up_g.away(output)
    mark = down_g.mix(mark)
    d_middle, d_projected, d_att_mine, d_att_away, sums2 = middle_back(
        core, after(d_upper, mark), up_matrix, normed2, factor2, projected, upstream16, modulation, out_matrix
    )
    d_shift2, d_scale2, d_gate1, out_offset_grad = sums2
    d_att_theirs = pair_swap(d_att_away)
    output = undeal(output)
    mark, down_total = down_g.finish(d_att_mine)
    mark = up_g.stay(mark, output)
    out_g = Grad(attended, d_projected)
    mark = out_g.away(mark)
    heads = HEADS // 2
    steps = 2
    own, got = [], []
    for i in range(steps):
        made = attend_back(
            limits, after(mine, mark), theirs, d_att_mine, d_att_theirs, lse, i * heads // steps, heads // steps
        )
        own.append(made[0])
        got.append(pair_swap(made[1]))
        mark = made
        if i == 0:
            mark = up_g.mix(mark)
            mark = out_g.stay(mark)
    mark, up_total = up_g.finish(mark, down_total)
    d_qkv = join_heads(core, own, got)
    qkv_g = Grad(moved, d_qkv)
    mark = qkv_g.away(mark)
    mark = out_g.mix(mark)
    input_grad, sums1, column_sums = input_back(after(d_qkv, mark), qkv_matrix, tokens16, modulation, d_middle)
    d_shift1, d_scale1 = sums1
    mark = qkv_g.stay(input_grad)
    input_grad = undeal(after(input_grad, mark)).astype(f32)
    column_sums = after(column_sums[0], mark)
    qv_offset_grad = jnp.concatenate([column_sums[:width], column_sums[2 * width :]])
    own_shapes = (qv_bias.shape[0], out_bias.shape[0], up_bias.shape[0], down_bias.shape[0])
    bias = jnp.concatenate(
        [
            g.reshape(devices, -1)
            for g in (qv_offset_grad, out_offset_grad, up_sums, down_offset_grad)
        ],
        axis=1,
    )
    length = bias.shape[1]
    bias = jnp.sum(lax.all_to_all(bias, "batch", 0, 0, tiled=True), axis=0, keepdims=True)
    bias = jnp.pad(bias, ((0, 7), (0, 3 * width - length)))
    partial_mod = jnp.concatenate([d_shift1, d_scale1, d_gate1, d_shift2, d_scale2, d_gate2[0]])
    partial_mod = after(partial_mod, mark)
    d_mod = (partial_mod + pair_swap(partial_mod)).astype(bf16)
    d_mod_four = all_samples(d_mod)
    mark = qkv_g.mix(bias, d_mod_four)
    d_mod_all = all_pairs(after(d_mod_four, mark))
    mark, _ = out_g.finish(mark, up_total)
    mark, _ = qkv_g.finish(mark, up_total, extra=bias)
    mod_grad = dot(xor_order(silu_rows, sample), d_mod_all, TN)
    mod_offset_grad = jnp.sum(
        lax.dynamic_slice(d_mod_all, (0, b * mod_bias.shape[0]), (2 * devices, mod_bias.shape[0])).astype(f32), axis=0
    )
    d_silu_rows = xor_order(dot(d_mod_all, mod_weight, NT), sample)
    d_silu = lax.all_to_all(d_silu_rows.reshape(devices, 2 * rows), "batch", 0, 0, tiled=True)
    d_silu = d_silu.reshape(devices, 2, rows).transpose(1, 0, 2).reshape(2, width)
    cond_grad = jax.vjp(jax.nn.silu, conds.astype(f32))[1](d_silu)[0]

    down_grad, up_grad, out_grad = (grad.result(d_mod_all) for grad in (down_g, up_g, out_g))
    qkv_grad, bias = qkv_g.result()
    bias = bias[0, :length]
    cuts = [sum(own_shapes[:i]) for i in range(5)]
    qv_b, out_b, up_b, down_b = (bias[cuts[i] : cuts[i + 1]] for i in range(4))
    return (
        output,
        input_grad,
        cond_grad,
        qkv_grad,
        qv_b,
        out_grad,
        out_b,
        up_grad,
        up_b,
        down_grad,
        down_b,
        mod_grad,
        mod_offset_grad,
    )


def solution(mesh):
    in_specs = (
        P("batch", "seq", None),
        P("batch", None),
        P("batch"),
        P("batch"),
        P("batch", None),
        P("batch"),
        P("batch", None),
        P("batch"),
        P("batch", None),
        P("batch"),
        P("batch", None),
        P("batch"),
        P("batch", None),
        P("batch"),
        P("batch", "seq", None),
    )
    out_specs = (
        P("batch", "seq", None),
        P("batch", "seq", None),
        P("batch", None),
        P("batch", None),
        P("batch"),
        P("batch", None),
        P("batch"),
        P("batch", None),
        P("batch"),
        P("batch", None),
        P("batch"),
        P("batch", None),
        P("batch"),
    )
    return jax.shard_map(body, mesh=mesh, in_specs=in_specs, out_specs=out_specs, check_vma=False)
```

```python
import functools

import jax
import jax.numpy as jnp
from jax import lax
from jax.experimental import pallas as pl
from jax.experimental.pallas import tpu as pltpu
from jax.sharding import PartitionSpec as P

HEADS = 16
HEAD = 72
SCALE = HEAD ** (-0.5)
LOG2E = 1.4426950408889634
f32 = jnp.float32
bf16 = jnp.bfloat16
NT = (((1,), (1,)), ((), ()))
TN = (((0,), (0,)), ((), ()))


def dot(a, b, dims=(((1,), (0,)), ((), ()))):
    return lax.dot_general(a, b, dims, preferred_element_type=f32)


WHOLE = pl.BlockSpec()
SMEM = pl.BlockSpec(memory_space=pltpu.SMEM)
HBM = pl.BlockSpec(memory_space=pltpu.HBM)
BLOCK = 512
PAD = 128
ROOT = 0.7978845608028654
EARLY = 0.6
VMEM_ATT = 48


def lasts(microseconds):
    return pl.CostEstimate(
        flops=int(EARLY * microseconds * 1e9), bytes_accessed=int(EARLY * microseconds * 3.3e6), transcendentals=0
    )


def shaped(shape, kind):
    return pltpu.HBM(shape, kind)


def in_hbm(*arrays):
    return tuple(pltpu.with_memory_space_constraint(array, pltpu.HBM) for array in arrays)


def lanes(wide):
    return -(-wide // 128) * 128


def params(mib):
    return pltpu.CompilerParams(vmem_limit_bytes=mib * 2**20)


def on_core(core, work):
    for c in range(2):
        pl.when(core[0] == c)(functools.partial(work, c))


def split_kernel(core, source, mine, away):
    wide = source.shape[1] // 2

    def work(c):
        for ref, d in ((mine, c), (away, 1 - c)):
            ref[:, :wide] = source[:, d * wide : (d + 1) * wide]

    on_core(core, work)


def split_heads(core, array):
    rows, wide = array.shape[0], array.shape[1] // 2
    return pl.pallas_call(
        split_kernel,
        out_shape=(shaped((rows, wide), bf16), shaped((rows, lanes(wide)), bf16)),
        in_specs=[SMEM, WHOLE],
        out_specs=(WHOLE,) * 2,
        compiler_params=params(48),
        cost_estimate=lasts(2),
    )(core, *in_hbm(array))


def join_kernel(steps, core, *refs):
    own, got, whole = refs[:steps], refs[steps : 2 * steps], refs[2 * steps]
    narrow = own[0].shape[1] // 3
    wide = 2 * narrow * steps

    def work(c):
        for kind in range(3):
            for d, arrays in ((c, own), (1 - c, got)):
                for i, ref in enumerate(arrays):
                    at = kind * wide + (d * steps + i) * narrow
                    whole[:, at : at + narrow] = ref[:, kind * narrow : (kind + 1) * narrow]

    on_core(core, work)


def join_heads(core, own, got):
    steps, (rows, wide) = len(own), own[0].shape
    return pl.pallas_call(
        functools.partial(join_kernel, steps),
        out_shape=shaped((rows, 2 * steps * wide), own[0].dtype),
        in_specs=[SMEM] + [WHOLE] * (2 * steps),
        out_specs=WHOLE,
        compiler_params=params(48),
        cost_estimate=lasts(2),
    )(core, *in_hbm(*own, *got))


def assemble(spots, pieces, matrix, sems):
    copies = []
    for i, piece in enumerate(pieces):
        rows = pl.ds(pl.multiple_of(spots[i], 16), piece.shape[0])
        copies.append(pltpu.make_async_copy(piece, matrix.at[rows], sems.at[i]))
    for copy in copies:
        copy.start()
    for copy in copies:
        copy.wait()


def norm_rows(value):
    centre = value - jnp.mean(value, axis=1, keepdims=True)
    scale = lax.rsqrt(jnp.mean(centre * centre, axis=1, keepdims=True) + 1e-06)
    return centre * scale, scale


def back_rows(grad, normed, scale):
    return scale * (
        grad - jnp.mean(grad, axis=1, keepdims=True) - normed * jnp.mean(grad * normed, axis=1, keepdims=True)
    )


def row_chunks(rows, step=128):
    return [slice(i, i + step) for i in range(0, rows, step)]


def project_kernel(core, tokens, mods, offset, matrix, mine, away, moved, made):
    width = tokens.shape[1]
    half = width // 2

    @pl.when(pl.program_id(0) == 0)
    def _():
        for at in row_chunks(tokens.shape[0]):
            normed, _ = norm_rows(tokens[at, :].astype(f32))
            moved[at, :] = (normed * (1.0 + mods[:, width : 2 * width]) + mods[:, :width]).astype(bf16)

    made[...] = (dot(moved[...], matrix[...]) + offset[...]).astype(bf16)
    for kind in range(3):

        @pl.when(pl.program_id(0) == kind)
        def _():
            def work(c):
                for ref, d in ((mine, c), (away, 1 - c)):
                    ref[:, kind * half : (kind + 1) * half] = made[:, d * half : (d + 1) * half]

            on_core(core, work)


def project(core, matrix, tokens, mods, offset):
    rows, width = tokens.shape
    wide = matrix.shape[1]
    return pl.pallas_call(
        project_kernel,
        out_shape=(
            shaped((rows, wide // 2), bf16),
            shaped((rows, lanes(wide // 2)), bf16),
            shaped((rows, width), bf16),
        ),
        grid=(3,),
        in_specs=[
            SMEM,
            WHOLE,
            WHOLE,
            pl.BlockSpec((1, width), lambda i: (0, i)),
            pl.BlockSpec((width, width), lambda i: (0, i)),
        ],
        out_specs=(WHOLE,) * 3,
        scratch_shapes=[pltpu.VMEM((rows, width), bf16)],
        compiler_params=params(48),
        cost_estimate=lasts(13),
    )(core, *in_hbm(tokens, mods, offset, matrix))


def middle_kernel(number, core, spots, own, got, tokens, mods, offset, *refs):
    pieces = refs[:number]
    attended, projected, normed, factor, moved, whole, matrix, sems, out_sem = refs[number:]
    assemble(spots, pieces, matrix, sems)
    out = pltpu.make_async_copy(matrix, whole, out_sem)
    out.start()
    width = matrix.shape[1]
    half = width // 2

    def work(c):
        attended[:, c * half : (c + 1) * half] = own[...]
        attended[:, (1 - c) * half : (2 - c) * half] = got[:, :half]

    on_core(core, work)
    gate1, shift2, scale2 = (mods[:, i * width : (i + 1) * width] for i in (2, 3, 4))
    projected[...] = dot(attended[...], matrix[...]) + offset[...]
    for at in row_chunks(own.shape[0]):
        made = projected[at, :]
        value = tokens[at, :].astype(f32) + gate1 * made
        value, scale = norm_rows(value)
        normed[at, :] = value
        factor[at, :] = scale
        moved[at, :] = (value * (1.0 + scale2) + shift2).astype(bf16)
    out.wait()


def middle_part(core, gathered, own, got, tokens, mods, offset):
    spots, pieces = gathered
    rows, width = tokens.shape
    return pl.pallas_call(
        functools.partial(middle_kernel, len(pieces)),
        out_shape=(
            shaped((rows, width), bf16),
            shaped((rows, width), f32),
            shaped((rows, width), f32),
            shaped((rows, 1), f32),
            shaped((rows, width), bf16),
            shaped((width, width), bf16),
        ),
        in_specs=[SMEM, SMEM] + [WHOLE] * 5 + [HBM] * len(pieces),
        out_specs=(WHOLE,) * 5 + (HBM,),
        scratch_shapes=[
            pltpu.VMEM((width, width), bf16),
            pltpu.SemaphoreType.DMA((len(pieces),)),
            pltpu.SemaphoreType.DMA,
        ],
        compiler_params=params(48),
        cost_estimate=lasts(9),
    )(core, spots, *in_hbm(own, got, tokens, mods, offset, *pieces))


def up_kernel(moved, matrix, offset, act, slope):
    for at in row_chunks(moved.shape[0], 256):
        u = dot(moved[at, :], matrix[...]) + offset[...]
        square = u * u
        t = jnp.tanh(ROOT * (u + 0.044715 * (square * u)))
        act[at, :] = (0.5 * u * (1.0 + t)).astype(bf16)
        slope[at, :] = 0.5 * (1.0 + t) + (0.5 * ROOT) * u * (1.0 - t * t) * (1.0 + (3 * 0.044715) * square)


def up_part(moved, matrix, offset):
    (rows, width), hidden = moved.shape, matrix.shape[1]
    step = hidden // 4
    return pl.pallas_call(
        up_kernel,
        out_shape=(shaped((rows, hidden), bf16), shaped((rows, hidden), f32)),
        grid=(4,),
        in_specs=[WHOLE, pl.BlockSpec((width, step), lambda i: (0, i)), pl.BlockSpec((1, step), lambda i: (0, i))],
        out_specs=(pl.BlockSpec((rows, step), lambda i: (0, i)), pl.BlockSpec((rows, step), lambda i: (0, i))),
        compiler_params=params(48),
        cost_estimate=lasts(16),
    )(*in_hbm(moved, matrix, offset))


def slope_kernel(number, spots, grad, slope, *refs):
    pieces = refs[:number]
    d_upper, sums, whole, matrix, sems, out_sem = refs[number:]
    step = pl.program_id(0)
    size = sums.shape[1]
    out = pltpu.make_async_copy(matrix, whole, out_sem)

    @pl.when(step == 0)
    def _():
        assemble(spots, pieces, matrix, sems)
        out.start()

    part = matrix.at[pl.ds(pl.multiple_of(step * size, size), size)]
    total = jnp.zeros(sums.shape, f32)
    for at in row_chunks(grad.shape[0], 256):
        value = (dot(grad[at, :], part[...], NT) * slope[at, :]).astype(bf16)
        d_upper[at, :] = value
        total = total + jnp.sum(value.astype(f32), axis=0, keepdims=True)
    sums[...] = total

    @pl.when(step == pl.num_programs(0) - 1)
    def _():
        out.wait()


def slope_part(grad, gathered, slope):
    spots, pieces = gathered
    (rows, width), hidden = grad.shape, slope.shape[1]
    step = hidden // 4
    across = pl.BlockSpec((rows, step), lambda i: (0, i))
    return pl.pallas_call(
        functools.partial(slope_kernel, len(pieces)),
        out_shape=(shaped((rows, hidden), bf16), shaped((1, hidden), f32), shaped((hidden, width), bf16)),
        grid=(4,),
        in_specs=[SMEM, WHOLE, across] + [HBM] * len(pieces),
        out_specs=(across, pl.BlockSpec((1, step), lambda i: (0, i)), HBM),
        scratch_shapes=[
            pltpu.VMEM((hidden, width), bf16),
            pltpu.SemaphoreType.DMA((len(pieces),)),
            pltpu.SemaphoreType.DMA,
        ],
        compiler_params=params(48),
        cost_estimate=lasts(40),
    )(spots, *in_hbm(grad, slope, *pieces))


def down_kernel(act, matrix, offset, tokens, projected, mods, grad, output, d_gate, total):
    step = pl.program_id(0)
    width = matrix.shape[1]

    @pl.when(step == 0)
    def _():
        total[...] = dot(act[...], matrix[...])

    @pl.when(step > 0)
    def _():
        total[...] += dot(act[...], matrix[...])

    @pl.when(step == pl.num_programs(0) - 1)
    def _():
        gate1, gate2 = mods[:, 2 * width : 3 * width], mods[:, 5 * width :]
        summed = jnp.zeros(d_gate.shape, f32)
        for at in row_chunks(act.shape[0]):
            lowered = total[at, :] + offset[...]
            middle = tokens[at, :].astype(f32) + gate1 * projected[at, :]
            output[at, :] = (middle + gate2 * lowered).astype(bf16)
            summed = summed + jnp.sum(grad[at, :].astype(f32) * lowered, axis=0, keepdims=True)
        d_gate[...] = summed


def down_part(act, matrix, offset, tokens, projected, mods, grad):
    rows, hidden = act.shape
    step, width = hidden // 4, matrix.shape[1]
    return pl.pallas_call(
        down_kernel,
        out_shape=(shaped((rows, width), bf16), shaped((1, width), f32)),
        grid=(4,),
        in_specs=[pl.BlockSpec((rows, step), lambda i: (0, i)), pl.BlockSpec((step, width), lambda i: (i, 0))]
        + [WHOLE] * 5,
        out_specs=(WHOLE, WHOLE),
        scratch_shapes=[pltpu.VMEM((rows, width), f32)],
        compiler_params=params(48),
        cost_estimate=lasts(6),
    )(*in_hbm(act, matrix, offset, tokens, projected, mods, grad))


def middle_back_kernel(core, d_upper, matrix, normed, factor, projected, grad, mods, out_matrix, d_middle, d_projected, mine, away, sums, total):
    step = pl.program_id(0)
    width = matrix.shape[0]
    half = width // 2

    @pl.when(step == 0)
    def _():
        total[...] = dot(d_upper[...], matrix[...], NT)

    @pl.when(step > 0)
    def _():
        total[...] += dot(d_upper[...], matrix[...], NT)

    @pl.when(step == pl.num_programs(0) - 1)
    def _():
        gate1, scale2 = mods[:, 2 * width : 3 * width], mods[:, 4 * width : 5 * width]
        summed = [jnp.zeros((1, width), f32) for _ in range(4)]
        for at in row_chunks(grad.shape[0]):
            d_moved, n = total[at, :], normed[at, :]
            value = grad[at, :].astype(f32) + back_rows(d_moved * (1.0 + scale2), n, factor[at, :])
            d_middle[at, :] = value
            d_proj = (gate1 * value).astype(bf16)
            d_projected[at, :] = d_proj
            terms = d_moved, d_moved * n, value * projected[at, :], d_proj.astype(f32)
            summed = [u + jnp.sum(v, axis=0, keepdims=True) for u, v in zip(summed, terms)]
        total[...] = dot(d_projected[...], out_matrix[...], NT)

        def work(c):
            mine[...] = total[:, c * half : (c + 1) * half].astype(bf16)
            away[:, :half] = total[:, (1 - c) * half : (2 - c) * half].astype(bf16)

        on_core(core, work)
        for i, value in enumerate(summed):
            sums[i : i + 1, :] = value


def middle_back(core, d_upper, matrix, normed, factor, projected, grad, mods, out_matrix):
    rows, hidden = d_upper.shape
    step, width = hidden // 4, matrix.shape[0]
    return pl.pallas_call(
        middle_back_kernel,
        out_shape=(
            shaped((rows, width), f32),
            shaped((rows, width), bf16),
            shaped((rows, width // 2), bf16),
            shaped((rows, lanes(width // 2)), bf16),
            shaped((4, width), f32),
        ),
        grid=(4,),
        in_specs=[SMEM, pl.BlockSpec((rows, step), lambda i: (0, i)), pl.BlockSpec((width, step), lambda i: (0, i))]
        + [WHOLE] * 6,
        out_specs=(WHOLE,) * 5,
        scratch_shapes=[pltpu.VMEM((rows, width), f32)],
        compiler_params=params(48),
        cost_estimate=lasts(150),
    )(core, *in_hbm(d_upper, matrix, normed, factor, projected, grad, mods, out_matrix))


def input_back_kernel(d_qkv, matrix, tokens, mods, d_middle, input_grad, sums, columns, total):
    step = pl.program_id(0)
    width = matrix.shape[0]
    columns[...] = jnp.sum(d_qkv[...].astype(f32), axis=0, keepdims=True)

    @pl.when(step == 0)
    def _():
        total[...] = dot(d_qkv[...], matrix[...], NT)

    @pl.when(step > 0)
    def _():
        total[...] += dot(d_qkv[...], matrix[...], NT)

    @pl.when(step == pl.num_programs(0) - 1)
    def _():
        scale1 = mods[:, width : 2 * width]
        summed = [jnp.zeros((1, width), f32) for _ in range(2)]
        for at in row_chunks(tokens.shape[0]):
            normed, factor = norm_rows(tokens[at, :].astype(f32))
            d_moved = total[at, :]
            input_grad[at, :] = (d_middle[at, :] + back_rows(d_moved * (1.0 + scale1), normed, factor)).astype(bf16)
            summed = [u + jnp.sum(v, axis=0, keepdims=True) for u, v in zip(summed, (d_moved, d_moved * normed))]
        for i, value in enumerate(summed):
            sums[i : i + 1, :] = value


def input_back(d_qkv, matrix, tokens, mods, d_middle):
    rows, wide = d_qkv.shape
    width = matrix.shape[0]
    return pl.pallas_call(
        input_back_kernel,
        out_shape=(shaped((rows, width), bf16), shaped((2, width), f32), shaped((1, wide), f32)),
        grid=(wide // width,),
        in_specs=[pl.BlockSpec((rows, width), lambda i: (0, i)), pl.BlockSpec((width, width), lambda i: (0, i))]
        + [WHOLE] * 3,
        out_specs=(WHOLE, WHOLE, pl.BlockSpec((1, width), lambda i: (0, i))),
        scratch_shapes=[pltpu.VMEM((rows, width), f32)],
        compiler_params=params(48),
        cost_estimate=lasts(120),
    )(*in_hbm(d_qkv, matrix, tokens, mods, d_middle))


def cut_of(rows):
    return rows // 2 // 8 * 8


def keep(made, e, value):
    if len(made) == 1:
        made[0][e] = value
    elif e == 3 and len(made) == 5:
        cut = made[3].shape[0]
        made[3][...], made[4][...] = value[:cut], value[cut:]
    else:
        made[e][...] = value


def pair_grad_kernel(added, where, left, right, *refs):
    gots, made = refs[:added], refs[added:]
    half = left.shape[1] // 2
    step = pl.program_id(0)
    for d in range(2):

        @pl.when(where[1] == d)
        def _():
            value = dot(left[:, d * half : (d + 1) * half], right[...], TN)
            for e in range(4):

                @pl.when(step == e)
                def _():
                    more = gots[0][e].astype(f32) if added else 0.0
                    keep(made, e, (value + more).astype(bf16))


def grad_shapes(rows, columns, added):
    cut = cut_of(rows)
    return [(rows, columns)] * 3 + [(cut, columns), (rows - cut, columns)] if added else [(4, rows, columns)]


def pair_grad(left, right, b, side, gots=()):
    slots, wide = left.shape
    step = wide // 4
    where = jnp.stack([b >> 1, side]).astype(jnp.int32)
    shapes = grad_shapes(step // 2, right.shape[1], len(gots))
    whole = lambda shape: pl.BlockSpec(shape, lambda m, where: (0,) * len(shape))
    specs = [pl.BlockSpec((slots, step), lambda m, where: (0, where[0] ^ m)), whole(right.shape)]
    return pl.pallas_call(
        functools.partial(pair_grad_kernel, len(gots)),
        out_shape=tuple(shaped(shape, bf16) for shape in shapes),
        grid_spec=pltpu.PrefetchScalarGridSpec(
            num_scalar_prefetch=1,
            grid=(4,),
            in_specs=specs + [whole(got.shape) for got in gots],
            out_specs=tuple(whole(shape) for shape in shapes),
        ),
        compiler_params=params(48),
        cost_estimate=lasts(9),
    )(where, *in_hbm(left, right, *gots))


def block_grad_kernel(added, spots, left, right, *refs):
    gots, made, (chosen, turned) = refs[:added], refs[added:-2], refs[-2:]
    rows = made[0].shape[-2]

    @pl.when(pl.program_id(0) == 0)
    def _():
        turned[...] = jnp.transpose(left[...])
        for e in range(4):
            at = pl.ds(pl.multiple_of(spots[e], 16), rows)
            chosen[e * rows : (e + 1) * rows, :] = turned[at, :]

    value = dot(chosen[...], right[...])
    for e in range(4):
        part = value[e * rows : (e + 1) * rows, :]
        if added:
            part = part + gots[0][e].astype(f32)
        keep(made, e, part.astype(bf16))


def block_grad(left, right, b, side, gots=()):
    (slots, wide), columns = left.shape, right.shape[1]
    rows = wide // 8
    spots = jnp.stack([((b >> 1) ^ m) * 2 * rows + side * rows for m in range(4)]).astype(jnp.int32)
    step = 1152 if columns % 1152 == 0 else columns
    shapes = grad_shapes(rows, columns, len(gots))
    block = lambda shape: pl.BlockSpec(shape[:-1] + (step,), lambda i: (0,) * (len(shape) - 1) + (i,))
    return pl.pallas_call(
        functools.partial(block_grad_kernel, len(gots)),
        out_shape=tuple(shaped(shape, bf16) for shape in shapes),
        grid=(columns // step,),
        in_specs=[SMEM, WHOLE, pl.BlockSpec((slots, step), lambda i: (0, i))] + [block(got.shape) for got in gots],
        out_specs=tuple(block(shape) for shape in shapes),
        scratch_shapes=[pltpu.VMEM((4 * rows, slots), bf16), pltpu.VMEM((wide, slots), bf16)],
        compiler_params=params(48),
        cost_estimate=lasts(columns // 1152),
    )(spots, *in_hbm(left, right, *gots))


def mix_kernel(to_x, to_y, got_x, got_y, out_x, out_y):
    cut = got_x.shape[0]
    out_x[:cut, :] = to_x[:cut, :]
    out_x[cut:, :] = add(to_x[cut:, :], got_y[...])
    out_y[:cut, :] = add(to_y[:cut, :], got_x[...])
    out_y[cut:, :] = to_y[cut:, :]


def mix(to_x, to_y, got_x, got_y):
    rows, columns = to_x.shape
    step = 1152
    block = lambda array: pl.BlockSpec((array.shape[0], step), lambda i: (0, i))
    return pl.pallas_call(
        mix_kernel,
        out_shape=(shaped(to_x.shape, bf16),) * 2,
        grid=(columns // step,),
        in_specs=[block(array) for array in (to_x, to_y, got_x, got_y)],
        out_specs=(block(to_x),) * 2,
        compiler_params=params(48),
        cost_estimate=lasts(1),
    )(*in_hbm(to_x, to_y, got_x, got_y))


def fill(h, heads, mine, theirs, qs, ks, vs):
    half, wide, lo = mine.shape[0], heads * HEAD, h * HEAD
    for part, ref in ((0, mine), (1, theirs)):
        rows = slice(part * half, (part + 1) * half)
        qs[rows, :HEAD] = ref[:, lo : lo + HEAD]
        ks[rows, :HEAD] = ref[:, wide + lo : wide + lo + HEAD]
        vs[rows, :] = ref[:, 2 * wide + lo : 2 * wide + lo + HEAD]


def mark_valid(limits, qs, ks):
    total = qs.shape[0]
    chunks = limits.shape[0]
    sub = lax.broadcasted_iota(jnp.int32, (total // chunks, 1), 0)
    bias = jnp.concatenate([jnp.where(sub < limits[i], 0.0, -1e30) for i in range(chunks)], axis=0)
    qs[...] = jnp.zeros_like(qs)
    ks[...] = jnp.zeros_like(ks)
    qs[:, HEAD : HEAD + 1] = jnp.ones((total, 1), bf16)
    ks[:, HEAD : HEAD + 1] = bias.astype(bf16)


def attend_kernel(heads, limits, mine, theirs, out_mine, out_theirs, lse, qs, ks, vs, os, ls):
    half = mine.shape[0]
    total = 2 * half
    mark_valid(limits, qs, ks)
    for h in range(heads):
        fill(h, heads, mine, theirs, qs, ks, vs)
        for i in range(total // BLOCK):
            at = slice(i * BLOCK, (i + 1) * BLOCK)
            scores = dot(qs[at, :], ks[...], NT) * (SCALE * LOG2E)
            peak = jnp.max(scores, axis=1, keepdims=True)
            expo = jnp.exp2(scores - peak)
            summed = jnp.sum(expo, axis=1, keepdims=True)
            probs = (expo * (1.0 / summed)).astype(bf16)
            os[at, :] = dot(probs, vs[...]).astype(bf16)
            ls[at, :] = peak + jnp.log2(summed)
        lo = h * HEAD
        out_mine[:, lo : lo + HEAD] = os[:half, :]
        out_theirs[:, lo : lo + HEAD] = os[half:, :]
        lse[h : h + 1, :] = jnp.transpose(ls[...])


def attend(limits, mine, theirs):
    half, wide3 = mine.shape
    wide = wide3 // 3
    heads = wide // HEAD
    total = 2 * half
    return pl.pallas_call(
        functools.partial(attend_kernel, heads),
        out_shape=(shaped((half, wide), bf16), shaped((half, lanes(wide)), bf16), shaped((heads, total), f32)),
        in_specs=[SMEM, WHOLE, WHOLE],
        out_specs=(WHOLE,) * 3,
        scratch_shapes=[
            pltpu.VMEM((total, PAD), bf16),
            pltpu.VMEM((total, PAD), bf16),
            pltpu.VMEM((total, HEAD), bf16),
            pltpu.VMEM((total, HEAD), bf16),
            pltpu.VMEM((total, 1), f32),
        ],
        compiler_params=params(VMEM_ATT),
        cost_estimate=lasts(27),
    )(limits, *in_hbm(mine, theirs))


def back_kernel(heads, first, number, limits, mine, theirs, d_mine, d_theirs, lse, out_mine, out_theirs, qs, ks, vs, ds, dq, dk, dv):
    half = mine.shape[0]
    total = 2 * half
    narrow = number * HEAD
    mark_valid(limits, qs, ks)
    for h in range(first, first + number):
        fill(h, heads, mine, theirs, qs, ks, vs)
        lo = h * HEAD
        ds[:half, :] = d_mine[:, lo : lo + HEAD]
        ds[half:, :] = d_theirs[:, lo : lo + HEAD]
        for i in range(total // BLOCK):
            at = slice(i * BLOCK, (i + 1) * BLOCK)
            query, d_out = qs[at, :], ds[at, :]
            exact = jnp.exp2(dot(ks[...], query, NT) * (SCALE * LOG2E) - lse[h : h + 1, at])
            d_probs = dot(vs[...], d_out, NT)
            more = dot(exact.astype(bf16), d_out)
            dv[...] = more if i == 0 else dv[...] + more
            product = exact * d_probs
            centred = jnp.sum(product, axis=0, keepdims=True)
            d_scores = (product - exact * centred).astype(bf16)
            more = dot(d_scores, query)
            dk[...] = more if i == 0 else dk[...] + more
            dq[at, :] = (dot(d_scores, ks[...], TN) * SCALE).astype(bf16)
        lo = (h - first) * HEAD
        for part, ref in ((0, out_mine), (1, out_theirs)):
            rows = slice(part * half, (part + 1) * half)
            ref[:, lo : lo + HEAD] = dq[rows, :HEAD]
            ref[:, narrow + lo : narrow + lo + HEAD] = (dk[rows, :HEAD] * SCALE).astype(bf16)
            ref[:, 2 * narrow + lo : 2 * narrow + lo + HEAD] = dv[rows, :].astype(bf16)


def attend_back(limits, mine, theirs, d_mine, d_theirs, lse, first, number):
    half, wide3 = mine.shape
    wide = wide3 // 3
    heads = wide // HEAD
    total = 2 * half
    return pl.pallas_call(
        functools.partial(back_kernel, heads, first, number),
        out_shape=(shaped((half, 3 * number * HEAD), bf16), shaped((half, lanes(3 * number * HEAD)), bf16)),
        in_specs=[SMEM] + [WHOLE] * 5,
        out_specs=(WHOLE,) * 2,
        scratch_shapes=[
            pltpu.VMEM((total, PAD), bf16),
            pltpu.VMEM((total, PAD), bf16),
            pltpu.VMEM((total, HEAD), bf16),
            pltpu.VMEM((total, HEAD), bf16),
            pltpu.VMEM((total, PAD), bf16),
            pltpu.VMEM((total, PAD), f32),
            pltpu.VMEM((total, HEAD), f32),
        ],
        compiler_params=params(VMEM_ATT),
        cost_estimate=lasts(4),
    )(limits, *in_hbm(mine, theirs, d_mine, d_theirs, lse))


def pair_swap(array):
    size = lax.axis_size("batch")
    return lax.ppermute(array, "batch", [(i, i ^ 1) for i in range(size)])


def by_core(own, other):
    first = (lax.axis_index("batch") & 1) == 0
    return jnp.where(first, jnp.stack([own, other]), jnp.stack([other, own]))


def deal(array):
    c = lax.axis_index("batch") & 1
    samples, slots, width = array.shape
    halves = array.reshape(samples, 2, slots // 2, width)
    own = lax.dynamic_index_in_dim(halves, c, axis=1, keepdims=False)
    other = pair_swap(lax.dynamic_index_in_dim(halves, 1 - c, axis=1, keepdims=False))
    every = by_core(own, other).reshape(2 * samples, slots // 2, width)
    return lax.all_to_all(every, "seq", 0, 0, tiled=True).reshape(samples * slots, width)


def undeal(array):
    c = lax.axis_index("batch") & 1
    rows, width = array.shape
    every = lax.all_to_all(array.reshape(4, rows // 4, width), "seq", 0, 0, tiled=True)
    every = every.reshape(2, 2, rows // 4, width)
    own = lax.dynamic_index_in_dim(every, c, axis=0, keepdims=False)
    other = pair_swap(lax.dynamic_index_in_dim(every, 1 - c, axis=0, keepdims=False))
    return by_core(own, other).transpose(1, 0, 2, 3).reshape(2, rows // 2, width)


def gather(array):
    return lax.all_gather(array, "batch", axis=0, tiled=True)


def hop(array, bits):
    size = lax.axis_size("batch")
    return lax.ppermute(array, "batch", [(i, i ^ bits) for i in range(size)])


class Hops:
    def __init__(self, array):
        self.array = array
        self.plain = lax.axis_size("batch") != 8
        if self.plain:
            self.whole = gather(array)
            self.moving = (self.whole,)
        else:
            self.moving = self.along_x, self.along_y = hop(array, 2), hop(array, 4)

    def turn(self, *done):
        if self.plain:
            return self.moving
        self.cut = self.array.shape[0] // 2 // 16 * 16
        self.along_x, self.along_y = after((self.along_x, self.along_y), *done)
        self.corner = hop(self.along_x[: self.cut], 4), hop(self.along_y[self.cut :], 2)
        self.moving = self.along_x, self.along_y, *self.corner
        return self.moving

    def pieces(self, *done):
        if self.plain:
            return jnp.zeros((1,), jnp.int32), [self.whole]
        rows, cut = self.array.shape[0], self.cut
        b = lax.axis_index("batch")
        along_x, along_y, *corner = after(self.moving, *done)
        pieces = [(0, 0, self.array), (2, 0, along_x), (4, 0, along_y), (6, 0, corner[0]), (6, cut, corner[1])]
        pieces += [(bits ^ 1, at, hop(piece, 1)) for bits, at, piece in pieces]
        spots = jnp.stack([(b ^ bits) * rows + at for bits, at, _ in pieces]).astype(jnp.int32)
        return spots, [piece for _, _, piece in pieces]


def after(value, *done):
    return lax.optimization_barrier((value, done))[0]


def add(u, v):
    return (u.astype(f32) + v.astype(f32)).astype(bf16)


class Grad:
    def __init__(self, left, right, paired=False):
        self.left, self.right, self.paired = left, right, paired
        self.rows = left.shape[1] // lax.axis_size("batch")
        self.plain = lax.axis_size("batch") != 8 or lax.axis_size("seq") != 4

    def away(self, *done):
        if self.plain:
            made = self.made = dot(after(self.left, *done), self.right, TN).astype(bf16)
            return made
        self.left = after(self.left, *done)
        b = lax.axis_index("batch")
        made = (pair_grad if self.paired else block_grad)(self.left, self.right, b, 1 - (b & 1))
        self.gots = [hop(made[0], 1)]
        return made

    def stay(self, *done):
        if self.plain:
            part = lax.psum_scatter(self.made, "batch", scatter_dimension=0, tiled=True)
            self.part = lax.psum(part, "seq")
            return self.part
        self.left = after(self.left, *done)
        b = lax.axis_index("batch")
        made = (pair_grad if self.paired else block_grad)(self.left, self.right, b, b & 1, self.gots)
        self.own, self.to_x, self.to_y, corner_x, corner_y = made
        self.got_x, self.got_y = hop(corner_x, 2), hop(corner_y, 4)
        return made

    def mix(self, *done):
        if self.plain:
            return self.part
        to_x, to_y = after((self.to_x, self.to_y), *done)
        made = mix(to_x, to_y, self.got_x, self.got_y)
        self.got_x, self.got_y = hop(made[0], 2), hop(made[1], 4)
        return made

    def finish(self, *done, extra=None):
        if self.plain:
            return (self.land(extra=extra),) * 2
        own = after(self.own, *done)
        part = (own.astype(f32) + self.got_x.astype(f32) + self.got_y.astype(f32)).astype(bf16)
        if extra is not None:
            part = jnp.concatenate([part, extra.astype(bf16)], axis=0)
        total = lax.psum(part, "seq")
        self.part, self.plain = total[: self.rows], True
        if extra is not None:
            self.extra = total[self.rows :].astype(f32)
        return part, total

    def land(self, *done, extra=None, chunks=1):
        if self.plain:
            if extra is not None:
                self.extra = lax.psum(extra, "seq")
            return self.part
        own = after(self.own, *done)
        part = (own.astype(f32) + self.got_x.astype(f32) + self.got_y.astype(f32)).astype(bf16)
        if extra is not None:
            part = jnp.concatenate([part, extra.astype(bf16)], axis=0)
        step = -(-part.shape[0] // chunks // 8) * 8
        self.parts = [part[i * step : (i + 1) * step] for i in range(chunks)]
        self.gots = [lax.ppermute(part, "seq", [(0, 1), (3, 2)]) for part in self.parts]
        return part

    def pass_on(self, pairs, done):
        if self.plain:
            return self.part
        parts = after(tuple(self.parts), *done)
        self.parts, gots = [], self.gots
        self.gots = []
        for part, got in zip(parts, gots):
            part = add(part, got)
            self.parts.append(part)
            self.gots.append(lax.ppermute(part, "seq", pairs))
        return tuple(self.parts)

    def across(self, *done):
        return self.pass_on([(1, 2), (2, 1)], done)

    def outward(self, *done):
        return self.pass_on([(1, 0), (2, 3)], done)

    def result(self, *done):
        if self.plain:
            part = after(self.part, *done).astype(f32)
            return part if not hasattr(self, "extra") else (part, self.extra)
        s = lax.axis_index("seq")
        ends = (s == 0) | (s == 3)
        parts = after(tuple(self.parts), *done)
        total = [jnp.where(ends, got, part).astype(f32) for part, got in zip(parts, self.gots)]
        total = total[0] if len(total) == 1 else jnp.concatenate(total, axis=0)
        if total.shape[0] > self.rows:
            return total[: self.rows], total[self.rows :]
        return total


def all_samples(row):
    rows = row[None]
    for bit in (1, 2):
        rows = jnp.concatenate([rows, lax.ppermute(rows, "seq", [(i, i ^ bit) for i in range(4)])], axis=0)
    return rows


def all_pairs(rows):
    bits = 2
    while bits < lax.axis_size("batch"):
        rows = jnp.concatenate([rows, hop(rows, bits)], axis=0)
        bits *= 2
    return rows


def xor_order(array, index):
    size, bit = array.shape[0], 1
    while bit < size:
        split = array.reshape((size // (2 * bit), 2, bit) + array.shape[1:])
        array = jnp.where((index & bit) != 0, split[:, ::-1], split).reshape(array.shape)
        bit *= 2
    return array


def body(
    inputs,
    conds,
    heights,
    widths,
    qkv_weight,
    qv_bias,
    out_weight,
    out_bias,
    up_weight,
    up_bias,
    down_weight,
    down_bias,
    mod_weight,
    mod_bias,
    cotangent,
):
    devices = lax.axis_size("batch")
    b, s = lax.axis_index("batch"), lax.axis_index("seq")
    c = b & 1
    width = inputs.shape[2]
    hidden = up_weight.shape[1]
    slot_dev = inputs.shape[1]
    half = slot_dev // 2
    rows = qkv_weight.shape[0]
    mods = mod_weight.shape[1]

    tokens16 = deal(inputs)
    upstream16 = deal(cotangent)

    core = jnp.reshape(c, (1,)).astype(jnp.int32)
    qkv_matrix = gather(qkv_weight)
    out_hops = Hops(out_weight)

    small = [conds.reshape(-1), qv_bias, out_bias, up_bias, down_bias, heights.astype(bf16), widths.astype(bf16)]
    spots = [sum(e.size for e in small[:i]) for i in range(len(small) + 1)]
    small.append(jnp.zeros((-spots[-1] % 128,), bf16))
    small = gather(jnp.concatenate(small)[None])
    every = [small[:, spots[i] : spots[i + 1]] for i in range(7)]
    cond_all = every[0].reshape(2 * devices, width)
    qv_offset, out_offset, up_offset, down_offset = (e.reshape(-1).astype(f32) for e in every[1:5])
    counts = (every[5].astype(jnp.int32) * every[6].astype(jnp.int32)).reshape(2 * devices)
    sample = 4 * (b // 2) + s
    count = lax.dynamic_index_in_dim(counts, sample, keepdims=False)

    silu_all = jax.nn.silu(cond_all.astype(f32)).astype(bf16)
    silu_rows = lax.dynamic_slice(silu_all, (0, b * rows), (2 * devices, rows))
    plane = lax.dynamic_index_in_dim(silu_rows.reshape(devices // 2, 4, rows), s, axis=1, keepdims=False)
    partial = dot(plane, mod_weight)
    own_bias = lax.dynamic_update_slice(jnp.zeros((mods,), f32), mod_bias.astype(f32), (b * mod_bias.shape[0],))
    partial = partial + own_bias[None]
    partial = jnp.broadcast_to(partial[:, None], (devices // 2, 2, mods)).reshape(devices, mods)
    modulation = jnp.sum(lax.all_to_all(partial, "batch", 0, 0, tiled=True), axis=0, keepdims=True)
    gate2 = modulation[:, 5 * width :]
    out_hops.turn(modulation)
    tokens16 = after(tokens16, out_hops.moving)
    out_pieces = out_hops.pieces()
    up_matrix = gather(after(up_weight, modulation))

    limits = [count - (slot_dev * i + half * (c ^ part)) for part in range(2) for i in range(4)]
    limits = jnp.stack(limits).astype(jnp.int32)

    offsets = jnp.concatenate([qv_offset[:width], jnp.zeros((width,), f32), qv_offset[width:]])
    mine, away, moved = project(core, qkv_matrix, tokens16, modulation, offsets[None])
    theirs = pair_swap(away)
    down_hops = Hops(after(down_weight, mine))
    att_mine, att_away, lse = attend(limits, after(mine, out_pieces[1]), theirs)
    first = down_hops.moving
    down_hops.turn(att_mine)
    down_pieces = down_hops.pieces()
    attended, projected, normed2, factor2, moved2, out_matrix = middle_part(
        core, out_pieces, att_mine, pair_swap(att_away), tokens16, modulation, out_offset[None]
    )
    act, slope = up_part(moved2, up_matrix, up_offset[None])

    d_lowered = (gate2 * upstream16.astype(f32)).astype(bf16)
    down_offset_grad = jnp.sum(d_lowered.astype(f32), axis=0)
    down_g = Grad(act, d_lowered, True)
    mark = down_g.away(act, first)
    mark = down_g.stay(mark)
    d_upper, up_sums, down_matrix = slope_part(after(d_lowered, mark), down_pieces, slope)
    mark = down_g.mix(d_upper)
    output, d_gate2 = down_part(
        after(act, mark), down_matrix, down_offset[None], tokens16, projected, modulation, upstream16
    )
    up_g = Grad(moved2, d_upper)
    mark = up_g.away(output)
    d_middle, d_projected, d_att_mine, d_att_away, sums2 = middle_back(
        core, after(d_upper, mark), up_matrix, normed2, factor2, projected, upstream16, modulation, out_matrix
    )
    d_shift2, d_scale2, d_gate1, out_offset_grad = sums2
    d_att_theirs = pair_swap(d_att_away)
    output = undeal(output)
    mark, down_total = down_g.finish(d_att_mine)
    mark = up_g.stay(mark)
    out_g = Grad(attended, d_projected)
    mark = out_g.away(mark)
    heads = HEADS // 2
    steps = 2
    own, got = [], []
    for i in range(steps):
        made = attend_back(
            limits, after(mine, mark), theirs, d_att_mine, d_att_theirs, lse, i * heads // steps, heads // steps
        )
        own.append(made[0])
        got.append(pair_swap(made[1]))
        mark = made
        if i == 0:
            mark = up_g.mix(mark)
            mark = out_g.stay(mark)
    d_qkv = join_heads(core, own, got)
    mark, up_total = up_g.finish(d_qkv, down_total, output)
    qkv_g = Grad(moved, d_qkv)
    mark = qkv_g.away(mark)
    mark = out_g.mix(mark)
    input_grad, sums1, column_sums = input_back(after(d_qkv, mark), qkv_matrix, tokens16, modulation, d_middle)
    d_shift1, d_scale1 = sums1
    mark = qkv_g.stay(input_grad)
    input_grad = undeal(after(input_grad, mark)).astype(f32)
    column_sums = after(column_sums[0], mark)
    qv_offset_grad = jnp.concatenate([column_sums[:width], column_sums[2 * width :]])
    own_shapes = (qv_bias.shape[0], out_bias.shape[0], up_bias.shape[0], down_bias.shape[0])
    bias = jnp.concatenate(
        [
            g.reshape(devices, -1)
            for g in (qv_offset_grad, out_offset_grad, up_sums, down_offset_grad)
        ],
        axis=1,
    )
    length = bias.shape[1]
    bias = jnp.sum(lax.all_to_all(bias, "batch", 0, 0, tiled=True), axis=0, keepdims=True)
    bias = jnp.pad(bias, ((0, 7), (0, 3 * width - length)))
    partial_mod = jnp.concatenate([d_shift1, d_scale1, d_gate1, d_shift2, d_scale2, d_gate2[0]])
    partial_mod = after(partial_mod, mark)
    d_mod = (partial_mod + pair_swap(partial_mod)).astype(bf16)
    d_mod_four = all_samples(d_mod)
    mark = qkv_g.mix(bias, d_mod_four)
    d_mod_all = all_pairs(after(d_mod_four, mark))
    mark, _ = out_g.finish(mark, up_total)
    mark, _ = qkv_g.finish(mark, up_total, extra=bias)
    mod_grad = dot(xor_order(silu_rows, sample), d_mod_all, TN)
    mod_offset_grad = jnp.sum(
        lax.dynamic_slice(d_mod_all, (0, b * mod_bias.shape[0]), (2 * devices, mod_bias.shape[0])).astype(f32), axis=0
    )
    d_silu_rows = xor_order(dot(d_mod_all, mod_weight, NT), sample)
    d_silu = lax.all_to_all(d_silu_rows.reshape(devices, 2 * rows), "batch", 0, 0, tiled=True)
    d_silu = d_silu.reshape(devices, 2, rows).transpose(1, 0, 2).reshape(2, width)
    cond_grad = jax.vjp(jax.nn.silu, conds.astype(f32))[1](d_silu)[0]

    down_grad, up_grad, out_grad = (grad.result(d_mod_all) for grad in (down_g, up_g, out_g))
    qkv_grad, bias = qkv_g.result()
    bias = bias[0, :length]
    cuts = [sum(own_shapes[:i]) for i in range(5)]
    qv_b, out_b, up_b, down_b = (bias[cuts[i] : cuts[i + 1]] for i in range(4))
    return (
        output,
        input_grad,
        cond_grad,
        qkv_grad,
        qv_b,
        out_grad,
        out_b,
        up_grad,
        up_b,
        down_grad,
        down_b,
        mod_grad,
        mod_offset_grad,
    )


def solution(mesh):
    in_specs = (
        P("batch", "seq", None),
        P("batch", None),
        P("batch"),
        P("batch"),
        P("batch", None),
        P("batch"),
        P("batch", None),
        P("batch"),
        P("batch", None),
        P("batch"),
        P("batch", None),
        P("batch"),
        P("batch", None),
        P("batch"),
        P("batch", "seq", None),
    )
    out_specs = (
        P("batch", "seq", None),
        P("batch", "seq", None),
        P("batch", None),
        P("batch", None),
        P("batch"),
        P("batch", None),
        P("batch"),
        P("batch", None),
        P("batch"),
        P("batch", None),
        P("batch"),
        P("batch", None),
        P("batch"),
    )
    return jax.shard_map(body, mesh=mesh, in_specs=in_specs, out_specs=out_specs, check_vma=False)
```

```python
import functools

import jax
import jax.numpy as jnp
from jax import lax
from jax.experimental import pallas as pl
from jax.experimental.pallas import tpu as pltpu
from jax.sharding import PartitionSpec as P

HEADS = 16
HEAD = 72
SCALE = HEAD ** (-0.5)
LOG2E = 1.4426950408889634
f32 = jnp.float32
bf16 = jnp.bfloat16
NT = (((1,), (1,)), ((), ()))
TN = (((0,), (0,)), ((), ()))


def dot(a, b, dims=(((1,), (0,)), ((), ()))):
    return lax.dot_general(a, b, dims, preferred_element_type=f32)


WHOLE = pl.BlockSpec()
SMEM = pl.BlockSpec(memory_space=pltpu.SMEM)
HBM = pl.BlockSpec(memory_space=pltpu.HBM)
BLOCK = 512
PAD = 128
ROOT = 0.7978845608028654
EARLY = 0.6
VMEM_ATT = 48


def lasts(microseconds):
    return pl.CostEstimate(
        flops=int(EARLY * microseconds * 1e9), bytes_accessed=int(EARLY * microseconds * 3.3e6), transcendentals=0
    )


def shaped(shape, kind):
    return pltpu.HBM(shape, kind)


def in_hbm(*arrays):
    return tuple(pltpu.with_memory_space_constraint(array, pltpu.HBM) for array in arrays)


def lanes(wide):
    return -(-wide // 128) * 128


def params(mib):
    return pltpu.CompilerParams(vmem_limit_bytes=mib * 2**20)


def on_core(core, work):
    for c in range(2):
        pl.when(core[0] == c)(functools.partial(work, c))


def split_kernel(core, source, mine, away):
    wide = source.shape[1] // 2

    def work(c):
        for ref, d in ((mine, c), (away, 1 - c)):
            ref[:, :wide] = source[:, d * wide : (d + 1) * wide]

    on_core(core, work)


def split_heads(core, array):
    rows, wide = array.shape[0], array.shape[1] // 2
    return pl.pallas_call(
        split_kernel,
        out_shape=(shaped((rows, wide), bf16), shaped((rows, lanes(wide)), bf16)),
        in_specs=[SMEM, WHOLE],
        out_specs=(WHOLE,) * 2,
        compiler_params=params(48),
        cost_estimate=lasts(2),
    )(core, *in_hbm(array))


def join_kernel(steps, core, *refs):
    own, got, whole = refs[:steps], refs[steps : 2 * steps], refs[2 * steps]
    narrow = own[0].shape[1] // 3
    wide = 2 * narrow * steps

    def work(c):
        for kind in range(3):
            for d, arrays in ((c, own), (1 - c, got)):
                for i, ref in enumerate(arrays):
                    at = kind * wide + (d * steps + i) * narrow
                    whole[:, at : at + narrow] = ref[:, kind * narrow : (kind + 1) * narrow]

    on_core(core, work)


def join_heads(core, own, got):
    steps, (rows, wide) = len(own), own[0].shape
    return pl.pallas_call(
        functools.partial(join_kernel, steps),
        out_shape=shaped((rows, 2 * steps * wide), own[0].dtype),
        in_specs=[SMEM] + [WHOLE] * (2 * steps),
        out_specs=WHOLE,
        compiler_params=params(48),
        cost_estimate=lasts(2),
    )(core, *in_hbm(*own, *got))


def assemble(spots, pieces, matrix, sems):
    copies = []
    for i, piece in enumerate(pieces):
        rows = pl.ds(pl.multiple_of(spots[i], 16), piece.shape[0])
        copies.append(pltpu.make_async_copy(piece, matrix.at[rows], sems.at[i]))
    for copy in copies:
        copy.start()
    for copy in copies:
        copy.wait()


def norm_rows(value):
    centre = value - jnp.mean(value, axis=1, keepdims=True)
    scale = lax.rsqrt(jnp.mean(centre * centre, axis=1, keepdims=True) + 1e-06)
    return centre * scale, scale


def back_rows(grad, normed, scale):
    return scale * (
        grad - jnp.mean(grad, axis=1, keepdims=True) - normed * jnp.mean(grad * normed, axis=1, keepdims=True)
    )


def row_chunks(rows, step=128):
    return [slice(i, i + step) for i in range(0, rows, step)]


def project_kernel(core, tokens, mods, offset, matrix, mine, away, moved, made):
    width = tokens.shape[1]
    half = width // 2

    @pl.when(pl.program_id(0) == 0)
    def _():
        for at in row_chunks(tokens.shape[0]):
            normed, _ = norm_rows(tokens[at, :].astype(f32))
            moved[at, :] = (normed * (1.0 + mods[:, width : 2 * width]) + mods[:, :width]).astype(bf16)

    made[...] = (dot(moved[...], matrix[...]) + offset[...]).astype(bf16)
    for kind in range(3):

        @pl.when(pl.program_id(0) == kind)
        def _():
            def work(c):
                for ref, d in ((mine, c), (away, 1 - c)):
                    ref[:, kind * half : (kind + 1) * half] = made[:, d * half : (d + 1) * half]

            on_core(core, work)


def project(core, matrix, tokens, mods, offset):
    rows, width = tokens.shape
    wide = matrix.shape[1]
    return pl.pallas_call(
        project_kernel,
        out_shape=(
            shaped((rows, wide // 2), bf16),
            shaped((rows, lanes(wide // 2)), bf16),
            shaped((rows, width), bf16),
        ),
        grid=(3,),
        in_specs=[
            SMEM,
            WHOLE,
            WHOLE,
            pl.BlockSpec((1, width), lambda i: (0, i)),
            pl.BlockSpec((width, width), lambda i: (0, i)),
        ],
        out_specs=(WHOLE,) * 3,
        scratch_shapes=[pltpu.VMEM((rows, width), bf16)],
        compiler_params=params(48),
        cost_estimate=lasts(13),
    )(core, *in_hbm(tokens, mods, offset, matrix))


def middle_kernel(number, core, spots, own, got, tokens, mods, offset, *refs):
    pieces = refs[:number]
    attended, projected, normed, factor, moved, whole, matrix, sems, out_sem = refs[number:]
    assemble(spots, pieces, matrix, sems)
    out = pltpu.make_async_copy(matrix, whole, out_sem)
    out.start()
    width = matrix.shape[1]
    half = width // 2

    def work(c):
        attended[:, c * half : (c + 1) * half] = own[...]
        attended[:, (1 - c) * half : (2 - c) * half] = got[:, :half]

    on_core(core, work)
    gate1, shift2, scale2 = (mods[:, i * width : (i + 1) * width] for i in (2, 3, 4))
    projected[...] = dot(attended[...], matrix[...]) + offset[...]
    for at in row_chunks(own.shape[0]):
        made = projected[at, :]
        value = tokens[at, :].astype(f32) + gate1 * made
        value, scale = norm_rows(value)
        normed[at, :] = value
        factor[at, :] = scale
        moved[at, :] = (value * (1.0 + scale2) + shift2).astype(bf16)
    out.wait()


def middle_part(core, gathered, own, got, tokens, mods, offset):
    spots, pieces = gathered
    rows, width = tokens.shape
    return pl.pallas_call(
        functools.partial(middle_kernel, len(pieces)),
        out_shape=(
            shaped((rows, width), bf16),
            shaped((rows, width), f32),
            shaped((rows, width), f32),
            shaped((rows, 1), f32),
            shaped((rows, width), bf16),
            shaped((width, width), bf16),
        ),
        in_specs=[SMEM, SMEM] + [WHOLE] * 5 + [HBM] * len(pieces),
        out_specs=(WHOLE,) * 5 + (HBM,),
        scratch_shapes=[
            pltpu.VMEM((width, width), bf16),
            pltpu.SemaphoreType.DMA((len(pieces),)),
            pltpu.SemaphoreType.DMA,
        ],
        compiler_params=params(48),
        cost_estimate=lasts(9),
    )(core, spots, *in_hbm(own, got, tokens, mods, offset, *pieces))


def up_kernel(moved, matrix, offset, act, slope):
    for at in row_chunks(moved.shape[0], 256):
        u = dot(moved[at, :], matrix[...]) + offset[...]
        square = u * u
        t = jnp.tanh(ROOT * (u + 0.044715 * (square * u)))
        act[at, :] = (0.5 * u * (1.0 + t)).astype(bf16)
        slope[at, :] = 0.5 * (1.0 + t) + (0.5 * ROOT) * u * (1.0 - t * t) * (1.0 + (3 * 0.044715) * square)


def up_part(moved, matrix, offset):
    (rows, width), hidden = moved.shape, matrix.shape[1]
    step = hidden // 4
    return pl.pallas_call(
        up_kernel,
        out_shape=(shaped((rows, hidden), bf16), shaped((rows, hidden), f32)),
        grid=(4,),
        in_specs=[WHOLE, pl.BlockSpec((width, step), lambda i: (0, i)), pl.BlockSpec((1, step), lambda i: (0, i))],
        out_specs=(pl.BlockSpec((rows, step), lambda i: (0, i)), pl.BlockSpec((rows, step), lambda i: (0, i))),
        compiler_params=params(48),
        cost_estimate=lasts(16),
    )(*in_hbm(moved, matrix, offset))


def slope_kernel(number, spots, grad, slope, *refs):
    pieces = refs[:number]
    d_upper, sums, whole, matrix, sems, out_sem = refs[number:]
    step = pl.program_id(0)
    size = sums.shape[1]
    out = pltpu.make_async_copy(matrix, whole, out_sem)

    @pl.when(step == 0)
    def _():
        assemble(spots, pieces, matrix, sems)
        out.start()

    part = matrix.at[pl.ds(pl.multiple_of(step * size, size), size)]
    total = jnp.zeros(sums.shape, f32)
    for at in row_chunks(grad.shape[0], 256):
        value = (dot(grad[at, :], part[...], NT) * slope[at, :]).astype(bf16)
        d_upper[at, :] = value
        total = total + jnp.sum(value.astype(f32), axis=0, keepdims=True)
    sums[...] = total

    @pl.when(step == pl.num_programs(0) - 1)
    def _():
        out.wait()


def slope_part(grad, gathered, slope):
    spots, pieces = gathered
    (rows, width), hidden = grad.shape, slope.shape[1]
    step = hidden // 4
    across = pl.BlockSpec((rows, step), lambda i: (0, i))
    return pl.pallas_call(
        functools.partial(slope_kernel, len(pieces)),
        out_shape=(shaped((rows, hidden), bf16), shaped((1, hidden), f32), shaped((hidden, width), bf16)),
        grid=(4,),
        in_specs=[SMEM, WHOLE, across] + [HBM] * len(pieces),
        out_specs=(across, pl.BlockSpec((1, step), lambda i: (0, i)), HBM),
        scratch_shapes=[
            pltpu.VMEM((hidden, width), bf16),
            pltpu.SemaphoreType.DMA((len(pieces),)),
            pltpu.SemaphoreType.DMA,
        ],
        compiler_params=params(48),
        cost_estimate=lasts(40),
    )(spots, *in_hbm(grad, slope, *pieces))


def down_kernel(act, matrix, offset, tokens, projected, mods, grad, output, d_gate, total):
    step = pl.program_id(0)
    width = matrix.shape[1]

    @pl.when(step == 0)
    def _():
        total[...] = dot(act[...], matrix[...])

    @pl.when(step > 0)
    def _():
        total[...] += dot(act[...], matrix[...])

    @pl.when(step == pl.num_programs(0) - 1)
    def _():
        gate1, gate2 = mods[:, 2 * width : 3 * width], mods[:, 5 * width :]
        summed = jnp.zeros(d_gate.shape, f32)
        for at in row_chunks(act.shape[0]):
            lowered = total[at, :] + offset[...]
            middle = tokens[at, :].astype(f32) + gate1 * projected[at, :]
            output[at, :] = (middle + gate2 * lowered).astype(bf16)
            summed = summed + jnp.sum(grad[at, :].astype(f32) * lowered, axis=0, keepdims=True)
        d_gate[...] = summed


def down_part(act, matrix, offset, tokens, projected, mods, grad):
    rows, hidden = act.shape
    step, width = hidden // 4, matrix.shape[1]
    return pl.pallas_call(
        down_kernel,
        out_shape=(shaped((rows, width), bf16), shaped((1, width), f32)),
        grid=(4,),
        in_specs=[pl.BlockSpec((rows, step), lambda i: (0, i)), pl.BlockSpec((step, width), lambda i: (i, 0))]
        + [WHOLE] * 5,
        out_specs=(WHOLE, WHOLE),
        scratch_shapes=[pltpu.VMEM((rows, width), f32)],
        compiler_params=params(48),
        cost_estimate=lasts(6),
    )(*in_hbm(act, matrix, offset, tokens, projected, mods, grad))


def middle_back_kernel(core, d_upper, matrix, normed, factor, projected, grad, mods, out_matrix, d_middle, d_projected, mine, away, sums, total):
    step = pl.program_id(0)
    width = matrix.shape[0]
    half = width // 2

    @pl.when(step == 0)
    def _():
        total[...] = dot(d_upper[...], matrix[...], NT)

    @pl.when(step > 0)
    def _():
        total[...] += dot(d_upper[...], matrix[...], NT)

    @pl.when(step == pl.num_programs(0) - 1)
    def _():
        gate1, scale2 = mods[:, 2 * width : 3 * width], mods[:, 4 * width : 5 * width]
        summed = [jnp.zeros((1, width), f32) for _ in range(4)]
        for at in row_chunks(grad.shape[0]):
            d_moved, n = total[at, :], normed[at, :]
            value = grad[at, :].astype(f32) + back_rows(d_moved * (1.0 + scale2), n, factor[at, :])
            d_middle[at, :] = value
            d_proj = (gate1 * value).astype(bf16)
            d_projected[at, :] = d_proj
            terms = d_moved, d_moved * n, value * projected[at, :], d_proj.astype(f32)
            summed = [u + jnp.sum(v, axis=0, keepdims=True) for u, v in zip(summed, terms)]
        total[...] = dot(d_projected[...], out_matrix[...], NT)

        def work(c):
            mine[...] = total[:, c * half : (c + 1) * half].astype(bf16)
            away[:, :half] = total[:, (1 - c) * half : (2 - c) * half].astype(bf16)

        on_core(core, work)
        for i, value in enumerate(summed):
            sums[i : i + 1, :] = value


def middle_back(core, d_upper, matrix, normed, factor, projected, grad, mods, out_matrix):
    rows, hidden = d_upper.shape
    step, width = hidden // 4, matrix.shape[0]
    return pl.pallas_call(
        middle_back_kernel,
        out_shape=(
            shaped((rows, width), f32),
            shaped((rows, width), bf16),
            shaped((rows, width // 2), bf16),
            shaped((rows, lanes(width // 2)), bf16),
            shaped((4, width), f32),
        ),
        grid=(4,),
        in_specs=[SMEM, pl.BlockSpec((rows, step), lambda i: (0, i)), pl.BlockSpec((width, step), lambda i: (0, i))]
        + [WHOLE] * 6,
        out_specs=(WHOLE,) * 5,
        scratch_shapes=[pltpu.VMEM((rows, width), f32)],
        compiler_params=params(48),
        cost_estimate=lasts(150),
    )(core, *in_hbm(d_upper, matrix, normed, factor, projected, grad, mods, out_matrix))


def input_back_kernel(d_qkv, matrix, tokens, mods, d_middle, input_grad, sums, columns, total):
    step = pl.program_id(0)
    width = matrix.shape[0]
    columns[...] = jnp.sum(d_qkv[...].astype(f32), axis=0, keepdims=True)

    @pl.when(step == 0)
    def _():
        total[...] = dot(d_qkv[...], matrix[...], NT)

    @pl.when(step > 0)
    def _():
        total[...] += dot(d_qkv[...], matrix[...], NT)

    @pl.when(step == pl.num_programs(0) - 1)
    def _():
        scale1 = mods[:, width : 2 * width]
        summed = [jnp.zeros((1, width), f32) for _ in range(2)]
        for at in row_chunks(tokens.shape[0]):
            normed, factor = norm_rows(tokens[at, :].astype(f32))
            d_moved = total[at, :]
            input_grad[at, :] = (d_middle[at, :] + back_rows(d_moved * (1.0 + scale1), normed, factor)).astype(bf16)
            summed = [u + jnp.sum(v, axis=0, keepdims=True) for u, v in zip(summed, (d_moved, d_moved * normed))]
        for i, value in enumerate(summed):
            sums[i : i + 1, :] = value


def input_back(d_qkv, matrix, tokens, mods, d_middle):
    rows, wide = d_qkv.shape
    width = matrix.shape[0]
    return pl.pallas_call(
        input_back_kernel,
        out_shape=(shaped((rows, width), bf16), shaped((2, width), f32), shaped((1, wide), f32)),
        grid=(wide // width,),
        in_specs=[pl.BlockSpec((rows, width), lambda i: (0, i)), pl.BlockSpec((width, width), lambda i: (0, i))]
        + [WHOLE] * 3,
        out_specs=(WHOLE, WHOLE, pl.BlockSpec((1, width), lambda i: (0, i))),
        scratch_shapes=[pltpu.VMEM((rows, width), f32)],
        compiler_params=params(48),
        cost_estimate=lasts(120),
    )(*in_hbm(d_qkv, matrix, tokens, mods, d_middle))


def cut_of(rows):
    return rows // 2 // 8 * 8


def keep(made, e, value):
    if len(made) == 1:
        made[0][e] = value
    elif e == 3 and len(made) == 5:
        cut = made[3].shape[0]
        made[3][...], made[4][...] = value[:cut], value[cut:]
    else:
        made[e][...] = value


def pair_grad_kernel(added, where, left, right, *refs):
    gots, made = refs[:added], refs[added:]
    half = left.shape[1] // 2
    step = pl.program_id(0)
    for d in range(2):

        @pl.when(where[1] == d)
        def _():
            value = dot(left[:, d * half : (d + 1) * half], right[...], TN)
            for e in range(4):

                @pl.when(step == e)
                def _():
                    more = gots[0][e].astype(f32) if added else 0.0
                    keep(made, e, (value + more).astype(bf16))


def grad_shapes(rows, columns, added):
    cut = cut_of(rows)
    return [(rows, columns)] * 3 + [(cut, columns), (rows - cut, columns)] if added else [(4, rows, columns)]


def pair_grad(left, right, b, side, gots=()):
    slots, wide = left.shape
    step = wide // 4
    where = jnp.stack([b >> 1, side]).astype(jnp.int32)
    shapes = grad_shapes(step // 2, right.shape[1], len(gots))
    whole = lambda shape: pl.BlockSpec(shape, lambda m, where: (0,) * len(shape))
    specs = [pl.BlockSpec((slots, step), lambda m, where: (0, where[0] ^ m)), whole(right.shape)]
    return pl.pallas_call(
        functools.partial(pair_grad_kernel, len(gots)),
        out_shape=tuple(shaped(shape, bf16) for shape in shapes),
        grid_spec=pltpu.PrefetchScalarGridSpec(
            num_scalar_prefetch=1,
            grid=(4,),
            in_specs=specs + [whole(got.shape) for got in gots],
            out_specs=tuple(whole(shape) for shape in shapes),
        ),
        compiler_params=params(48),
        cost_estimate=lasts(9),
    )(where, *in_hbm(left, right, *gots))


def block_grad_kernel(added, spots, left, right, *refs):
    gots, made, (chosen, turned) = refs[:added], refs[added:-2], refs[-2:]
    rows = made[0].shape[-2]

    @pl.when(pl.program_id(0) == 0)
    def _():
        turned[...] = jnp.transpose(left[...])
        for e in range(4):
            at = pl.ds(pl.multiple_of(spots[e], 16), rows)
            chosen[e * rows : (e + 1) * rows, :] = turned[at, :]

    value = dot(chosen[...], right[...])
    for e in range(4):
        part = value[e * rows : (e + 1) * rows, :]
        if added:
            part = part + gots[0][e].astype(f32)
        keep(made, e, part.astype(bf16))


def block_grad(left, right, b, side, gots=()):
    (slots, wide), columns = left.shape, right.shape[1]
    rows = wide // 8
    spots = jnp.stack([((b >> 1) ^ m) * 2 * rows + side * rows for m in range(4)]).astype(jnp.int32)
    step = 1152 if columns % 1152 == 0 else columns
    shapes = grad_shapes(rows, columns, len(gots))
    block = lambda shape: pl.BlockSpec(shape[:-1] + (step,), lambda i: (0,) * (len(shape) - 1) + (i,))
    return pl.pallas_call(
        functools.partial(block_grad_kernel, len(gots)),
        out_shape=tuple(shaped(shape, bf16) for shape in shapes),
        grid=(columns // step,),
        in_specs=[SMEM, WHOLE, pl.BlockSpec((slots, step), lambda i: (0, i))] + [block(got.shape) for got in gots],
        out_specs=tuple(block(shape) for shape in shapes),
        scratch_shapes=[pltpu.VMEM((4 * rows, slots), bf16), pltpu.VMEM((wide, slots), bf16)],
        compiler_params=params(48),
        cost_estimate=lasts(columns // 1152),
    )(spots, *in_hbm(left, right, *gots))


def mix_kernel(to_x, to_y, got_x, got_y, out_x, out_y):
    cut = got_x.shape[0]
    out_x[:cut, :] = to_x[:cut, :]
    out_x[cut:, :] = add(to_x[cut:, :], got_y[...])
    out_y[:cut, :] = add(to_y[:cut, :], got_x[...])
    out_y[cut:, :] = to_y[cut:, :]


def mix(to_x, to_y, got_x, got_y):
    rows, columns = to_x.shape
    step = 1152
    block = lambda array: pl.BlockSpec((array.shape[0], step), lambda i: (0, i))
    return pl.pallas_call(
        mix_kernel,
        out_shape=(shaped(to_x.shape, bf16),) * 2,
        grid=(columns // step,),
        in_specs=[block(array) for array in (to_x, to_y, got_x, got_y)],
        out_specs=(block(to_x),) * 2,
        compiler_params=params(48),
        cost_estimate=lasts(1),
    )(*in_hbm(to_x, to_y, got_x, got_y))


def fill(h, heads, mine, theirs, qs, ks, vs):
    half, wide, lo = mine.shape[0], heads * HEAD, h * HEAD
    for part, ref in ((0, mine), (1, theirs)):
        rows = slice(part * half, (part + 1) * half)
        qs[rows, :HEAD] = ref[:, lo : lo + HEAD]
        ks[rows, :HEAD] = ref[:, wide + lo : wide + lo + HEAD]
        vs[rows, :] = ref[:, 2 * wide + lo : 2 * wide + lo + HEAD]


def mark_valid(limits, qs, ks):
    total = qs.shape[0]
    chunks = limits.shape[0]
    sub = lax.broadcasted_iota(jnp.int32, (total // chunks, 1), 0)
    bias = jnp.concatenate([jnp.where(sub < limits[i], 0.0, -1e30) for i in range(chunks)], axis=0)
    qs[...] = jnp.zeros_like(qs)
    ks[...] = jnp.zeros_like(ks)
    qs[:, HEAD : HEAD + 1] = jnp.ones((total, 1), bf16)
    ks[:, HEAD : HEAD + 1] = bias.astype(bf16)


def attend_kernel(heads, limits, mine, theirs, out_mine, out_theirs, lse, qs, ks, vs, os, ls):
    half = mine.shape[0]
    total = 2 * half
    mark_valid(limits, qs, ks)
    for h in range(heads):
        fill(h, heads, mine, theirs, qs, ks, vs)
        for i in range(total // BLOCK):
            at = slice(i * BLOCK, (i + 1) * BLOCK)
            scores = dot(qs[at, :], ks[...], NT) * (SCALE * LOG2E)
            peak = jnp.max(scores, axis=1, keepdims=True)
            expo = jnp.exp2(scores - peak)
            summed = jnp.sum(expo, axis=1, keepdims=True)
            probs = (expo * (1.0 / summed)).astype(bf16)
            os[at, :] = dot(probs, vs[...]).astype(bf16)
            ls[at, :] = peak + jnp.log2(summed)
        lo = h * HEAD
        out_mine[:, lo : lo + HEAD] = os[:half, :]
        out_theirs[:, lo : lo + HEAD] = os[half:, :]
        lse[h : h + 1, :] = jnp.transpose(ls[...])


def attend(limits, mine, theirs):
    half, wide3 = mine.shape
    wide = wide3 // 3
    heads = wide // HEAD
    total = 2 * half
    return pl.pallas_call(
        functools.partial(attend_kernel, heads),
        out_shape=(shaped((half, wide), bf16), shaped((half, lanes(wide)), bf16), shaped((heads, total), f32)),
        in_specs=[SMEM, WHOLE, WHOLE],
        out_specs=(WHOLE,) * 3,
        scratch_shapes=[
            pltpu.VMEM((total, PAD), bf16),
            pltpu.VMEM((total, PAD), bf16),
            pltpu.VMEM((total, HEAD), bf16),
            pltpu.VMEM((total, HEAD), bf16),
            pltpu.VMEM((total, 1), f32),
        ],
        compiler_params=params(VMEM_ATT),
        cost_estimate=lasts(27),
    )(limits, *in_hbm(mine, theirs))


def back_kernel(heads, first, number, limits, mine, theirs, d_mine, d_theirs, lse, out_mine, out_theirs, qs, ks, vs, ds, dq, dk, dv):
    half = mine.shape[0]
    total = 2 * half
    narrow = number * HEAD
    mark_valid(limits, qs, ks)
    for h in range(first, first + number):
        fill(h, heads, mine, theirs, qs, ks, vs)
        lo = h * HEAD
        ds[:half, :] = d_mine[:, lo : lo + HEAD]
        ds[half:, :] = d_theirs[:, lo : lo + HEAD]
        for i in range(total // BLOCK):
            at = slice(i * BLOCK, (i + 1) * BLOCK)
            query, d_out = qs[at, :], ds[at, :]
            exact = jnp.exp2(dot(ks[...], query, NT) * (SCALE * LOG2E) - lse[h : h + 1, at])
            d_probs = dot(vs[...], d_out, NT)
            more = dot(exact.astype(bf16), d_out)
            dv[...] = more if i == 0 else dv[...] + more
            product = exact * d_probs
            centred = jnp.sum(product, axis=0, keepdims=True)
            d_scores = (product - exact * centred).astype(bf16)
            more = dot(d_scores, query)
            dk[...] = more if i == 0 else dk[...] + more
            dq[at, :] = (dot(d_scores, ks[...], TN) * SCALE).astype(bf16)
        lo = (h - first) * HEAD
        for part, ref in ((0, out_mine), (1, out_theirs)):
            rows = slice(part * half, (part + 1) * half)
            ref[:, lo : lo + HEAD] = dq[rows, :HEAD]
            ref[:, narrow + lo : narrow + lo + HEAD] = (dk[rows, :HEAD] * SCALE).astype(bf16)
            ref[:, 2 * narrow + lo : 2 * narrow + lo + HEAD] = dv[rows, :].astype(bf16)


def attend_back(limits, mine, theirs, d_mine, d_theirs, lse, first, number):
    half, wide3 = mine.shape
    wide = wide3 // 3
    heads = wide // HEAD
    total = 2 * half
    return pl.pallas_call(
        functools.partial(back_kernel, heads, first, number),
        out_shape=(shaped((half, 3 * number * HEAD), bf16), shaped((half, lanes(3 * number * HEAD)), bf16)),
        in_specs=[SMEM] + [WHOLE] * 5,
        out_specs=(WHOLE,) * 2,
        scratch_shapes=[
            pltpu.VMEM((total, PAD), bf16),
            pltpu.VMEM((total, PAD), bf16),
            pltpu.VMEM((total, HEAD), bf16),
            pltpu.VMEM((total, HEAD), bf16),
            pltpu.VMEM((total, PAD), bf16),
            pltpu.VMEM((total, PAD), f32),
            pltpu.VMEM((total, HEAD), f32),
        ],
        compiler_params=params(VMEM_ATT),
        cost_estimate=lasts(4),
    )(limits, *in_hbm(mine, theirs, d_mine, d_theirs, lse))


def pair_swap(array):
    size = lax.axis_size("batch")
    return lax.ppermute(array, "batch", [(i, i ^ 1) for i in range(size)])


def by_core(own, other):
    first = (lax.axis_index("batch") & 1) == 0
    return jnp.where(first, jnp.stack([own, other]), jnp.stack([other, own]))


def deal(array):
    c = lax.axis_index("batch") & 1
    samples, slots, width = array.shape
    halves = array.reshape(samples, 2, slots // 2, width)
    own = lax.dynamic_index_in_dim(halves, c, axis=1, keepdims=False)
    other = pair_swap(lax.dynamic_index_in_dim(halves, 1 - c, axis=1, keepdims=False))
    every = by_core(own, other).reshape(2 * samples, slots // 2, width)
    return lax.all_to_all(every, "seq", 0, 0, tiled=True).reshape(samples * slots, width)


def undeal(array):
    c = lax.axis_index("batch") & 1
    rows, width = array.shape
    every = lax.all_to_all(array.reshape(4, rows // 4, width), "seq", 0, 0, tiled=True)
    every = every.reshape(2, 2, rows // 4, width)
    own = lax.dynamic_index_in_dim(every, c, axis=0, keepdims=False)
    other = pair_swap(lax.dynamic_index_in_dim(every, 1 - c, axis=0, keepdims=False))
    return by_core(own, other).transpose(1, 0, 2, 3).reshape(2, rows // 2, width)


def gather(array):
    return lax.all_gather(array, "batch", axis=0, tiled=True)


def hop(array, bits):
    size = lax.axis_size("batch")
    return lax.ppermute(array, "batch", [(i, i ^ bits) for i in range(size)])


class Hops:
    def __init__(self, array):
        self.array = array
        self.plain = lax.axis_size("batch") != 8
        if self.plain:
            self.whole = gather(array)
            self.moving = (self.whole,)
        else:
            self.moving = self.along_x, self.along_y = hop(array, 2), hop(array, 4)

    def turn(self, *done):
        if self.plain:
            return self.moving
        self.cut = self.array.shape[0] // 2 // 16 * 16
        self.along_x, self.along_y = after((self.along_x, self.along_y), *done)
        self.corner = hop(self.along_x[: self.cut], 4), hop(self.along_y[self.cut :], 2)
        self.moving = self.along_x, self.along_y, *self.corner
        return self.moving

    def pieces(self, *done):
        if self.plain:
            return jnp.zeros((1,), jnp.int32), [self.whole]
        rows, cut = self.array.shape[0], self.cut
        b = lax.axis_index("batch")
        along_x, along_y, *corner = after(self.moving, *done)
        pieces = [(0, 0, self.array), (2, 0, along_x), (4, 0, along_y), (6, 0, corner[0]), (6, cut, corner[1])]
        pieces += [(bits ^ 1, at, hop(piece, 1)) for bits, at, piece in pieces]
        spots = jnp.stack([(b ^ bits) * rows + at for bits, at, _ in pieces]).astype(jnp.int32)
        return spots, [piece for _, _, piece in pieces]


def after(value, *done):
    return lax.optimization_barrier((value, done))[0]


def add(u, v):
    return (u.astype(f32) + v.astype(f32)).astype(bf16)


class Grad:
    def __init__(self, left, right, paired=False):
        self.left, self.right, self.paired = left, right, paired
        self.rows = left.shape[1] // lax.axis_size("batch")
        self.plain = lax.axis_size("batch") != 8 or lax.axis_size("seq") != 4

    def away(self, *done):
        if self.plain:
            made = self.made = dot(after(self.left, *done), self.right, TN).astype(bf16)
            return made
        self.left = after(self.left, *done)
        b = lax.axis_index("batch")
        made = (pair_grad if self.paired else block_grad)(self.left, self.right, b, 1 - (b & 1))
        self.gots = [hop(made[0], 1)]
        return made

    def stay(self, *done):
        if self.plain:
            part = lax.psum_scatter(self.made, "batch", scatter_dimension=0, tiled=True)
            self.part = lax.psum(part, "seq")
            return self.part
        self.left = after(self.left, *done)
        b = lax.axis_index("batch")
        made = (pair_grad if self.paired else block_grad)(self.left, self.right, b, b & 1, self.gots)
        self.own, self.to_x, self.to_y, corner_x, corner_y = made
        self.got_x, self.got_y = hop(corner_x, 2), hop(corner_y, 4)
        return made

    def mix(self, *done):
        if self.plain:
            return self.part
        to_x, to_y = after((self.to_x, self.to_y), *done)
        made = mix(to_x, to_y, self.got_x, self.got_y)
        self.got_x, self.got_y = hop(made[0], 2), hop(made[1], 4)
        return made

    def finish(self, *done, extra=None):
        if self.plain:
            return (self.land(extra=extra),) * 2
        own = after(self.own, *done)
        part = (own.astype(f32) + self.got_x.astype(f32) + self.got_y.astype(f32)).astype(bf16)
        if extra is not None:
            part = jnp.concatenate([part, extra.astype(bf16)], axis=0)
        total = lax.psum(part, "seq")
        self.part, self.plain = total[: self.rows], True
        if extra is not None:
            self.extra = total[self.rows :].astype(f32)
        return part, total

    def land(self, *done, extra=None, chunks=1):
        if self.plain:
            if extra is not None:
                self.extra = lax.psum(extra, "seq")
            return self.part
        own = after(self.own, *done)
        part = (own.astype(f32) + self.got_x.astype(f32) + self.got_y.astype(f32)).astype(bf16)
        if extra is not None:
            part = jnp.concatenate([part, extra.astype(bf16)], axis=0)
        step = -(-part.shape[0] // chunks // 8) * 8
        self.parts = [part[i * step : (i + 1) * step] for i in range(chunks)]
        self.gots = [lax.ppermute(part, "seq", [(0, 1), (3, 2)]) for part in self.parts]
        return part

    def pass_on(self, pairs, done):
        if self.plain:
            return self.part
        parts = after(tuple(self.parts), *done)
        self.parts, gots = [], self.gots
        self.gots = []
        for part, got in zip(parts, gots):
            part = add(part, got)
            self.parts.append(part)
            self.gots.append(lax.ppermute(part, "seq", pairs))
        return tuple(self.parts)

    def across(self, *done):
        return self.pass_on([(1, 2), (2, 1)], done)

    def outward(self, *done):
        return self.pass_on([(1, 0), (2, 3)], done)

    def result(self, *done):
        if self.plain:
            part = after(self.part, *done).astype(f32)
            return part if not hasattr(self, "extra") else (part, self.extra)
        s = lax.axis_index("seq")
        ends = (s == 0) | (s == 3)
        parts = after(tuple(self.parts), *done)
        total = [jnp.where(ends, got, part).astype(f32) for part, got in zip(parts, self.gots)]
        total = total[0] if len(total) == 1 else jnp.concatenate(total, axis=0)
        if total.shape[0] > self.rows:
            return total[: self.rows], total[self.rows :]
        return total


def all_samples(row):
    rows = row[None]
    for bit in (1, 2):
        rows = jnp.concatenate([rows, lax.ppermute(rows, "seq", [(i, i ^ bit) for i in range(4)])], axis=0)
    return rows


def all_pairs(rows):
    bits = 2
    while bits < lax.axis_size("batch"):
        rows = jnp.concatenate([rows, hop(rows, bits)], axis=0)
        bits *= 2
    return rows


def xor_order(array, index):
    size, bit = array.shape[0], 1
    while bit < size:
        split = array.reshape((size // (2 * bit), 2, bit) + array.shape[1:])
        array = jnp.where((index & bit) != 0, split[:, ::-1], split).reshape(array.shape)
        bit *= 2
    return array


def body(
    inputs,
    conds,
    heights,
    widths,
    qkv_weight,
    qv_bias,
    out_weight,
    out_bias,
    up_weight,
    up_bias,
    down_weight,
    down_bias,
    mod_weight,
    mod_bias,
    cotangent,
):
    devices = lax.axis_size("batch")
    b, s = lax.axis_index("batch"), lax.axis_index("seq")
    c = b & 1
    width = inputs.shape[2]
    hidden = up_weight.shape[1]
    slot_dev = inputs.shape[1]
    half = slot_dev // 2
    rows = qkv_weight.shape[0]
    mods = mod_weight.shape[1]

    tokens16 = deal(inputs)
    upstream16 = deal(cotangent)

    core = jnp.reshape(c, (1,)).astype(jnp.int32)
    qkv_matrix = gather(qkv_weight)
    out_hops = Hops(out_weight)

    small = [conds.reshape(-1), qv_bias, out_bias, up_bias, down_bias, heights.astype(bf16), widths.astype(bf16)]
    spots = [sum(e.size for e in small[:i]) for i in range(len(small) + 1)]
    small.append(jnp.zeros((-spots[-1] % 128,), bf16))
    small = gather(jnp.concatenate(small)[None])
    every = [small[:, spots[i] : spots[i + 1]] for i in range(7)]
    cond_all = every[0].reshape(2 * devices, width)
    qv_offset, out_offset, up_offset, down_offset = (e.reshape(-1).astype(f32) for e in every[1:5])
    counts = (every[5].astype(jnp.int32) * every[6].astype(jnp.int32)).reshape(2 * devices)
    sample = 4 * (b // 2) + s
    count = lax.dynamic_index_in_dim(counts, sample, keepdims=False)

    silu_all = jax.nn.silu(cond_all.astype(f32)).astype(bf16)
    silu_rows = lax.dynamic_slice(silu_all, (0, b * rows), (2 * devices, rows))
    plane = lax.dynamic_index_in_dim(silu_rows.reshape(devices // 2, 4, rows), s, axis=1, keepdims=False)
    partial = dot(plane, mod_weight)
    own_bias = lax.dynamic_update_slice(jnp.zeros((mods,), f32), mod_bias.astype(f32), (b * mod_bias.shape[0],))
    partial = partial + own_bias[None]
    partial = jnp.broadcast_to(partial[:, None], (devices // 2, 2, mods)).reshape(devices, mods)
    modulation = jnp.sum(lax.all_to_all(partial, "batch", 0, 0, tiled=True), axis=0, keepdims=True)
    gate2 = modulation[:, 5 * width :]
    out_hops.turn(modulation)
    tokens16 = after(tokens16, out_hops.moving)
    out_pieces = out_hops.pieces()
    up_matrix = gather(after(up_weight, modulation))

    limits = [count - (slot_dev * i + half * (c ^ part)) for part in range(2) for i in range(4)]
    limits = jnp.stack(limits).astype(jnp.int32)
    tokens16 = after(tokens16, limits)

    offsets = jnp.concatenate([qv_offset[:width], jnp.zeros((width,), f32), qv_offset[width:]])
    mine, away, moved = project(core, qkv_matrix, tokens16, modulation, offsets[None])
    theirs = pair_swap(away)
    down_hops = Hops(after(down_weight, mine))
    att_mine, att_away, lse = attend(limits, after(mine, out_pieces[1]), theirs)
    first = down_hops.moving
    down_hops.turn(att_mine)
    down_pieces = down_hops.pieces()
    attended, projected, normed2, factor2, moved2, out_matrix = middle_part(
        core, out_pieces, att_mine, pair_swap(att_away), tokens16, modulation, out_offset[None]
    )
    act, slope = up_part(moved2, up_matrix, up_offset[None])

    d_lowered = (gate2 * upstream16.astype(f32)).astype(bf16)
    down_offset_grad = jnp.sum(d_lowered.astype(f32), axis=0)
    down_g = Grad(act, d_lowered, True)
    mark = down_g.away(act, first)
    mark = down_g.stay(mark)
    d_upper, up_sums, down_matrix = slope_part(after(d_lowered, mark), down_pieces, slope)
    mark = down_g.mix(d_upper)
    output, d_gate2 = down_part(
        after(act, mark), down_matrix, down_offset[None], tokens16, projected, modulation, upstream16
    )
    up_g = Grad(moved2, d_upper)
    mark = up_g.away(output)
    d_middle, d_projected, d_att_mine, d_att_away, sums2 = middle_back(
        core, after(d_upper, mark), up_matrix, normed2, factor2, projected, upstream16, modulation, out_matrix
    )
    d_shift2, d_scale2, d_gate1, out_offset_grad = sums2
    d_att_theirs = pair_swap(d_att_away)
    output = undeal(output)
    mark, down_total = down_g.finish(d_att_mine)
    mark = up_g.stay(mark)
    out_g = Grad(attended, d_projected)
    mark = out_g.away(mark)
    heads = HEADS // 2
    steps = 2
    own, got = [], []
    for i in range(steps):
        made = attend_back(
            limits, after(mine, mark), theirs, d_att_mine, d_att_theirs, lse, i * heads // steps, heads // steps
        )
        own.append(made[0])
        got.append(pair_swap(made[1]))
        mark = made
        if i == 0:
            mark = up_g.mix(mark)
            mark = out_g.stay(mark)
    d_qkv = join_heads(core, own, got)
    mark, up_total = up_g.finish(d_qkv, down_total, output)
    qkv_g = Grad(moved, d_qkv)
    mark = qkv_g.away(mark)
    mark = out_g.mix(mark)
    input_grad, sums1, column_sums = input_back(after(d_qkv, mark), qkv_matrix, tokens16, modulation, d_middle)
    d_shift1, d_scale1 = sums1
    mark = qkv_g.stay(input_grad)
    input_grad = undeal(after(input_grad, mark)).astype(f32)
    column_sums = after(column_sums[0], mark)
    qv_offset_grad = jnp.concatenate([column_sums[:width], column_sums[2 * width :]])
    own_shapes = (qv_bias.shape[0], out_bias.shape[0], up_bias.shape[0], down_bias.shape[0])
    bias = jnp.concatenate(
        [
            g.reshape(devices, -1)
            for g in (qv_offset_grad, out_offset_grad, up_sums, down_offset_grad)
        ],
        axis=1,
    )
    length = bias.shape[1]
    bias = jnp.sum(lax.all_to_all(bias, "batch", 0, 0, tiled=True), axis=0, keepdims=True)
    bias = jnp.pad(bias, ((0, 7), (0, 3 * width - length)))
    partial_mod = jnp.concatenate([d_shift1, d_scale1, d_gate1, d_shift2, d_scale2, d_gate2[0]])
    partial_mod = after(partial_mod, mark)
    d_mod = (partial_mod + pair_swap(partial_mod)).astype(bf16)
    d_mod_four = all_samples(d_mod)
    mark = qkv_g.mix(bias, d_mod_four)
    d_mod_all = all_pairs(after(d_mod_four, mark))
    mark, _ = out_g.finish(mark, up_total)
    mark, _ = qkv_g.finish(mark, up_total, extra=bias)
    mod_grad = dot(xor_order(silu_rows, sample), d_mod_all, TN)
    mod_offset_grad = jnp.sum(
        lax.dynamic_slice(d_mod_all, (0, b * mod_bias.shape[0]), (2 * devices, mod_bias.shape[0])).astype(f32), axis=0
    )
    d_silu_rows = xor_order(dot(d_mod_all, mod_weight, NT), sample)
    d_silu = lax.all_to_all(d_silu_rows.reshape(devices, 2 * rows), "batch", 0, 0, tiled=True)
    d_silu = d_silu.reshape(devices, 2, rows).transpose(1, 0, 2).reshape(2, width)
    cond_grad = jax.vjp(jax.nn.silu, conds.astype(f32))[1](d_silu)[0]

    down_grad, up_grad, out_grad = (grad.result(d_mod_all) for grad in (down_g, up_g, out_g))
    qkv_grad, bias = qkv_g.result()
    bias = bias[0, :length]
    cuts = [sum(own_shapes[:i]) for i in range(5)]
    qv_b, out_b, up_b, down_b = (bias[cuts[i] : cuts[i + 1]] for i in range(4))
    return (
        output,
        input_grad,
        cond_grad,
        qkv_grad,
        qv_b,
        out_grad,
        out_b,
        up_grad,
        up_b,
        down_grad,
        down_b,
        mod_grad,
        mod_offset_grad,
    )


def solution(mesh):
    in_specs = (
        P("batch", "seq", None),
        P("batch", None),
        P("batch"),
        P("batch"),
        P("batch", None),
        P("batch"),
        P("batch", None),
        P("batch"),
        P("batch", None),
        P("batch"),
        P("batch", None),
        P("batch"),
        P("batch", None),
        P("batch"),
        P("batch", "seq", None),
    )
    out_specs = (
        P("batch", "seq", None),
        P("batch", "seq", None),
        P("batch", None),
        P("batch", None),
        P("batch"),
        P("batch", None),
        P("batch"),
        P("batch", None),
        P("batch"),
        P("batch", None),
        P("batch"),
        P("batch", None),
        P("batch"),
    )
    return jax.shard_map(body, mesh=mesh, in_specs=in_specs, out_specs=out_specs, check_vma=False)
```
